256 devices in a mesh: tm: 4 (over x), seq: 64 (over z, y, core).
Axes of the slice: x: 4, y: 4, z: 8, core: 2. Of those that a mesh axis runs over, the one named last changes fastest.
Arguments:
- noise: float32 [2048, 64], P('seq'), may hold values from -6 to 6
- step_ids: int32 [5], replicated, may hold values from 18 to 28, as said below
- mod_table: float32 [28, 3, 3072], replicated, may hold values from -4 to 4
- embed_weight: bfloat16 [64, 3072], replicated, may hold values from -0.75 to 0.75
- qkv_weight: bfloat16 [3072, 4608], P(None, 'tm'), may hold values from -0.109375 to 0.109375
- q_gain: float32 [128], replicated, may hold values from 1.4 to 2.8
- k_gain: float32 [128], replicated, may hold values from 1.4 to 2.8
- out_weight: bfloat16 [1536, 3072], P('tm'), may hold values from -0.15625 to 0.15625
- final_weight: float32 [3072, 64], replicated, may hold values from -0.109375 to 0.109375
Outputs:
- latents: float32 [4, 2048, 64], P('tm', 'seq')
- drifts: float32 [4, 2048, 64], P('tm', 'seq')
The draws below stay inside these ranges and needn't reach their ends.
Inputs may be any that keep to these rules, and one draw needn't show every extreme that they name: `step_ids`: strictly increasing; the last entry is 28; the gaps between neighbours are a reordering of 1, 2, 3, 4 repeated.
All inputs are finite; a program needn't handle non-finite values.
Results may differ from the reference program's by a relative error of at most 0.017.
Values may be sent and summed in bfloat16 or wider, within the bound.
A program may use at most 128 MiB of HBM per device.

```python
import math
import jax
import jax.numpy as jnp
from jax import lax

C = 64
D = 3072
HEADS = 12
HD = 128
TOTAL = 28
SWEEPS = 2
TOKENS = 2048
WINDOW = 4


def draw_step_ids(key, part):
    key = jax.random.fold_in(key, 11)
    order = jax.random.permutation(key, WINDOW)
    gaps = 1 + order % 4
    ends = jnp.cumsum(gaps).astype(jnp.int32)
    begin = TOTAL - ends[-1]
    return (jnp.concatenate([jnp.zeros((1,), jnp.int32), ends]) + begin).astype(jnp.int32)


def shard_levels(stream_key, dims, cuts, low, high):
    def one(axis_at, parts):
        heights = jax.random.uniform(jax.random.fold_in(jax.random.fold_in(stream_key, 6), axis_at), (parts,), jnp.float32, low / len(cuts), high / len(cuts))
        return jnp.repeat(jnp.exp(heights), dims[axis_at] // parts).reshape((-1,) + (1,) * (len(dims) - axis_at - 1))

    factor_of = one(*cuts[0])
    for cut in cuts[1:]:
        factor_of = factor_of * one(*cut)
    return factor_of


def gaussian(rng, extent, spread, most, split=(), kind=jnp.bfloat16):
    level = shard_levels(rng, extent, split, -0.22, 0.18) if split else 1.0
    entries = jax.random.normal(rng, extent, jnp.float32) * spread * level
    return jnp.minimum(jnp.maximum(entries, -most), most).astype(kind)


def setup_inputs(seed: int = 0) -> dict:
    seeds = jax.random.split(jax.random.key(seed), 10)
    noise = gaussian(seeds[0], (TOKENS, C), 1.0, 6.0, ((0, 64),), jnp.float32)
    step_ids = draw_step_ids(jax.random.fold_in(seeds[9], 71), 0)
    mod_table = gaussian(seeds[2], (TOTAL, 3, D), 0.7, 4.0, (), jnp.float32)
    embed_weight = gaussian(seeds[3], (C, D), C ** -0.5, 0.75)
    qkv_weight = gaussian(seeds[4], (D, HEADS * 3 * HD), D ** -0.5, 0.109375, ((1, 4),))
    q_gain = jnp.clip(jnp.exp(jax.random.uniform(seeds[5], (HD,), jnp.float32, math.log(1.4), math.log(2.8))), 1.4, 2.8)
    k_gain = jnp.clip(jnp.exp(jax.random.uniform(seeds[6], (HD,), jnp.float32, math.log(1.4), math.log(2.8))), 1.4, 2.8)
    out_weight = gaussian(seeds[7], (HEADS * HD, D), (HEADS * HD) ** -0.5, 0.15625, ((0, 4),))
    final_weight = gaussian(seeds[8], (D, C), D ** -0.5, 0.109375, (), jnp.float32)
    return {"noise": noise, "step_ids": step_ids, "mod_table": mod_table, "embed_weight": embed_weight, "qkv_weight": qkv_weight, "q_gain": q_gain, "k_gain": k_gain, "out_weight": out_weight, "final_weight": final_weight}


time_shift = 3.0
norm_eps = 1e-06

def sigma_of(step_values):
    time_left = 1.0 - step_values.astype(jnp.float32) / TOTAL
    return time_shift * time_left / (1.0 + (time_shift - 1.0) * time_left)

def rms_norm(values, gain_vector):
    return values * lax.rsqrt(lax.optimization_barrier(jnp.mean(values * values, axis=-1, keepdims=True)) + norm_eps) * gain_vector

def layer_norm(values):
    average = lax.optimization_barrier(jnp.mean(values, axis=-1, keepdims=True))
    centred = values - average
    return centred * lax.rsqrt(lax.optimization_barrier(jnp.mean(centred * centred, axis=-1, keepdims=True)) + norm_eps)

def attend(triple):
    queries_head, keys_head, values_head = triple
    scores = jnp.dot(queries_head, keys_head.T, preferred_element_type=jnp.float32) * HD ** (-0.5)
    weights = jnp.exp(scores)
    denominator = lax.optimization_barrier(jnp.sum(weights, axis=1, keepdims=True))
    summed = jnp.dot(weights.astype(jnp.bfloat16), values_head, preferred_element_type=jnp.float32)
    return (summed / denominator).astype(jnp.bfloat16)

def by_head(values):
    return values.transpose(0, 2, 1, 3).reshape(WINDOW * HEADS, TOKENS, HD)

def drift(inputs, modulation, embed_weight, qkv_weight, q_gain, k_gain, out_weight, final_weight):
    flat_inputs = inputs.astype(jnp.bfloat16).reshape(WINDOW * TOKENS, C)
    embedded = jnp.dot(flat_inputs, embed_weight, preferred_element_type=jnp.float32).reshape(WINDOW, TOKENS, D)
    shift_rows = modulation[:, 0][:, None, :]
    scale_rows = modulation[:, 1][:, None, :]
    gate_rows = modulation[:, 2][:, None, :]
    modulated = (layer_norm(embedded) * (1.0 + scale_rows) + shift_rows).astype(jnp.bfloat16)
    projected = jnp.dot(modulated.reshape(WINDOW * TOKENS, D), qkv_weight, preferred_element_type=jnp.float32)
    projected = projected.reshape(WINDOW, TOKENS, HEADS, 3, HD)
    queries = rms_norm(projected[:, :, :, 0], q_gain).astype(jnp.bfloat16)
    keys = rms_norm(projected[:, :, :, 1], k_gain).astype(jnp.bfloat16)
    values = projected[:, :, :, 2].astype(jnp.bfloat16)
    mixed_heads = lax.map(attend, (by_head(queries), by_head(keys), by_head(values)))
    mixed_heads = mixed_heads.reshape(WINDOW, HEADS, TOKENS, HD).transpose(0, 2, 1, 3).reshape(WINDOW * TOKENS, HEADS * HD)
    attended = jnp.dot(mixed_heads, out_weight, preferred_element_type=jnp.float32).reshape(WINDOW, TOKENS, D)
    combined = embedded + gate_rows * attended
    result = jnp.dot(combined.reshape(WINDOW * TOKENS, D), final_weight, precision=lax.Precision.HIGHEST, preferred_element_type=jnp.float32)
    return result.reshape(WINDOW, TOKENS, C)

def reference(noise, step_ids, mod_table, embed_weight, qkv_weight, q_gain, k_gain, out_weight, final_weight):
    sigmas = sigma_of(step_ids)
    deltas = sigmas[1:] - sigmas[:-1]
    modulation = mod_table[step_ids[:WINDOW]]
    inputs = jnp.broadcast_to(noise[None], (WINDOW, TOKENS, C))
    for sweep_index in range(SWEEPS):
        drifts = drift(inputs, modulation, embed_weight, qkv_weight, q_gain, k_gain, out_weight, final_weight)
        step_terms = deltas[:, None, None] * drifts
        inclusive = jnp.cumsum(step_terms, axis=0)
        exclusive = jnp.concatenate([jnp.zeros_like(step_terms[:1]), inclusive[:-1]], axis=0)
        inputs = noise[None] + exclusive
    return (noise[None] + inclusive, drifts)
```

```python
import math

import jax
import jax.numpy as jnp
from jax import lax
from jax.experimental import pallas as pl
from jax.experimental.pallas import tpu as pltpu
from jax.sharding import PartitionSpec as P

MESH = pl.DeviceIdType.MESH
F32 = jnp.float32
BF16 = jnp.bfloat16
C = 64
D = 3072
HD = 128
HEADS = 3
WINDOW = 4
TOTAL = 28
EPS = 1e-6
PARTS = 6
DEPTH = D // PARTS
COLS = 3 * HD * HEADS
CONTRACT_LAST = (((1,), (1,)), ((), ()))


def dot(left, right):
    return jnp.dot(left, right, preferred_element_type=F32)


def dot_t(left, right):
    return lax.dot_general(left, right, CONTRACT_LAST, preferred_element_type=F32)


def split(value, pieces):
    out = []
    for _ in range(pieces):
        piece = value.astype(BF16)
        out.append(piece)
        value = value - piece.astype(F32)
    return out


def left_half(value):
    return jnp.concatenate([value, jnp.zeros_like(value)], axis=1)


def right_half(value):
    return jnp.concatenate([jnp.zeros_like(value), value], axis=1)


def kernel(
    noise_ref, ids_ref, mod_ref, e_ref, w_ref, qg_ref, kg_ref, o_ref, f_ref,
    lat_ref, dr_ref,
    noise_in, mod_in, e_in, w_in, o_in, f_in, local_sem, w_sem,
    nz, xb1, xb2, part1, part2, red, outs, acc, proj, wa, wb, bias, g12, g3, nw, efw, a_hi,
    lat_acc, dr_acc,
    a1_s, a1_r, a2_s, a2_r, r_s, r_r, b1_s, b1_r, b2_s, b2_r, o_s, o_r,
):
    c = lax.axis_index("tm")
    s = lax.axis_index("seq")
    z = s // 8
    y = (s // 2) % 4
    core = s % 2
    k = z // 2
    zlo = z % 2
    g = s % 8

    def seq_of(zz, gg):
        return zz * 8 + gg

    def device(cc, zz, gg):
        return (cc, seq_of(zz, gg))

    copies = [
        pltpu.make_async_copy(noise_ref, noise_in, local_sem.at[0]),
        pltpu.make_async_copy(e_ref, e_in, local_sem.at[1]),
        pltpu.make_async_copy(mod_ref, mod_in, local_sem.at[2]),
        pltpu.make_async_copy(f_ref, f_in, local_sem.at[3]),
        pltpu.make_async_copy(o_ref, o_in, local_sem.at[4]),
    ]
    w_copies = [
        pltpu.make_async_copy(
            w_ref.at[pl.ds(n * DEPTH, DEPTH)], w_in.at[pl.ds(n * DEPTH, DEPTH)], w_sem.at[n]
        )
        for n in range(PARTS)
    ]
    for copy in copies[:3]:
        copy.start()
    for copy in w_copies:
        copy.start()
    for copy in copies[3:]:
        copy.start()

    barrier = pltpu.get_barrier_semaphore()

    def greet(target):
        pl.semaphore_signal(barrier, inc=1, device_id=target, device_id_type=MESH)

    def greet_block(j, carry):
        greet(device((c + j % 4) % 4, 2 * ((k + j // 4) % 4) + zlo, g))
        return carry

    def greet_row(j, carry):
        greet(device((c + j) % 4, 2 * k + 1 - zlo, g))
        return carry

    def greet_column(j, carry):
        greet(device(c, 2 * ((k + j) % 4) + 1 - zlo, g))
        return carry

    def greet_plane(j, carry):
        greet(device(c, z, (g + j) % 8))
        return carry

    lax.fori_loop(1, 16, greet_block, 0)
    lax.fori_loop(0, 4, greet_row, 0)
    lax.fori_loop(1, 4, greet_column, 0)
    lax.fori_loop(1, 8, greet_plane, 0)

    copies[0].wait()
    nz[z] = jnp.concatenate([noise_in[0:16, :], noise_in[16:32, :]], axis=1)
    pl.semaphore_wait(barrier, 29)

    def a1(slot, j):
        return pltpu.make_async_remote_copy(
            src_ref=nz.at[slot], dst_ref=nz.at[slot], send_sem=a1_s.at[j], recv_sem=a1_r.at[slot],
            device_id=device(c, (z + j) % 8, g), device_id_type=MESH,
        )

    def a1_start(j, carry):
        a1(z, j).start()
        return carry

    lax.fori_loop(1, 8, a1_start, 0)

    def plane(buffer, slot, j, send, recv):
        return pltpu.make_async_remote_copy(
            src_ref=buffer.at[slot], dst_ref=buffer.at[slot], send_sem=send.at[j], recv_sem=recv.at[slot],
            device_id=device(c, z, (g + j) % 8), device_id_type=MESH,
        )

    copies[1].wait()
    embed = e_in[...].astype(F32)
    centred = embed - jnp.mean(embed, axis=1, keepdims=True)
    copies[2].wait()
    modulation = mod_in[ids_ref[k]]
    shift = modulation[0:1]
    scale = modulation[1:2]
    gate = modulation[2:3]
    scaled = split(centred * (1.0 + scale), 2)
    a_hi[0:64] = scaled[0]
    a_hi[64:128] = scaled[1]
    shifts = split(shift, 2)
    row = lax.broadcasted_iota(jnp.int32, (16, D), 0)
    zeros = jnp.zeros((16, D), BF16)
    a_hi[128:144] = jnp.where(
        row == 0, jnp.broadcast_to(shift, (16, D)),
        jnp.where(row == 1, jnp.broadcast_to(shift - shifts[0].astype(F32), (16, D)), 0.0),
    ).astype(BF16)

    def a1_wait(j, carry):
        a1((z + j) % 8, j).wait_recv()
        return carry

    lax.fori_loop(1, 8, a1_wait, 0)
    xb1[g] = nz[...].astype(BF16)

    def a2_start(j, carry):
        plane(xb1, g, j, a2_s, a2_r).start()
        return carry

    lax.fori_loop(1, 8, a2_start, 0)

    pieces = split(centred, 3)
    stacked = jnp.concatenate(pieces, axis=0)
    gram = sum(dot_t(stacked, piece) for piece in pieces)
    gram = (gram[0:64] + gram[64:128] + gram[128:192]) * (1.0 / D)
    g1, g2, gl = split(gram, 3)
    g12[0:64] = left_half(g1)
    g12[64:128] = right_half(g1)
    g12[128:192] = left_half(g2)
    g12[192:256] = right_half(g2)
    g3[0:64] = left_half(gl)
    g3[64:128] = right_half(gl)

    for n in range(PARTS):
        w_copies[n].wait()
        rows = slice(n * DEPTH, (n + 1) * DEPTH)
        for h in range(HEADS):
            cols = slice(h * 3 * HD, (h + 1) * 3 * HD)
            term = dot(a_hi[:, rows], w_in[rows, cols])
            if n == 0:
                proj[:, cols] = term
            else:
                proj[:, cols] += term
    small = proj[0:64] + proj[64:128]
    bias[...] = proj[128:136]
    small_hi, small_lo = split(small, 2)
    none = jnp.zeros((64, COLS), BF16)
    for n, value in enumerate((small_hi, none, small_lo, none)):
        wa[n * 64:(n + 1) * 64] = value
    for n, value in enumerate((none, small_hi, none, small_lo)):
        wb[n * 64:(n + 1) * 64] = value

    copies[3].wait()
    copies[4].wait()
    head_out = jnp.zeros((HEADS * HD, 2 * C), F32)
    embed_out = jnp.zeros((C, 2 * C), F32)
    for n in range(PARTS):
        rows = slice(n * DEPTH, (n + 1) * DEPTH)
        final = jnp.concatenate(split(f_in[rows], 2), axis=1)
        gated = (o_in[:, rows].astype(F32) * gate[:, rows]).astype(BF16)
        head_out += dot(gated, final)
        embed_out += dot(e_in[:, rows], final)
    head_out = head_out[:, 0:64] + head_out[:, 64:128]
    own = (c == 0).astype(F32)
    embed_out = (embed_out[:, 0:64] + embed_out[:, 64:128]) * own
    for n, value in enumerate(split(head_out, 2)):
        nw[n, 0:384] = left_half(value)
        nw[n, 384:768] = right_half(value)
    for n, value in enumerate(split(embed_out, 2)):
        efw[n * 128:n * 128 + 64] = left_half(value)
        efw[n * 128 + 64:n * 128 + 128] = right_half(value)

    gains = qg_ref[...] * kg_ref[...] * (HD ** -0.5 * math.log2(math.e))
    ones = jnp.full((HD, HD), 1.0 / HD, BF16)

    def doubled(x):
        return jnp.concatenate([x, x], axis=1)

    def inverse_deviation(x, xx):
        term = (dot(xx, g12[...]) + dot(x, g3[...])) * x.astype(F32)
        lane = lax.broadcasted_iota(jnp.int32, term.shape, 1)
        first = jnp.sum(jnp.where(lane < 64, term, 0.0), axis=1, keepdims=True)
        second = jnp.sum(jnp.where(lane < 64, 0.0, term), axis=1, keepdims=True)
        return lax.rsqrt(first + EPS), lax.rsqrt(second + EPS)

    def bias_of(start):
        return bias[0:1, start:start + HD] + bias[1:2, start:start + HD]

    def sweep(xb, recv, send, part):
        xq = jnp.concatenate([xb[g, 2 * i + zlo] for i in range(4)], axis=0)
        xxq = doubled(xq)
        ra, rb = inverse_deviation(xq, xxq)
        queries = []
        for h in range(HEADS):
            start = h * 3 * HD
            qa = dot(xxq, wa[:, start:start + HD]) * ra
            qb = dot(xxq, wb[:, start:start + HD]) * rb
            q = jnp.concatenate([qa, qb], axis=0) + bias_of(start)
            q = q * lax.rsqrt(jnp.mean(q * q, axis=1, keepdims=True) + EPS) * gains
            queries.append(q.astype(BF16))
        acc[...] = jnp.zeros_like(acc)

        def step(j, carry):
            gg = ((y + j // 2) % 4) * 2 + (core + j) % 2

            @pl.when(j > 0)
            def _():
                plane(xb, gg, j, send, recv).wait_recv()

            x = xb[gg].reshape(128, 128)
            xx = doubled(x)
            va, vb = inverse_deviation(x, xx)
            for h in range(HEADS):
                start = h * 3 * HD + HD
                kva = dot(xx, wa[:, start:start + 2 * HD]) * va
                kvb = dot(xx, wb[:, start:start + 2 * HD]) * vb
                kv = jnp.concatenate([kva, kvb], axis=0)
                keys = kv[:, 0:HD] + bias_of(start)
                values = (kv[:, HD:] + bias_of(start + HD)).astype(BF16)
                square = dot((keys * keys).astype(BF16), ones)
                keys = (keys * lax.rsqrt(square + EPS)).astype(BF16)
                weights = jnp.exp2(dot_t(queries[h], keys)).astype(BF16)
                values = jnp.concatenate([values, jnp.ones_like(values)], axis=1)
                acc[h] += dot(weights, values)
            return carry

        lax.fori_loop(0, 8, step, 0)
        attention = jnp.concatenate(
            [(acc[h, :, 0:HD] / acc[h, :, HD:]).astype(BF16) for h in range(HEADS)], axis=1
        )
        attention = jnp.concatenate([attention[0:64], attention[64:128]], axis=1)
        result = dot(attention, nw[0]) + dot(attention, nw[1]) + dot(xxq, efw[...])
        part[...] = result.reshape(4, 16, 128)

    def delta_of(t):
        def sigma(n):
            left = 1.0 - jnp.full((16, 128), n).astype(F32) / TOTAL
            return 3.0 * left / (1.0 + 2.0 * left)

        return sigma(ids_ref[t + 1]) - sigma(ids_ref[t])

    def r_copy(t, i):
        return pltpu.make_async_remote_copy(
            src_ref=part1.at[i], dst_ref=red.at[k * 4 + c], send_sem=r_s.at[t * 4 + i], recv_sem=r_r.at[k * 4 + c],
            device_id=device(i, 2 * t + zlo, g), device_id_type=MESH,
        )

    def o_copy(part, t, i):
        return pltpu.make_async_remote_copy(
            src_ref=part.at[i], dst_ref=outs.at[k * 4 + c], send_sem=o_s.at[t * 4 + i], recv_sem=o_r.at[k * 4 + c],
            device_id=device(t, 2 * i + zlo, g), device_id_type=MESH,
        )

    def each(first, act):
        def one(n, carry):
            act(n // 4, n % 4)
            return carry

        lax.fori_loop(first * 4, 16, one, 0)

    def send_out(part):
        def act(t, i):
            mine = jnp.logical_and(t == c, i == k)

            @pl.when(mine)
            def _():
                outs[k * 4 + c] = part[i]

            @pl.when(jnp.logical_not(mine))
            def _():
                o_copy(part, t, i).start()

        each(k, act)

    def wait_out(part):
        def act(t, i):
            @pl.when(jnp.logical_not(jnp.logical_and(t == c, i == k)))
            def _():
                o_copy(part, t, i).wait_send()

        each(k, act)

    def r_start(t, i):
        r_copy(t, i).start()

    def r_wait(t, i):
        r_copy(t, i).wait_send()

    @pl.when(k < 3)
    def _():
        sweep(xb1, a2_r, a2_s, part1)
        each(k + 1, r_start)

    @pl.when(k == 0)
    def _():
        send_out(part1)

    @pl.when(k == 3)
    def _():
        def wait(j, carry):
            plane(xb1, (g + j) % 8, j, a2_s, a2_r).wait_recv()
            return carry

        lax.fori_loop(1, 8, wait, 0)

    @pl.when(k > 0)
    def _():
        mine = 2 * c + zlo
        lat_acc[...] = nz[mine]
        for t in range(3):
            @pl.when(t < k)
            def _():
                for cc in range(4):
                    pltpu.make_async_remote_copy(
                        src_ref=red.at[t * 4 + cc], dst_ref=red.at[t * 4 + cc],
                        send_sem=r_s.at[0], recv_sem=r_r.at[t * 4 + cc],
                        device_id=device(cc, 2 * t + zlo, g), device_id_type=MESH,
                    ).wait_recv()
                total = (red[t * 4] + red[t * 4 + 1]) + (red[t * 4 + 2] + red[t * 4 + 3])
                lat_acc[...] += delta_of(t) * total
        xb2[g, mine] = lat_acc[...].astype(BF16)

        def b1(slot, j):
            other = (mine + j) % 8
            return pltpu.make_async_remote_copy(
                src_ref=xb2.at[g, slot], dst_ref=xb2.at[g, slot], send_sem=b1_s.at[j], recv_sem=b1_r.at[slot],
                device_id=device(other // 2, 2 * k + other % 2, g), device_id_type=MESH,
            )

        def b1_start(j, carry):
            b1(mine, j).start()
            return carry

        def b1_wait(j, carry):
            b1((mine + j) % 8, j).wait_recv()
            return carry

        def b1_sent(j, carry):
            b1(mine, j).wait_send()
            return carry

        def b2_start(j, carry):
            plane(xb2, g, j, b2_s, b2_r).start()
            return carry

        def b2_sent(j, carry):
            plane(xb2, g, j, b2_s, b2_r).wait_send()
            return carry

        lax.fori_loop(1, 8, b1_start, 0)
        lax.fori_loop(1, 8, b1_wait, 0)
        lax.fori_loop(1, 8, b2_start, 0)
        sweep(xb2, b2_r, b2_s, part2)
        send_out(part2)
        lax.fori_loop(1, 8, b1_sent, 0)
        lax.fori_loop(1, 8, b2_sent, 0)
        wait_out(part2)

    def a_sent(j, carry):
        a1(z, j).wait_send()
        plane(xb1, g, j, a2_s, a2_r).wait_send()
        return carry

    lax.fori_loop(1, 8, a_sent, 0)

    @pl.when(k < 3)
    def _():
        each(k + 1, r_wait)

    @pl.when(k == 0)
    def _():
        wait_out(part1)

    lat_acc[...] = nz[z]
    for t in range(4):
        @pl.when(t <= c)
        def _():
            for cc in range(4):
                @pl.when(jnp.logical_not(jnp.logical_and(t == k, cc == c)))
                def _():
                    pltpu.make_async_remote_copy(
                        src_ref=outs.at[t * 4 + cc], dst_ref=outs.at[t * 4 + cc],
                        send_sem=o_s.at[0], recv_sem=o_r.at[t * 4 + cc],
                        device_id=device(cc, 2 * t + zlo, g), device_id_type=MESH,
                    ).wait_recv()
            total = (outs[t * 4] + outs[t * 4 + 1]) + (outs[t * 4 + 2] + outs[t * 4 + 3])
            lat_acc[...] += delta_of(t) * total
            dr_acc[...] = total
    lat_ref[0, 0:16, :] = lat_acc[:, 0:64]
    lat_ref[0, 16:32, :] = lat_acc[:, 64:128]
    dr_ref[0, 0:16, :] = dr_acc[:, 0:64]
    dr_ref[0, 16:32, :] = dr_acc[:, 64:128]


def body(
    noise, step_ids, mod_table, embed_weight, qkv_weight, q_gain, k_gain, out_weight, final_weight
):
    anywhere = pl.BlockSpec(memory_space=pl.ANY)
    vmem = pl.BlockSpec(memory_space=pltpu.VMEM)
    out = jax.ShapeDtypeStruct((1, 32, C), F32)
    dma = pltpu.SemaphoreType.DMA
    return pl.pallas_call(
        kernel,
        out_shape=(out, out),
        in_specs=[
            anywhere, pl.BlockSpec(memory_space=pltpu.SMEM), anywhere, anywhere, anywhere,
            vmem, vmem, anywhere, anywhere,
        ],
        out_specs=(vmem, vmem),
        scratch_shapes=[
            pltpu.VMEM((32, C), F32),
            pltpu.VMEM((TOTAL, 3, D), F32),
            pltpu.VMEM((C, D), BF16),
            pltpu.VMEM((D, COLS), BF16),
            pltpu.VMEM((HEADS * HD, D), BF16),
            pltpu.VMEM((D, C), F32),
            dma((5,)),
            dma((PARTS,)),
            pltpu.VMEM((8, 16, 128), F32),
            pltpu.VMEM((8, 8, 16, 128), BF16),
            pltpu.VMEM((8, 8, 16, 128), BF16),
            pltpu.VMEM((4, 16, 128), F32),
            pltpu.VMEM((4, 16, 128), F32),
            pltpu.VMEM((12, 16, 128), F32),
            pltpu.VMEM((16, 16, 128), F32),
            pltpu.VMEM((HEADS, 128, 2 * HD), F32),
            pltpu.VMEM((144, COLS), F32),
            pltpu.VMEM((256, COLS), BF16),
            pltpu.VMEM((256, COLS), BF16),
            pltpu.VMEM((8, COLS), F32),
            pltpu.VMEM((256, 128), BF16),
            pltpu.VMEM((128, 128), BF16),
            pltpu.VMEM((2, 768, 128), BF16),
            pltpu.VMEM((256, 128), BF16),
            pltpu.VMEM((144, D), BF16),
            pltpu.VMEM((16, 128), F32),
            pltpu.VMEM((16, 128), F32),
            dma((8,)), dma((8,)), dma((8,)), dma((8,)), dma((16,)), dma((12,)),
            dma((8,)), dma((8,)), dma((8,)), dma((8,)), dma((16,)), dma((16,)),
        ],
        compiler_params=pltpu.CompilerParams(
            collective_id=0, has_side_effects=True, vmem_limit_bytes=50 * 1024 * 1024
        ),
        cost_estimate=pl.CostEstimate(flops=4_000_000_000, bytes_accessed=14_000_000, transcendentals=1_700_000),
    )(
        noise, step_ids, mod_table, embed_weight, qkv_weight,
        q_gain.reshape(1, HD), k_gain.reshape(1, HD), out_weight, final_weight,
    )


def solution(mesh):
    in_specs = (P("seq", None), P(), P(), P(), P(None, "tm"), P(), P(), P("tm", None), P())
    out_specs = (P("tm", "seq", None), P("tm", "seq", None))
    return jax.shard_map(body, mesh=mesh, in_specs=in_specs, out_specs=out_specs, check_vma=False)
```

```python
import math

import jax
import jax.numpy as jnp
from jax import lax
from jax.experimental import pallas as pl
from jax.experimental.pallas import tpu as pltpu
from jax.sharding import PartitionSpec as P

MESH = pl.DeviceIdType.MESH
F32 = jnp.float32
BF16 = jnp.bfloat16
C = 64
D = 3072
HD = 128
HEADS = 3
WINDOW = 4
TOTAL = 28
EPS = 1e-6
PARTS = 6
DEPTH = D // PARTS
COLS = 3 * HD * HEADS
FAR_FIRST = sorted(
    [(a, b) for a in range(8) for b in range(4) if a or b],
    key=lambda ab: -(min(ab[0], 8 - ab[0]) + min(ab[1], 4 - ab[1])),
)
CONTRACT_LAST = (((1,), (1,)), ((), ()))


def dot(left, right):
    return jnp.dot(left, right, preferred_element_type=F32)


def dot_t(left, right):
    return lax.dot_general(left, right, CONTRACT_LAST, preferred_element_type=F32)


def split(value, pieces):
    out = []
    for _ in range(pieces):
        piece = value.astype(BF16)
        out.append(piece)
        value = value - piece.astype(F32)
    return out


def left_half(value):
    return jnp.concatenate([value, jnp.zeros_like(value)], axis=1)


def right_half(value):
    return jnp.concatenate([jnp.zeros_like(value), value], axis=1)


def kernel(
    noise_ref, ids_in, mod_ref, e_ref, w_ref, qgain_ref, kgain_ref, o_ref, f_ref,
    out_ref,
    noise_in, ids_ref, mod_in, e_in, w_in, qg_ref, kg_ref, o_in, f_in, local_sem, w_sem,
    own_noise, red_noise, xb1, xb2, keys_ref, values_ref, part1, part2, red, outs,
    proj, wa, wb, bias, g12, g3, nw, efw, a_hi, lat_acc, dr_acc,
    a_s, a_r, n_s, n_r, h_s, h_r, r_s, r_r, b_s, b_r, o_s, o_r,
):
    c = lax.axis_index("tm")
    s = lax.axis_index("seq")
    z = s // 8
    y = (s // 2) % 4
    core = s % 2

    def device(cc, zz, yy):
        return (cc % 4, (zz % 8) * 8 + (yy % 4) * 2 + core)

    slot = y * 8 + z
    mine = c * 8 + z
    sibling = (c, z * 8 + y * 2 + 1 - core)

    noise_copy = pltpu.make_async_copy(noise_ref, noise_in, local_sem.at[0])
    noise_copy.start()

    barrier = pltpu.get_barrier_semaphore()

    def greet(target):
        pl.semaphore_signal(barrier, inc=1, device_id=target, device_id_type=MESH)

    for dz, dy in FAR_FIRST:
        greet(device(c, z + dz, y + dy))
    for dz, dx in FAR_FIRST:
        if dx:
            greet(device(c + dx, z + dz, y))
    for dx in range(1, 4):
        for dy in range(1, 4):
            greet(device(c + dx, z, y + dy))
    greet(sibling)

    copies = [
        pltpu.make_async_copy(e_ref, e_in, local_sem.at[1]),
        pltpu.make_async_copy(ids_in, ids_ref, local_sem.at[2]),
        pltpu.make_async_copy(mod_ref, mod_in, local_sem.at[3]),
        pltpu.make_async_copy(f_ref, f_in, local_sem.at[4]),
        pltpu.make_async_copy(o_ref, o_in, local_sem.at[5]),
        pltpu.make_async_copy(qgain_ref, qg_ref, local_sem.at[6]),
        pltpu.make_async_copy(kgain_ref, kg_ref, local_sem.at[7]),
    ]
    w_copies = [
        pltpu.make_async_copy(
            w_ref.at[pl.ds(n * DEPTH, DEPTH)], w_in.at[pl.ds(n * DEPTH, DEPTH)], w_sem.at[n]
        )
        for n in range(PARTS)
    ]

    for copy in copies[:3] + w_copies + copies[3:]:
        copy.start()

    def small_matrices():
        copies[0].wait()
        embed = e_in[...].astype(F32)
        centred = embed - jnp.mean(embed, axis=1, keepdims=True)
        copies[1].wait()
        copies[2].wait()
        here = pl.ds(ids_ref[y], 1)
        shift = mod_in[0, here]
        scale = mod_in[1, here]
        gate = mod_in[2, here]
        scaled = split(centred * (1.0 + scale), 2)
        a_hi[0:64] = scaled[0]
        a_hi[64:128] = scaled[1]
        shifts = split(shift, 2)
        row = lax.broadcasted_iota(jnp.int32, (16, D), 0)
        a_hi[128:144] = jnp.where(
            row == 0, jnp.broadcast_to(shift, (16, D)),
            jnp.where(row == 1, jnp.broadcast_to(shift - shifts[0].astype(F32), (16, D)), 0.0),
        ).astype(BF16)

        pieces = split(centred, 3)
        stacked = jnp.concatenate(pieces, axis=0)
        gram = dot_t(stacked, stacked)
        gram = gram[0:64] + gram[64:128] + gram[128:192]
        gram = (gram[:, 0:64] + gram[:, 64:128] + gram[:, 128:192]) * (1.0 / D)
        g1, g2, gl = split(gram, 3)
        g12[0:64] = left_half(g1)
        g12[64:128] = right_half(g1)
        g12[128:192] = left_half(g2)
        g12[192:256] = right_half(g2)
        g3[0:64] = left_half(gl)
        g3[64:128] = right_half(gl)

        for copy in w_copies:
            copy.wait()
        proj[...] = dot(a_hi[...], w_in[...])
        small = proj[0:64] + proj[64:128]
        bias[...] = proj[128:136]
        small_hi, small_lo = split(small, 2)
        none = jnp.zeros((64, COLS), BF16)
        for n, value in enumerate((small_hi, none, small_lo, none)):
            wa[n * 64:(n + 1) * 64] = value
        for n, value in enumerate((none, small_hi, none, small_lo)):
            wb[n * 64:(n + 1) * 64] = value

        values_ref[:, :, HD:] = jnp.ones((HEADS, 2048, HD), BF16)
        for copy in copies[3:]:
            copy.wait()
        final = f_in[...]
        final_hl = jnp.concatenate(split(final, 2), axis=0)
        gated_hl = jnp.concatenate(split(final * gate, 2), axis=0)
        head_out = dot_t(o_in[...], gated_hl)
        embed_out = dot_t(e_in[...], final_hl)
        head_out = head_out[:, 0:64] + head_out[:, 64:128]
        own = (c == 0).astype(F32)
        embed_out = (embed_out[:, 0:64] + embed_out[:, 64:128]) * own
        for n, value in enumerate(split(head_out, 2)):
            nw[n, 0:384] = left_half(value)
            nw[n, 384:768] = right_half(value)
        for n, value in enumerate(split(embed_out, 2)):
            efw[n * 128:n * 128 + 64] = left_half(value)
            efw[n * 128 + 64:n * 128 + 128] = right_half(value)

    @pl.when(z < 4)
    def _():
        small_matrices()

    noise_copy.wait()
    packed = jnp.concatenate([noise_in[0:16], noise_in[16:32]], axis=1)
    own_noise[...] = packed
    xb1[core, slot] = packed.astype(BF16)
    pl.semaphore_wait(barrier, 65)

    def block_copy(buffer, where, target, send, recv):
        return pltpu.make_async_remote_copy(
            src_ref=buffer.at[core, where], dst_ref=buffer.at[core, where], send_sem=send, recv_sem=recv,
            device_id=target, device_id_type=MESH,
        )

    def blocks(buffer, count, send, recv):
        part = buffer.at[core, pl.ds(0, count)]
        return pltpu.make_async_remote_copy(
            src_ref=part, dst_ref=part, send_sem=send, recv_sem=recv, device_id=sibling, device_id_type=MESH,
        )

    def a_send(dz, yy):
        block_copy(xb1, slot, device(c, z + dz, yy), a_s.at[0], a_r.at[0]).start()

    for dz in (4, 3, 5, 2, 6, 1, 7):
        for yy in range(3):
            a_send(dz, yy)
    for yy in range(3):
        @pl.when(y != yy)
        def _():
            a_send(0, yy)

    def n_copy(t):
        return pltpu.make_async_remote_copy(
            src_ref=own_noise, dst_ref=red_noise, send_sem=n_s.at[t], recv_sem=n_r.at[0],
            device_id=device(c, z, t), device_id_type=MESH,
        )

    @pl.when(y == c)
    def _():
        red_noise[...] = own_noise[...]
        for t in range(1, WINDOW):
            @pl.when(y != t)
            def _():
                n_copy(t).start()

    @pl.when(z >= 4)
    def _():
        small_matrices()

    ones = jnp.full((HD, HD), 1.0 / HD, BF16)

    def doubled(x):
        return jnp.concatenate([x, x], axis=1)

    def inverse_deviation(x, xx):
        term = (dot(xx, g12[...]) + dot(x, g3[...])) * x.astype(F32)
        lane = lax.broadcasted_iota(jnp.int32, term.shape, 1)
        first = jnp.sum(jnp.where(lane < 64, term, 0.0), axis=1, keepdims=True)
        second = jnp.sum(jnp.where(lane < 64, 0.0, term), axis=1, keepdims=True)
        return lax.rsqrt(first + EPS), lax.rsqrt(second + EPS)

    def bias_of(start):
        return bias[0:1, start:start + HD] + bias[1:2, start:start + HD]

    def project(x, first):
        xx = doubled(x)
        va, vb = inverse_deviation(x, xx)
        rows = slice(first * 1024, (first + 1) * 1024)
        for h in range(HEADS):
            start = h * 3 * HD + HD
            kva = dot(xx, wa[:, start:start + 2 * HD]) * va
            kvb = dot(xx, wb[:, start:start + 2 * HD]) * vb
            kv = jnp.concatenate([kva, kvb], axis=0)
            keys = kv[:, 0:HD] + bias_of(start)
            square = dot((keys * keys).astype(BF16), ones)
            keys_ref[h, rows] = (keys * lax.rsqrt(square + EPS)).astype(BF16)
            values_ref[h, rows, 0:HD] = (kv[:, HD:] + bias_of(start + HD)).astype(BF16)

    def half_copy(buffer, which, send, recv):
        return pltpu.make_async_remote_copy(
            src_ref=buffer.at[which], dst_ref=buffer.at[which], send_sem=send, recv_sem=recv,
            device_id=sibling, device_id_type=MESH,
        )

    def sweep(xb, sweep_index, send, recv, part):
        blocks(xb, 31, send, recv).wait_recv()
        half_copy(xb, core, h_s.at[sweep_index], h_r.at[sweep_index]).start()
        gains = qg_ref[...] * kg_ref[...] * (HD ** -0.5 * math.log2(math.e))
        xq = jnp.concatenate([xb[core, i * 8 + z] for i in range(4)], axis=0)
        xxq = doubled(xq)
        ra, rb = inverse_deviation(xq, xxq)
        queries = []
        for h in range(HEADS):
            start = h * 3 * HD
            qa = dot(xxq, wa[:, start:start + HD]) * ra
            qb = dot(xxq, wb[:, start:start + HD]) * rb
            q = jnp.concatenate([qa, qb], axis=0) + bias_of(start)
            q = q * lax.rsqrt(jnp.mean(q * q, axis=1, keepdims=True) + EPS) * gains
            queries.append(q.astype(BF16))
        project(xb[core].reshape(512, 128), 0)
        half_copy(xb, 1 - core, h_s.at[sweep_index], h_r.at[sweep_index]).wait_recv()
        project(xb[1 - core].reshape(512, 128), 1)
        heads = []
        for h in range(HEADS):
            weights = jnp.exp2(dot_t(queries[h], keys_ref[h])).astype(BF16)
            summed = dot(weights, values_ref[h])
            heads.append((summed[:, 0:HD] / summed[:, HD:]).astype(BF16))
        attention = jnp.concatenate(heads, axis=1)
        attention = jnp.concatenate([attention[0:64], attention[64:128]], axis=1)
        result = dot(attention, nw[0]) + dot(attention, nw[1]) + dot(xxq, efw[...])
        part[...] = result.reshape(4, 16, 128)

    def delta_of(t):
        def sigma(n):
            left = 1.0 - jnp.full((16, 128), n).astype(F32) / TOTAL
            return 3.0 * left / (1.0 + 2.0 * left)

        return sigma(ids_ref[t + 1]) - sigma(ids_ref[t])

    def r_copy(t, i):
        return pltpu.make_async_remote_copy(
            src_ref=part1.at[i], dst_ref=red.at[y * 4 + c], send_sem=r_s.at[t * 4 + i], recv_sem=r_r.at[y * 4 + c],
            device_id=device(i, z, t), device_id_type=MESH,
        )

    def o_copy(part, t, i):
        return pltpu.make_async_remote_copy(
            src_ref=part.at[i], dst_ref=outs.at[y * 4 + c], send_sem=o_s.at[t * 4 + i], recv_sem=o_r.at[y * 4 + c],
            device_id=device(t, z, i), device_id_type=MESH,
        )

    def each(first, act):
        count = 4 - first

        def one(n, carry):
            act(first + n % count, n // count)
            return carry

        lax.fori_loop(0, 4 * count, one, 0)

    def send_out(part):
        def act(t, i):
            mine = jnp.logical_and(t == c, i == y)

            @pl.when(mine)
            def _():
                outs[y * 4 + c] = part[i]

            @pl.when(jnp.logical_not(mine))
            def _():
                o_copy(part, t, i).start()

        each(y, act)

    def wait_out(part):
        def act(t, i):
            @pl.when(jnp.logical_not(jnp.logical_and(t == c, i == y)))
            def _():
                o_copy(part, t, i).wait_send()

        each(y, act)

    def r_start(t, i):
        r_copy(t, i).start()

    def r_wait(t, i):
        r_copy(t, i).wait_send()

    @pl.when(y < 3)
    def _():
        sweep(xb1, 0, a_s.at[0], a_r.at[0], part1)
        each(y + 1, r_start)

    @pl.when(y == 0)
    def _():
        send_out(part1)

    @pl.when(y > 0)
    def _():
        @pl.when(y != c)
        def _():
            n_copy(y).wait_recv()

        lat_acc[...] = red_noise[...]
        for t in range(3):
            @pl.when(t < y)
            def _():
                for cc in range(4):
                    pltpu.make_async_remote_copy(
                        src_ref=red.at[t * 4 + cc], dst_ref=red.at[t * 4 + cc],
                        send_sem=r_s.at[0], recv_sem=r_r.at[t * 4 + cc],
                        device_id=device(cc, z, t), device_id_type=MESH,
                    ).wait_recv()
                total = (red[t * 4] + red[t * 4 + 1]) + (red[t * 4 + 2] + red[t * 4 + 3])
                lat_acc[...] += delta_of(t) * total
        xb2[core, mine] = lat_acc[...].astype(BF16)
        for dz, dx in FAR_FIRST:
            block_copy(xb2, mine, device(c + dx, z + dz, y), b_s.at[0], b_r.at[0]).start()
        sweep(xb2, 1, b_s.at[0], b_r.at[0], part2)
        send_out(part2)

    lat_acc[...] = own_noise[...]
    for t in range(4):
        @pl.when(t <= c)
        def _():
            for cc in range(4):
                @pl.when(jnp.logical_not(jnp.logical_and(t == y, cc == c)))
                def _():
                    pltpu.make_async_remote_copy(
                        src_ref=outs.at[t * 4 + cc], dst_ref=outs.at[t * 4 + cc],
                        send_sem=o_s.at[0], recv_sem=o_r.at[t * 4 + cc],
                        device_id=device(cc, z, t), device_id_type=MESH,
                    ).wait_recv()
            total = (outs[t * 4] + outs[t * 4 + 1]) + (outs[t * 4 + 2] + outs[t * 4 + 3])
            lat_acc[...] += delta_of(t) * total
            dr_acc[...] = total
    out_ref[0:16, 0:C] = lat_acc[:, 0:C]
    out_ref[16:32, 0:C] = lat_acc[:, C:]
    out_ref[0:16, C:] = dr_acc[:, 0:C]
    out_ref[16:32, C:] = dr_acc[:, C:]
    @pl.when(y < 3)
    def _():
        blocks(xb1, 23, a_s.at[0], a_r.at[0]).wait_send()
        half_copy(xb1, core, h_s.at[0], h_r.at[0]).wait_send()
        each(y + 1, r_wait)

    @pl.when(y == 3)
    def _():
        blocks(xb1, 24, a_s.at[0], a_r.at[0]).wait_send()

    @pl.when(y == 0)
    def _():
        wait_out(part1)

    @pl.when(y > 0)
    def _():
        blocks(xb2, 31, b_s.at[0], b_r.at[0]).wait_send()
        half_copy(xb2, core, h_s.at[1], h_r.at[1]).wait_send()
        wait_out(part2)

    @pl.when(y == c)
    def _():
        for t in range(1, WINDOW):
            @pl.when(y != t)
            def _():
                n_copy(t).wait_send()


def body(
    noise, step_ids, mod_table, embed_weight, qkv_weight, q_gain, k_gain, out_weight, final_weight
):
    hbm = pl.BlockSpec(memory_space=pltpu.HBM)
    vmem = pl.BlockSpec(memory_space=pltpu.VMEM)
    out = pltpu.VMEM((32, 2 * C), F32)
    dma = pltpu.SemaphoreType.DMA
    both = pl.pallas_call(
        kernel,
        out_shape=out,
        in_specs=[hbm] * 9,
        out_specs=vmem,
        scratch_shapes=[
            pltpu.VMEM((32, C), F32),
            pltpu.SMEM((WINDOW + 1,), jnp.int32),
            pltpu.VMEM((3, TOTAL, D), F32),
            pltpu.VMEM((C, D), BF16),
            pltpu.VMEM((D, COLS), BF16),
            pltpu.VMEM((1, HD), F32),
            pltpu.VMEM((1, HD), F32),
            pltpu.VMEM((HEADS * HD, D), BF16),
            pltpu.VMEM((C, D), F32),
            dma((8,)),
            dma((PARTS,)),
            pltpu.VMEM((16, 128), F32),
            pltpu.VMEM((16, 128), F32),
            pltpu.VMEM((2, 32, 16, 128), BF16),
            pltpu.VMEM((2, 32, 16, 128), BF16),
            pltpu.VMEM((HEADS, 2048, HD), BF16),
            pltpu.VMEM((HEADS, 2048, 2 * HD), BF16),
            pltpu.VMEM((4, 16, 128), F32),
            pltpu.VMEM((4, 16, 128), F32),
            pltpu.VMEM((12, 16, 128), F32),
            pltpu.VMEM((16, 16, 128), F32),
            pltpu.VMEM((144, COLS), F32),
            pltpu.VMEM((256, COLS), BF16),
            pltpu.VMEM((256, COLS), BF16),
            pltpu.VMEM((8, COLS), F32),
            pltpu.VMEM((256, 128), BF16),
            pltpu.VMEM((128, 128), BF16),
            pltpu.VMEM((2, 768, 128), BF16),
            pltpu.VMEM((256, 128), BF16),
            pltpu.VMEM((144, D), BF16),
            pltpu.VMEM((16, 128), F32),
            pltpu.VMEM((16, 128), F32),
            dma((1,)), dma((1,)), dma((4,)), dma((1,)), dma((2,)), dma((2,)),
            dma((16,)), dma((12,)), dma((1,)), dma((1,)), dma((16,)), dma((16,)),
        ],
        compiler_params=pltpu.CompilerParams(
            collective_id=0, has_side_effects=True, vmem_limit_bytes=60 * 1024 * 1024
        ),
        cost_estimate=pl.CostEstimate(flops=4_000_000_000, bytes_accessed=14_000_000, transcendentals=1_700_000),
    )(
        noise, step_ids, mod_table.transpose(1, 0, 2), embed_weight, qkv_weight,
        q_gain.reshape(1, HD), k_gain.reshape(1, HD), out_weight, final_weight.T,
    )
    return both[None, :, 0:C], both[None, :, C:]


def solution(mesh):
    in_specs = (P("seq", None), P(), P(), P(), P(None, "tm"), P(), P(), P("tm", None), P())
    out_specs = (P("tm", "seq", None), P("tm", "seq", None))
    return jax.shard_map(body, mesh=mesh, in_specs=in_specs, out_specs=out_specs, check_vma=False)
```

```python
import math

import jax
import jax.numpy as jnp
from jax import lax
from jax.experimental import pallas as pl
from jax.experimental.pallas import tpu as pltpu
from jax.sharding import PartitionSpec as P

MESH = pl.DeviceIdType.MESH
F32 = jnp.float32
BF16 = jnp.bfloat16
C = 64
D = 3072
HD = 128
HEADS = 3
WINDOW = 4
TOTAL = 28
EPS = 1e-6
PARTS = 6
DEPTH = D // PARTS
COLS = 3 * HD * HEADS
FAR_FIRST = sorted(
    [(a, b) for a in range(8) for b in range(4) if a or b],
    key=lambda ab: -(min(ab[0], 8 - ab[0]) + min(ab[1], 4 - ab[1])),
)
CONTRACT_LAST = (((1,), (1,)), ((), ()))


def dot(left, right):
    return jnp.dot(left, right, preferred_element_type=F32)


def dot_t(left, right):
    return lax.dot_general(left, right, CONTRACT_LAST, preferred_element_type=F32)


def split(value, pieces):
    out = []
    for _ in range(pieces):
        piece = value.astype(BF16)
        out.append(piece)
        value = value - piece.astype(F32)
    return out


def left_half(value):
    return jnp.concatenate([value, jnp.zeros_like(value)], axis=1)


def right_half(value):
    return jnp.concatenate([jnp.zeros_like(value), value], axis=1)


def kernel(
    noise_ref, ids_in, mod_ref, e_ref, w_ref, qgain_ref, kgain_ref, o_ref, f_ref,
    out_ref,
    noise_in, ids_ref, mod_in, e_in, w_in, qg_ref, kg_ref, o_in, f_in, local_sem, w_sem,
    own_noise, red_noise, xb1, xb2, keys_ref, values_ref, queries_ref, part1, part2, box, final_box, zero_sum, zero_box,
    lat_rows,
    proj, wa, wb, bias, g12, g3, nw, efw, a_hi, lat_acc, dr_acc, next_inputs, deltas,
    a_s, a_r, n_s, n_r, h_s, h_r, r_r, b_s, b_r, out_s, out2_s, zero_s, o_r,
):
    c = lax.axis_index("tm")
    s = lax.axis_index("seq")
    z = s // 8
    y = (s // 2) % 4
    core = s % 2

    def device(cc, zz, yy):
        return (cc % 4, (zz % 8) * 8 + (yy % 4) * 2 + core)

    sibling = (c, z * 8 + y * 2 + 1 - core)

    noise_copy = pltpu.make_async_copy(noise_ref, noise_in, local_sem.at[0])
    noise_copy.start()

    barrier = pltpu.get_barrier_semaphore()
    early = z < 4
    worker = jnp.logical_and(early, y < 3)
    half = z // 4
    near_z = jnp.where(early, z, (z + 2) % 4)
    partner = 4 + (z + 2) % 4

    def greet(target):
        pl.semaphore_signal(barrier, inc=1, device_id=target, device_id_type=MESH)

    @pl.when(early)
    def _():
        for dz, dy in FAR_FIRST:
            greet(device(c, z + dz, y + dy))
        for dx in range(1, 4):
            for dy in range(4):
                greet(device(c + dx, z, y + dy))
        greet(sibling)

    copies = [
        pltpu.make_async_copy(e_ref, e_in, local_sem.at[1]),
        pltpu.make_async_copy(ids_in, ids_ref, local_sem.at[2]),
        pltpu.make_async_copy(mod_ref, mod_in, local_sem.at[3]),
        pltpu.make_async_copy(f_ref, f_in, local_sem.at[4]),
        pltpu.make_async_copy(o_ref, o_in, local_sem.at[5]),
        pltpu.make_async_copy(qgain_ref, qg_ref, local_sem.at[6]),
        pltpu.make_async_copy(kgain_ref, kg_ref, local_sem.at[7]),
    ]
    w_copies = [
        pltpu.make_async_copy(
            w_ref.at[pl.ds(n * DEPTH, DEPTH)], w_in.at[pl.ds(n * DEPTH, DEPTH)], w_sem.at[0]
        )
        for n in range(PARTS)
    ]

    def fetch():
        for copy in copies[:3] + w_copies + copies[3:]:
            copy.start()

    def small_matrices():
        copies[0].wait()
        embed = e_in[...].astype(F32)
        centred = embed - jnp.mean(embed, axis=1, keepdims=True)
        copies[1].wait()
        copies[2].wait()
        here = pl.ds(ids_ref[y], 1)
        shift = mod_in[0, here]
        scale = mod_in[1, here]
        gate = mod_in[2, here]
        scaled = split(centred * (1.0 + scale), 2)
        a_hi[0:64] = scaled[0]
        a_hi[64:128] = scaled[1]
        shifts = split(shift, 2)
        row = lax.broadcasted_iota(jnp.int32, (16, D), 0)
        a_hi[128:144] = jnp.where(
            row == 0, jnp.broadcast_to(shift, (16, D)),
            jnp.where(row == 1, jnp.broadcast_to(shift - shifts[0].astype(F32), (16, D)), 0.0),
        ).astype(BF16)

        pieces = split(centred, 3)
        stacked = jnp.concatenate(pieces, axis=0)
        gram = dot_t(stacked, stacked)
        gram = gram[0:64] + gram[64:128] + gram[128:192]
        gram = (gram[:, 0:64] + gram[:, 64:128] + gram[:, 128:192]) * (1.0 / D)
        g1, g2, gl = split(gram, 3)
        g12[0:64] = left_half(g1)
        g12[64:128] = right_half(g1)
        g12[128:192] = left_half(g2)
        g12[192:256] = right_half(g2)
        g3[0:64] = left_half(gl)
        g3[64:128] = right_half(gl)

        pltpu.make_async_copy(w_ref, w_in, w_sem.at[0]).wait()
        proj[...] = dot(a_hi[...], w_in[...])
        small = proj[0:64] + proj[64:128]
        bias[...] = proj[128:136]
        small_hi, small_lo = split(small, 2)
        none = jnp.zeros((64, COLS), BF16)
        for n, value in enumerate((small_hi, none, small_lo, none)):
            wa[n * 64:(n + 1) * 64] = value
        for n, value in enumerate((none, small_hi, none, small_lo)):
            wb[n * 64:(n + 1) * 64] = value

        values_ref[:, :, HD:] = jnp.ones((HEADS, 2048, HD), BF16)
        for copy in copies[3:]:
            copy.wait()
        final = f_in[...]
        final_hl = jnp.concatenate(split(final, 2), axis=0)
        gated_hl = jnp.concatenate(split(final * gate, 2), axis=0)
        head_out = dot_t(o_in[...], gated_hl)
        embed_out = dot_t(e_in[...], final_hl)
        head_out = head_out[:, 0:64] + head_out[:, 64:128]
        own = (c == 0).astype(F32)
        embed_out = (embed_out[:, 0:64] + embed_out[:, 64:128]) * own
        for n, value in enumerate(split(head_out, 2)):
            nw[n, 0:384] = left_half(value)
            nw[n, 384:768] = right_half(value)
        for n, value in enumerate(split(embed_out, 2)):
            efw[n * 128:n * 128 + 64] = left_half(value)
            efw[n * 128 + 64:n * 128 + 128] = right_half(value)

    @pl.when(early)
    def _():
        fetch()

    noise_copy.wait()
    packed = jnp.concatenate([noise_in[0:16], noise_in[16:32]], axis=1)
    own_noise[...] = packed
    slot = half * 16 + near_z * 4 + y
    xb1[core, slot] = packed.astype(BF16)

    @pl.when(early)
    def _():
        pl.semaphore_wait(barrier, 28)

    @pl.when(jnp.logical_not(early))
    def _():
        pl.semaphore_wait(barrier, 16)


    def a_copy(zz, yy):
        return pltpu.make_async_remote_copy(
            src_ref=xb1.at[core, slot], dst_ref=xb1.at[core, slot], send_sem=a_s.at[0], recv_sem=a_r.at[half],
            device_id=device(c, zz, yy), device_id_type=MESH,
        )

    def blocks(buffer, count, send, recv):
        part = buffer.at[core, pl.ds(0, count)]
        return pltpu.make_async_remote_copy(
            src_ref=part, dst_ref=part, send_sem=send, recv_sem=recv, device_id=sibling, device_id_type=MESH,
        )

    @pl.when(early)
    def _():
        for zz in range(4):
            for yy in range(3):
                @pl.when(jnp.logical_not(jnp.logical_and(z == zz, y == yy)))
                def _():
                    a_copy(zz, yy).start()

    @pl.when(jnp.logical_not(early))
    def _():
        for dz in (4, 3, 5, 2, 6, 1, 7):
            @pl.when((z + dz) % 8 < 4)
            def _():
                for yy in range(3):
                    a_copy(z + dz, yy).start()

    def n_copy(t):
        return pltpu.make_async_remote_copy(
            src_ref=own_noise, dst_ref=red_noise.at[half], send_sem=n_s.at[t], recv_sem=n_r.at[half],
            device_id=device(c, near_z, t), device_id_type=MESH,
        )

    @pl.when(y == c)
    def _():
        @pl.when(jnp.logical_and(early, y > 0))
        def _():
            red_noise[0] = own_noise[...]

        for t in range(1, WINDOW):
            @pl.when(jnp.logical_or(y != t, z >= 4))
            def _():
                n_copy(t).start()

    @pl.when(early)
    def _():
        small_matrices()

    @pl.when(jnp.logical_not(early))
    def _():
        copies[1].start()
        copies[1].wait()

    def sigma(n):
        left = 1.0 - jnp.full((16, 128), ids_ref[n]).astype(F32) / TOTAL
        return 3.0 * left / (1.0 + 2.0 * left)

    for t in range(WINDOW):
        deltas[t] = sigma(t + 1) - sigma(t)

    def doubled(x):
        return jnp.concatenate([x, x], axis=1)

    def inverse_deviation(x, xx):
        term = (dot(xx, g12[...]) + dot(x, g3[...])) * x.astype(F32)
        lane = lax.broadcasted_iota(jnp.int32, term.shape, 1)
        first = jnp.sum(jnp.where(lane < 64, term, 0.0), axis=1, keepdims=True)
        second = jnp.sum(jnp.where(lane < 64, 0.0, term), axis=1, keepdims=True)
        return lax.rsqrt(first + EPS), lax.rsqrt(second + EPS)

    def bias_of(start):
        return bias[0:1, start:start + HD] + bias[1:2, start:start + HD]

    def project(x, begin):
        x = x.reshape(x.shape[0] * 16, 128)
        xx = doubled(x)
        va, vb = inverse_deviation(x, xx)
        rows = slice(begin, begin + 2 * x.shape[0])
        for h in range(HEADS):
            start = h * 3 * HD + HD
            kva = dot(xx, wa[:, start:start + 2 * HD]) * va
            kvb = dot(xx, wb[:, start:start + 2 * HD]) * vb
            kv = jnp.concatenate([kva, kvb], axis=0)
            keys = kv[:, 0:HD] + bias_of(start)
            square = jnp.mean(keys * keys, axis=1, keepdims=True)
            keys_ref[h, rows] = (keys * lax.rsqrt(square + EPS)).astype(BF16)
            values_ref[h, rows, 0:HD] = kv[:, HD:].astype(BF16)

    def half_copy(buffer, which, n, index):
        part = buffer.at[which, pl.ds(n * 16, 16)]
        return pltpu.make_async_remote_copy(
            src_ref=part, dst_ref=part, send_sem=h_s.at[index], recv_sem=h_r.at[index],
            device_id=sibling, device_id_type=MESH,
        )

    def make_queries(blocks_in, begin):
        gains = qg_ref[...] * kg_ref[...] * (HD ** -0.5 * math.log2(math.e))
        xq = jnp.concatenate(blocks_in, axis=0)
        xxq = doubled(xq)
        ra, rb = inverse_deviation(xq, xxq)
        for h in range(HEADS):
            start = h * 3 * HD
            qa = dot(xxq, wa[:, start:start + HD]) * ra
            qb = dot(xxq, wb[:, start:start + HD]) * rb
            q = jnp.concatenate([qa, qb], axis=0) + bias_of(start)
            q = q * lax.rsqrt(jnp.mean(q * q, axis=1, keepdims=True) + EPS) * gains
            queries_ref[h, begin:begin + 128] = q.astype(BF16)
        return xxq

    def attend(rows, inputs):
        heads = []
        for h in range(HEADS):
            weights = jnp.exp2(dot_t(queries_ref[h, 0:rows], keys_ref[h])).astype(BF16)
            summed = dot(weights, values_ref[h])
            heads.append((summed[:, 0:HD] / summed[:, HD:] + bias_of((3 * h + 2) * HD)).astype(BF16))
        attention = jnp.concatenate(heads, axis=1)
        out = []
        for n, xxq in enumerate(inputs):
            pair = jnp.concatenate(
                [attention[n * 128:n * 128 + 64], attention[n * 128 + 64:n * 128 + 128]], axis=1
            )
            out.append(
                (dot(pair, nw[0]) + dot(pair, nw[1]) + dot(xxq, efw[...])).reshape(4, 16, 128)
            )
        return out

    def first_sweep():
        blocks(xb1, 15, a_s.at[0], a_r.at[0]).wait_recv()
        half_copy(xb1, core, 0, 0).start()
        xxq = make_queries([xb1[core, z * 4 + i] for i in range(4)], 0)
        project(xb1[core, 0:16], 0)
        half_copy(xb1, 1 - core, 0, 0).wait_recv()
        project(xb1[1 - core, 0:16], 512)
        blocks(xb1, 16, a_s.at[0], a_r.at[1]).wait_recv()
        half_copy(xb1, core, 1, 1).start()
        xxq2 = make_queries([xb1[core, 16 + z * 4 + i] for i in range(4)], 128)
        project(xb1[core, 16:32], 1024)
        half_copy(xb1, 1 - core, 1, 1).wait_recv()
        project(xb1[1 - core, 16:32], 1536)
        first, second = attend(256, (xxq, xxq2))
        part1[0] = first.astype(BF16)
        part1[1] = second.astype(BF16)

    def second_sweep():
        one = z // 2
        two = 1 - one
        blocks(xb2, 14, b_s.at[0], b_r.at[one]).wait_recv()
        half_copy(xb2, core, one, 2).start()
        xxq = make_queries([xb2[core, z * 8 + i * 2] for i in range(4)], 0)
        xxq2 = make_queries([xb2[core, z * 8 + i * 2 + 1] for i in range(4)], 128)
        project(xb2[core, pl.ds(one * 16, 16)], 0)
        blocks(xb2, 16, b_s.at[0], b_r.at[two]).wait_recv()
        half_copy(xb2, core, two, 3).start()
        project(xb2[core, pl.ds(two * 16, 16)], 512)
        half_copy(xb2, 1 - core, one, 2).wait_recv()
        half_copy(xb2, 1 - core, two, 3).wait_recv()
        project(xb2[1 - core], 1024)
        first, second = attend(256, (xxq, xxq2))
        part2[0] = first.astype(BF16)
        part2[1] = second.astype(BF16)

    def r_copy(t, i):
        return pltpu.make_async_remote_copy(
            src_ref=part1.at[:, i], dst_ref=box.at[y * 4 + c], send_sem=out_s.at[0], recv_sem=r_r.at[y],
            device_id=device(i, z, t), device_id_type=MESH,
        )

    def o_copy(t, h, i):
        return pltpu.make_async_remote_copy(
            src_ref=part2.at[h, i], dst_ref=final_box.at[y * 4 + c], send_sem=out2_s.at[0], recv_sem=o_r.at[y],
            device_id=device(t, partner if h else z, i), device_id_type=MESH,
        )

    def zero_copy(t, h):
        return pltpu.make_async_remote_copy(
            src_ref=zero_sum.at[h], dst_ref=zero_box, send_sem=zero_s.at[0], recv_sem=o_r.at[0],
            device_id=device(t, partner if h else z, c), device_id_type=MESH,
        )

    def boxes(count, recv):
        part = box.at[pl.ds(0, count)]
        return pltpu.make_async_remote_copy(
            src_ref=part, dst_ref=part, send_sem=out_s.at[0], recv_sem=recv, device_id=sibling, device_id_type=MESH,
        )

    def final_boxes(count, recv):
        part = final_box.at[pl.ds(0, count)]
        return pltpu.make_async_remote_copy(
            src_ref=part, dst_ref=part, send_sem=out2_s.at[0], recv_sem=recv, device_id=sibling, device_id_type=MESH,
        )

    def send_out():
        for t in range(1, WINDOW):
            @pl.when(t >= y)
            def _():
                for i in range(4):
                    mine = jnp.logical_and(t == c, i == y)
                    o_copy(t, 1, i).start()

                    @pl.when(mine)
                    def _():
                        final_box[y * 4 + c] = part2[0, i]

                    @pl.when(jnp.logical_not(mine))
                    def _():
                        o_copy(t, 0, i).start()

    @pl.when(worker)
    def _():
        first_sweep()
        for t in range(1, WINDOW):
            @pl.when(t > y)
            def _():
                for i in range(4):
                    r_copy(t, i).start()

    @pl.when(jnp.logical_and(early, y > 0))
    def _():
        @pl.when(y != c)
        def _():
            n_copy(0).wait_recv()

        late_noise = pltpu.make_async_remote_copy(
            src_ref=own_noise, dst_ref=red_noise.at[1], send_sem=n_s.at[0], recv_sem=n_r.at[1],
            device_id=sibling, device_id_type=MESH,
        )
        late_noise.wait_recv()
        next_inputs[...] = red_noise[...]
        for t in range(3):
            @pl.when(t < y)
            def _():
                boxes(4, r_r.at[t]).wait_recv()
                total = sum(box[t * 4 + cc].astype(F32) for cc in range(4))
                next_inputs[...] += deltas[t][None] * total
                if t == 0:
                    zero_sum[...] = total
        place = near_z * 8 + c * 2
        xb2[core, pl.ds(place, 2)] = next_inputs[...].astype(BF16)
        part = xb2.at[core, pl.ds(place, 2)]
        for dz in (3, -3, 2, -2, 1, -1, 0):
            @pl.when(jnp.logical_and(z + dz >= 0, z + dz < 4))
            def _():
                for dx in (2, 1, 3, 0):
                    if dx or dz:
                        pltpu.make_async_remote_copy(
                            src_ref=part, dst_ref=part, send_sem=b_s.at[0], recv_sem=b_r.at[z // 2],
                            device_id=device(c + dx, z + dz, y), device_id_type=MESH,
                        ).start()

        @pl.when(y == 1)
        def _():
            for t in range(WINDOW):
                for n in range(2):
                    if t == 1 and n == 0:
                        @pl.when(c != 1)
                        def _():
                            zero_copy(t, n).start()

                        @pl.when(c == 1)
                        def _():
                            zero_box[...] = zero_sum[0]
                    else:
                        zero_copy(t, n).start()

    @pl.when(jnp.logical_and(early, y > 0))
    def _():
        second_sweep()
        send_out()

    @pl.when(worker)
    def _():
        blocks(xb1, 11, a_s.at[0], a_r.at[0]).wait_send()
        half_copy(xb1, core, 0, 0).wait_send()
        half_copy(xb1, core, 1, 1).wait_send()
        for t in range(3):
            @pl.when(y == t)
            def _():
                boxes(4 * (3 - t), r_r.at[0]).wait_send()

    @pl.when(jnp.logical_not(worker))
    def _():
        blocks(xb1, 12, a_s.at[0], a_r.at[0]).wait_send()

    @pl.when(y == c)
    def _():
        for t in range(1, WINDOW):
            @pl.when(jnp.logical_or(y != t, z >= 4))
            def _():
                n_copy(t).wait_send()

    @pl.when(jnp.logical_and(early, y > 0))
    def _():
        part = xb2.at[core, pl.ds(0, 30)]
        pltpu.make_async_remote_copy(
            src_ref=part, dst_ref=part, send_sem=b_s.at[0], recv_sem=b_r.at[0],
            device_id=sibling, device_id_type=MESH,
        ).wait_send()
        half_copy(xb2, core, 0, 2).wait_send()
        half_copy(xb2, core, 1, 3).wait_send()
        for t in range(1, WINDOW):
            for kept in range(2):
                @pl.when(jnp.logical_and(y == t, (c >= t) == jnp.bool_(kept)))
                def _():
                    final_boxes(8 * (4 - t) - kept, o_r.at[0]).wait_send()

        def zero_sent(count):
            part = lat_rows.at[pl.ds(0, count)]
            pltpu.make_async_remote_copy(
                src_ref=part, dst_ref=part, send_sem=zero_s.at[0], recv_sem=o_r.at[0],
                device_id=sibling, device_id_type=MESH,
            ).wait_send()

        @pl.when(jnp.logical_and(y == 1, c == 1))
        def _():
            zero_sent(7)

        @pl.when(jnp.logical_and(y == 1, c != 1))
        def _():
            zero_sent(8)

    lat_acc[...] = own_noise[...]
    for t in range(WINDOW):
        @pl.when(t <= c)
        def _():
            if t == 0:
                @pl.when(jnp.logical_not(jnp.logical_and(early, jnp.logical_and(y == 1, c == 1))))
                def _():
                    pltpu.make_async_remote_copy(
                        src_ref=zero_box, dst_ref=zero_box, send_sem=zero_s.at[0], recv_sem=o_r.at[0],
                        device_id=sibling, device_id_type=MESH,
                    ).wait_recv()

                total = zero_box[...]
            else:
                @pl.when(jnp.logical_and(early, t == y))
                def _():
                    final_boxes(3, o_r.at[t]).wait_recv()

                @pl.when(jnp.logical_not(jnp.logical_and(early, t == y)))
                def _():
                    final_boxes(4, o_r.at[t]).wait_recv()

                first = t * 4
                total = sum(final_box[first + cc].astype(F32) for cc in range(4))
            lat_acc[...] += deltas[t] * total
            dr_acc[...] = total
    out_ref[0:16, 0:C] = lat_acc[:, 0:C]
    out_ref[16:32, 0:C] = lat_acc[:, C:]
    out_ref[0:16, C:] = dr_acc[:, 0:C]
    out_ref[16:32, C:] = dr_acc[:, C:]


def body(
    noise, step_ids, mod_table, embed_weight, qkv_weight, q_gain, k_gain, out_weight, final_weight
):
    hbm = pl.BlockSpec(memory_space=pltpu.HBM)
    vmem = pl.BlockSpec(memory_space=pltpu.VMEM)
    out = pltpu.VMEM((32, 2 * C), F32)
    dma = pltpu.SemaphoreType.DMA
    both = pl.pallas_call(
        kernel,
        out_shape=out,
        in_specs=[hbm] * 9,
        out_specs=vmem,
        scratch_shapes=[
            pltpu.VMEM((32, C), F32),
            pltpu.SMEM((WINDOW + 1,), jnp.int32),
            pltpu.VMEM((3, TOTAL, D), F32),
            pltpu.VMEM((C, D), BF16),
            pltpu.VMEM((D, COLS), BF16),
            pltpu.VMEM((1, HD), F32),
            pltpu.VMEM((1, HD), F32),
            pltpu.VMEM((HEADS * HD, D), BF16),
            pltpu.VMEM((C, D), F32),
            dma((8,)),
            dma((1,)),
            pltpu.VMEM((16, 128), F32),
            pltpu.VMEM((2, 16, 128), F32),
            pltpu.VMEM((2, 32, 16, 128), BF16),
            pltpu.VMEM((2, 32, 16, 128), BF16),
            pltpu.VMEM((HEADS, 2048, HD), BF16),
            pltpu.VMEM((HEADS, 2048, 2 * HD), BF16),
            pltpu.VMEM((HEADS, 256, HD), BF16),
            pltpu.VMEM((2, 4, 16, 128), BF16),
            pltpu.VMEM((2, 4, 16, 128), BF16),
            pltpu.VMEM((12, 2, 16, 128), BF16),
            pltpu.VMEM((24, 16, 128), BF16),
            pltpu.VMEM((2, 16, 128), F32),
            pltpu.VMEM((16, 128), F32),
            pltpu.VMEM((8, 16, 128), F32),
            pltpu.VMEM((144, COLS), F32),
            pltpu.VMEM((256, COLS), BF16),
            pltpu.VMEM((256, COLS), BF16),
            pltpu.VMEM((8, COLS), F32),
            pltpu.VMEM((256, 128), BF16),
            pltpu.VMEM((128, 128), BF16),
            pltpu.VMEM((2, 768, 128), BF16),
            pltpu.VMEM((256, 128), BF16),
            pltpu.VMEM((144, D), BF16),
            pltpu.VMEM((16, 128), F32),
            pltpu.VMEM((16, 128), F32),
            pltpu.VMEM((2, 16, 128), F32),
            pltpu.VMEM((WINDOW, 16, 128), F32),
            dma((1,)), dma((2,)), dma((4,)), dma((2,)), dma((4,)), dma((4,)),
            dma((3,)), dma((1,)), dma((2,)), dma((1,)), dma((1,)), dma((1,)), dma((4,)),
        ],
        compiler_params=pltpu.CompilerParams(
            collective_id=0, has_side_effects=True, vmem_limit_bytes=60 * 1024 * 1024
        ),
        cost_estimate=pl.CostEstimate(flops=4_000_000_000, bytes_accessed=14_000_000, transcendentals=1_700_000),
    )(
        noise, step_ids, mod_table.transpose(1, 0, 2), embed_weight, qkv_weight,
        q_gain.reshape(1, HD), k_gain.reshape(1, HD), out_weight, final_weight.T,
    )
    return both[None, :, 0:C], both[None, :, C:]


def solution(mesh):
    in_specs = (P("seq", None), P(), P(), P(), P(None, "tm"), P(), P(), P("tm", None), P())
    out_specs = (P("tm", "seq", None), P("tm", "seq", None))
    return jax.shard_map(body, mesh=mesh, in_specs=in_specs, out_specs=out_specs, check_vma=False)
```

```python
import math

import jax
import jax.numpy as jnp
from jax import lax
from jax.experimental import pallas as pl
from jax.experimental.pallas import tpu as pltpu
from jax.sharding import PartitionSpec as P

MESH = pl.DeviceIdType.MESH
F32 = jnp.float32
BF16 = jnp.bfloat16
C = 64
D = 3072
HD = 128
HEADS = 3
WINDOW = 4
TOTAL = 28
EPS = 1e-6
PARTS = 6
DEPTH = D // PARTS
COLS = 3 * HD * HEADS
FAR_FIRST = sorted(
    [(a, b) for a in range(8) for b in range(4) if a or b],
    key=lambda ab: -(min(ab[0], 8 - ab[0]) + min(ab[1], 4 - ab[1])),
)
CONTRACT_LAST = (((1,), (1,)), ((), ()))


def dot(left, right):
    return jnp.dot(left, right, preferred_element_type=F32)


def dot_t(left, right):
    return lax.dot_general(left, right, CONTRACT_LAST, preferred_element_type=F32)


def split(value, pieces):
    out = []
    for _ in range(pieces):
        piece = value.astype(BF16)
        out.append(piece)
        value = value - piece.astype(F32)
    return out


def left_half(value):
    return jnp.concatenate([value, jnp.zeros_like(value)], axis=1)


def right_half(value):
    return jnp.concatenate([jnp.zeros_like(value), value], axis=1)


def kernel(
    noise_ref, ids_in, mod_ref, e_ref, w_ref, qgain_ref, kgain_ref, o_ref, f_ref,
    out_ref,
    noise_in, ids_ref, mod_in, e_in, w_in, qg_ref, kg_ref, o_in, f_in, local_sem, w_sem,
    own_noise, red_noise, xb1, xb2, keys_ref, values_ref, queries_ref, early_sum, part1, part2, box, final_box, zero_sum, zero_box,
    lat_rows,
    proj, wa, wb, bias, g12, g3, nw, efw, a_hi, lat_acc, dr_acc, next_inputs, deltas,
    a_s, a_r, n_s, n_r, h_s, h_r, r_r, b_s, b_r, out_s, out2_s, zero_s, o_r,
):
    c = lax.axis_index("tm")
    s = lax.axis_index("seq")
    z = s // 8
    y = (s // 2) % 4
    core = s % 2

    def device(cc, zz, yy):
        return (cc % 4, (zz % 8) * 8 + (yy % 4) * 2 + core)

    sibling = (c, z * 8 + y * 2 + 1 - core)

    noise_copy = pltpu.make_async_copy(noise_ref, noise_in, local_sem.at[0])
    noise_copy.start()

    barrier = pltpu.get_barrier_semaphore()
    early = z < 4
    worker = jnp.logical_and(early, y < 3)
    half = z // 4
    near_z = jnp.where(early, z, (z + 2) % 4)
    partner = 4 + (z + 2) % 4

    def greet(target):
        pl.semaphore_signal(barrier, inc=1, device_id=target, device_id_type=MESH)

    @pl.when(early)
    def _():
        for dz, dy in FAR_FIRST:
            greet(device(c, z + dz, y + dy))
        for dx in range(1, 4):
            for dy in range(4):
                greet(device(c + dx, z, y + dy))
        greet(sibling)

    copies = [
        pltpu.make_async_copy(e_ref, e_in, local_sem.at[1]),
        pltpu.make_async_copy(ids_in, ids_ref, local_sem.at[2]),
        pltpu.make_async_copy(mod_ref, mod_in, local_sem.at[3]),
        pltpu.make_async_copy(f_ref, f_in, local_sem.at[4]),
        pltpu.make_async_copy(o_ref, o_in, local_sem.at[5]),
        pltpu.make_async_copy(qgain_ref, qg_ref, local_sem.at[6]),
        pltpu.make_async_copy(kgain_ref, kg_ref, local_sem.at[7]),
    ]
    w_copies = [
        pltpu.make_async_copy(
            w_ref.at[pl.ds(n * DEPTH, DEPTH)], w_in.at[pl.ds(n * DEPTH, DEPTH)], w_sem.at[0]
        )
        for n in range(PARTS)
    ]

    def fetch():
        for copy in copies + w_copies:
            copy.start()

    def small_matrices():
        for copy in copies[:3]:
            copy.wait()
        embed = e_in[...].astype(F32)
        centred = embed - jnp.mean(embed, axis=1, keepdims=True)
        here = pl.ds(ids_ref[y], 1)
        shift = mod_in[0, here]
        scale = mod_in[1, here]
        gate = mod_in[2, here]
        scaled = split(centred * (1.0 + scale), 2)
        a_hi[0:64] = scaled[0]
        a_hi[64:128] = scaled[1]
        shifts = split(shift, 2)
        row = lax.broadcasted_iota(jnp.int32, (16, D), 0)
        a_hi[128:144] = jnp.where(
            row == 0, jnp.broadcast_to(shift, (16, D)),
            jnp.where(row == 1, jnp.broadcast_to(shift - shifts[0].astype(F32), (16, D)), 0.0),
        ).astype(BF16)

        pieces = split(centred, 3)
        stacked = jnp.concatenate(pieces, axis=0)
        gram = dot_t(stacked, stacked)
        gram = gram[0:64] + gram[64:128] + gram[128:192]
        gram = (gram[:, 0:64] + gram[:, 64:128] + gram[:, 128:192]) * (1.0 / D)
        g1, g2, gl = split(gram, 3)
        g12[0:64] = left_half(g1)
        g12[64:128] = right_half(g1)
        g12[128:192] = left_half(g2)
        g12[192:256] = right_half(g2)
        g3[0:64] = left_half(gl)
        g3[64:128] = right_half(gl)

        for copy in copies[3:]:
            copy.wait()
        final = f_in[...]
        final_hl = jnp.concatenate(split(final, 2), axis=0)
        gated_hl = jnp.concatenate(split(final * gate, 2), axis=0)
        head_out = dot_t(o_in[...], gated_hl)
        embed_out = dot_t(e_in[...], final_hl)
        head_out = head_out[:, 0:64] + head_out[:, 64:128]
        own = (c == 0).astype(F32)
        embed_out = (embed_out[:, 0:64] + embed_out[:, 64:128]) * own
        for n, value in enumerate(split(head_out, 2)):
            nw[n, 0:384] = left_half(value)
            nw[n, 384:768] = right_half(value)
        for n, value in enumerate(split(embed_out, 2)):
            efw[n * 128:n * 128 + 64] = left_half(value)
            efw[n * 128 + 64:n * 128 + 128] = right_half(value)
        pltpu.make_async_copy(w_ref, w_in, w_sem.at[0]).wait()
        proj[...] = dot(a_hi[...], w_in[...])
        small = proj[0:64] + proj[64:128]
        bias[...] = proj[128:136]
        small_hi, small_lo = split(small, 2)
        none = jnp.zeros((64, COLS), BF16)
        for n, value in enumerate((small_hi, none, small_lo, none)):
            wa[n * 64:(n + 1) * 64] = value
        for n, value in enumerate((none, small_hi, none, small_lo)):
            wb[n * 64:(n + 1) * 64] = value

    @pl.when(early)
    def _():
        fetch()
        values_ref[:, :, HD:] = jnp.ones((HEADS, 2048, HD), BF16)

    noise_copy.wait()
    packed = jnp.concatenate([noise_in[0:16], noise_in[16:32]], axis=1)
    own_noise[...] = packed
    slot = half * 16 + near_z * 4 + y
    xb1[core, slot] = packed.astype(BF16)

    @pl.when(early)
    def _():
        pl.semaphore_wait(barrier, 28)

    @pl.when(jnp.logical_not(early))
    def _():
        pl.semaphore_wait(barrier, 16)


    def a_copy(zz, yy):
        return pltpu.make_async_remote_copy(
            src_ref=xb1.at[core, slot], dst_ref=xb1.at[core, slot], send_sem=a_s.at[0], recv_sem=a_r.at[half],
            device_id=device(c, zz, yy), device_id_type=MESH,
        )

    def blocks(buffer, count, send, recv):
        part = buffer.at[core, pl.ds(0, count)]
        return pltpu.make_async_remote_copy(
            src_ref=part, dst_ref=part, send_sem=send, recv_sem=recv, device_id=sibling, device_id_type=MESH,
        )

    @pl.when(early)
    def _():
        for zz in range(4):
            for yy in range(3):
                @pl.when(jnp.logical_not(jnp.logical_and(z == zz, y == yy)))
                def _():
                    a_copy(zz, yy).start()

    @pl.when(jnp.logical_not(early))
    def _():
        for dz in (4, 3, 5, 2, 6, 1, 7):
            @pl.when((z + dz) % 8 < 4)
            def _():
                for yy in range(3):
                    a_copy(z + dz, yy).start()

    def n_copy(t):
        return pltpu.make_async_remote_copy(
            src_ref=own_noise, dst_ref=red_noise.at[half], send_sem=n_s.at[t], recv_sem=n_r.at[half],
            device_id=device(c, near_z, t), device_id_type=MESH,
        )

    @pl.when(y == c)
    def _():
        @pl.when(jnp.logical_and(early, y > 0))
        def _():
            red_noise[0] = own_noise[...]

        for t in range(1, WINDOW):
            @pl.when(jnp.logical_or(y != t, z >= 4))
            def _():
                n_copy(t).start()

    @pl.when(early)
    def _():
        small_matrices()

    @pl.when(jnp.logical_not(early))
    def _():
        copies[1].start()
        copies[1].wait()

    def sigma(n):
        left = 1.0 - jnp.full((16, 128), ids_ref[n]).astype(F32) / TOTAL
        return 3.0 * left / (1.0 + 2.0 * left)

    for t in range(WINDOW):
        deltas[t] = sigma(t + 1) - sigma(t)

    def doubled(x):
        return jnp.concatenate([x, x], axis=1)

    def inverse_deviation(x, xx):
        term = (dot(xx, g12[...]) + dot(x, g3[...])) * x.astype(F32)
        lane = lax.broadcasted_iota(jnp.int32, term.shape, 1)
        first = jnp.sum(jnp.where(lane < 64, term, 0.0), axis=1, keepdims=True)
        second = jnp.sum(jnp.where(lane < 64, 0.0, term), axis=1, keepdims=True)
        return lax.rsqrt(first + EPS), lax.rsqrt(second + EPS)

    def bias_of(start):
        return bias[0:1, start:start + HD] + bias[1:2, start:start + HD]

    def project(x, begin):
        x = x.reshape(x.shape[0] * 16, 128)
        xx = doubled(x)
        va, vb = inverse_deviation(x, xx)
        rows = slice(begin, begin + 2 * x.shape[0])
        for h in range(HEADS):
            start = h * 3 * HD + HD
            kva = dot(xx, wa[:, start:start + 2 * HD]) * va
            kvb = dot(xx, wb[:, start:start + 2 * HD]) * vb
            kv = jnp.concatenate([kva, kvb], axis=0)
            keys = kv[:, 0:HD] + bias_of(start)
            square = jnp.mean(keys * keys, axis=1, keepdims=True)
            keys_ref[h, rows] = (keys * lax.rsqrt(square + EPS)).astype(BF16)
            values_ref[h, rows, 0:HD] = kv[:, HD:].astype(BF16)

    def half_copy(buffer, which, n, index):
        part = buffer.at[which, pl.ds(n * 16, 16)]
        return pltpu.make_async_remote_copy(
            src_ref=part, dst_ref=part, send_sem=h_s.at[index], recv_sem=h_r.at[index],
            device_id=sibling, device_id_type=MESH,
        )

    def make_queries(blocks_in, begin):
        gains = qg_ref[...] * kg_ref[...] * (HD ** -0.5 * math.log2(math.e))
        xq = jnp.concatenate(blocks_in, axis=0)
        xxq = doubled(xq)
        ra, rb = inverse_deviation(xq, xxq)
        for h in range(HEADS):
            start = h * 3 * HD
            qa = dot(xxq, wa[:, start:start + HD]) * ra
            qb = dot(xxq, wb[:, start:start + HD]) * rb
            q = jnp.concatenate([qa, qb], axis=0) + bias_of(start)
            q = q * lax.rsqrt(jnp.mean(q * q, axis=1, keepdims=True) + EPS) * gains
            queries_ref[h, begin:begin + 128] = q.astype(BF16)
        return xxq

    def weighted(h, rows, keys):
        weights = jnp.exp2(dot_t(queries_ref[h, rows], keys_ref[h, keys])).astype(BF16)
        return dot(weights, values_ref[h, keys])

    def finish(sums, xxq):
        heads = []
        for h, summed in enumerate(sums):
            heads.append((summed[:, 0:HD] / summed[:, HD:] + bias_of((3 * h + 2) * HD)).astype(BF16))
        attention = jnp.concatenate(heads, axis=1)
        pair = jnp.concatenate([attention[0:64], attention[64:128]], axis=1)
        result = dot(pair, nw[0]) + dot(pair, nw[1]) + dot(xxq, efw[...])
        return result.reshape(4, 16, 128).astype(BF16)

    low, high, every = slice(0, 128), slice(128, 256), slice(0, 2048)

    def first_sweep():
        blocks(xb1, 15, a_s.at[0], a_r.at[0]).wait_recv()
        half_copy(xb1, core, 0, 0).start()
        xxq = make_queries([xb1[core, z * 4 + i] for i in range(4)], 0)
        project(xb1[core, 0:16], 0)
        half_copy(xb1, 1 - core, 0, 0).wait_recv()
        project(xb1[1 - core, 0:16], 512)
        for h in range(HEADS):
            early_sum[h] = weighted(h, low, slice(0, 1024))
        blocks(xb1, 16, a_s.at[0], a_r.at[1]).wait_recv()
        half_copy(xb1, core, 1, 1).start()
        xxq2 = make_queries([xb1[core, 16 + z * 4 + i] for i in range(4)], 128)
        project(xb1[core, 16:32], 1024)
        half_copy(xb1, 1 - core, 1, 1).wait_recv()
        project(xb1[1 - core, 16:32], 1536)
        first = [early_sum[h] + weighted(h, low, slice(1024, 2048)) for h in range(HEADS)]
        second = [weighted(h, high, every) for h in range(HEADS)]
        part1[0] = finish(first, xxq)
        part1[1] = finish(second, xxq2)

    def second_sweep():
        one = z // 2
        two = 1 - one
        blocks(xb2, 14, b_s.at[0], b_r.at[one]).wait_recv()
        half_copy(xb2, core, one, 2).start()
        xxq = make_queries([xb2[core, z * 8 + i * 2] for i in range(4)], 0)
        project(xb2[core, pl.ds(one * 16, 16)], 0)
        blocks(xb2, 16, b_s.at[0], b_r.at[two]).wait_recv()
        half_copy(xb2, core, two, 3).start()
        half_copy(xb2, 1 - core, one, 2).wait_recv()
        project(jnp.concatenate([xb2[1 - core, pl.ds(one * 16, 16)], xb2[core, pl.ds(two * 16, 16)]], axis=0), 512)
        half_copy(xb2, 1 - core, two, 3).wait_recv()
        project(xb2[1 - core, pl.ds(two * 16, 16)], 1536)
        part2[0] = finish([weighted(h, low, every) for h in range(HEADS)], xxq)
        send_out(0)
        xxq2 = make_queries([xb2[core, z * 8 + i * 2 + 1] for i in range(4)], 128)
        part2[1] = finish([weighted(h, high, every) for h in range(HEADS)], xxq2)
        send_out(1)

    def r_copy(t, i):
        return pltpu.make_async_remote_copy(
            src_ref=part1.at[:, i], dst_ref=box.at[y * 4 + c], send_sem=out_s.at[0], recv_sem=r_r.at[y],
            device_id=device(i, z, t), device_id_type=MESH,
        )

    def o_copy(t, h, i):
        return pltpu.make_async_remote_copy(
            src_ref=part2.at[h, i], dst_ref=final_box.at[y * 4 + c], send_sem=out2_s.at[0], recv_sem=o_r.at[y],
            device_id=device(t, partner if h else z, i), device_id_type=MESH,
        )

    def zero_copy(t, h):
        return pltpu.make_async_remote_copy(
            src_ref=zero_sum.at[h], dst_ref=zero_box, send_sem=zero_s.at[0], recv_sem=o_r.at[0],
            device_id=device(t, partner if h else z, c), device_id_type=MESH,
        )

    def boxes(count, recv):
        part = box.at[pl.ds(0, count)]
        return pltpu.make_async_remote_copy(
            src_ref=part, dst_ref=part, send_sem=out_s.at[0], recv_sem=recv, device_id=sibling, device_id_type=MESH,
        )

    def final_boxes(count, recv):
        part = final_box.at[pl.ds(0, count)]
        return pltpu.make_async_remote_copy(
            src_ref=part, dst_ref=part, send_sem=out2_s.at[0], recv_sem=recv, device_id=sibling, device_id_type=MESH,
        )

    def send_out(h):
        for t in range(1, WINDOW):
            @pl.when(t >= y)
            def _():
                for i in range(4):
                    if h:
                        o_copy(t, h, i).start()
                        continue
                    mine = jnp.logical_and(t == c, i == y)

                    @pl.when(mine)
                    def _():
                        final_box[y * 4 + c] = part2[0, i]

                    @pl.when(jnp.logical_not(mine))
                    def _():
                        o_copy(t, h, i).start()

    @pl.when(worker)
    def _():
        first_sweep()
        for t in range(1, WINDOW):
            @pl.when(t > y)
            def _():
                for i in range(4):
                    r_copy(t, i).start()

    @pl.when(jnp.logical_and(early, y > 0))
    def _():
        @pl.when(y != c)
        def _():
            n_copy(0).wait_recv()

        late_noise = pltpu.make_async_remote_copy(
            src_ref=own_noise, dst_ref=red_noise.at[1], send_sem=n_s.at[0], recv_sem=n_r.at[1],
            device_id=sibling, device_id_type=MESH,
        )
        late_noise.wait_recv()
        next_inputs[...] = red_noise[...]
        for t in range(3):
            @pl.when(t < y)
            def _():
                boxes(4, r_r.at[t]).wait_recv()
                total = sum(box[t * 4 + cc].astype(F32) for cc in range(4))
                next_inputs[...] += deltas[t][None] * total
                if t == 0:
                    zero_sum[...] = total
        place = near_z * 8 + c * 2
        xb2[core, pl.ds(place, 2)] = next_inputs[...].astype(BF16)
        part = xb2.at[core, pl.ds(place, 2)]
        for dz in (3, -3, 2, -2, 1, -1, 0):
            @pl.when(jnp.logical_and(z + dz >= 0, z + dz < 4))
            def _():
                for dx in (2, 1, 3, 0):
                    if dx or dz:
                        pltpu.make_async_remote_copy(
                            src_ref=part, dst_ref=part, send_sem=b_s.at[0], recv_sem=b_r.at[z // 2],
                            device_id=device(c + dx, z + dz, y), device_id_type=MESH,
                        ).start()

        @pl.when(y == 1)
        def _():
            for t in range(WINDOW):
                for n in range(2):
                    if t == 1 and n == 0:
                        @pl.when(c != 1)
                        def _():
                            zero_copy(t, n).start()

                        @pl.when(c == 1)
                        def _():
                            zero_box[...] = zero_sum[0]
                    else:
                        zero_copy(t, n).start()

    @pl.when(jnp.logical_and(early, y > 0))
    def _():
        second_sweep()

    @pl.when(worker)
    def _():
        blocks(xb1, 11, a_s.at[0], a_r.at[0]).wait_send()
        half_copy(xb1, core, 0, 0).wait_send()
        half_copy(xb1, core, 1, 1).wait_send()
        for t in range(3):
            @pl.when(y == t)
            def _():
                boxes(4 * (3 - t), r_r.at[0]).wait_send()

    @pl.when(jnp.logical_not(worker))
    def _():
        blocks(xb1, 12, a_s.at[0], a_r.at[0]).wait_send()

    @pl.when(y == c)
    def _():
        for t in range(1, WINDOW):
            @pl.when(jnp.logical_or(y != t, z >= 4))
            def _():
                n_copy(t).wait_send()

    @pl.when(jnp.logical_and(early, y > 0))
    def _():
        part = xb2.at[core, pl.ds(0, 30)]
        pltpu.make_async_remote_copy(
            src_ref=part, dst_ref=part, send_sem=b_s.at[0], recv_sem=b_r.at[0],
            device_id=sibling, device_id_type=MESH,
        ).wait_send()
        half_copy(xb2, core, 0, 2).wait_send()
        half_copy(xb2, core, 1, 3).wait_send()
        for t in range(1, WINDOW):
            for kept in range(2):
                @pl.when(jnp.logical_and(y == t, (c >= t) == jnp.bool_(kept)))
                def _():
                    final_boxes(8 * (4 - t) - kept, o_r.at[0]).wait_send()

        def zero_sent(count):
            part = lat_rows.at[pl.ds(0, count)]
            pltpu.make_async_remote_copy(
                src_ref=part, dst_ref=part, send_sem=zero_s.at[0], recv_sem=o_r.at[0],
                device_id=sibling, device_id_type=MESH,
            ).wait_send()

        @pl.when(jnp.logical_and(y == 1, c == 1))
        def _():
            zero_sent(7)

        @pl.when(jnp.logical_and(y == 1, c != 1))
        def _():
            zero_sent(8)

    lat_acc[...] = own_noise[...]
    for t in range(WINDOW):
        @pl.when(t <= c)
        def _():
            if t == 0:
                @pl.when(jnp.logical_not(jnp.logical_and(early, jnp.logical_and(y == 1, c == 1))))
                def _():
                    pltpu.make_async_remote_copy(
                        src_ref=zero_box, dst_ref=zero_box, send_sem=zero_s.at[0], recv_sem=o_r.at[0],
                        device_id=sibling, device_id_type=MESH,
                    ).wait_recv()

                total = zero_box[...]
            else:
                @pl.when(jnp.logical_and(early, t == y))
                def _():
                    final_boxes(3, o_r.at[t]).wait_recv()

                @pl.when(jnp.logical_not(jnp.logical_and(early, t == y)))
                def _():
                    final_boxes(4, o_r.at[t]).wait_recv()

                first = t * 4
                total = sum(final_box[first + cc].astype(F32) for cc in range(4))
            lat_acc[...] += deltas[t] * total
            dr_acc[...] = total
    out_ref[0:16, 0:C] = lat_acc[:, 0:C]
    out_ref[16:32, 0:C] = lat_acc[:, C:]
    out_ref[0:16, C:] = dr_acc[:, 0:C]
    out_ref[16:32, C:] = dr_acc[:, C:]


def body(
    noise, step_ids, mod_table, embed_weight, qkv_weight, q_gain, k_gain, out_weight, final_weight
):
    hbm = pl.BlockSpec(memory_space=pltpu.HBM)
    vmem = pl.BlockSpec(memory_space=pltpu.VMEM)
    out = pltpu.VMEM((32, 2 * C), F32)
    dma = pltpu.SemaphoreType.DMA
    both = pl.pallas_call(
        kernel,
        out_shape=out,
        in_specs=[hbm] * 9,
        out_specs=vmem,
        scratch_shapes=[
            pltpu.VMEM((32, C), F32),
            pltpu.SMEM((WINDOW + 1,), jnp.int32),
            pltpu.VMEM((3, TOTAL, D), F32),
            pltpu.VMEM((C, D), BF16),
            pltpu.VMEM((D, COLS), BF16),
            pltpu.VMEM((1, HD), F32),
            pltpu.VMEM((1, HD), F32),
            pltpu.VMEM((HEADS * HD, D), BF16),
            pltpu.VMEM((C, D), F32),
            dma((8,)),
            dma((1,)),
            pltpu.VMEM((16, 128), F32),
            pltpu.VMEM((2, 16, 128), F32),
            pltpu.VMEM((2, 32, 16, 128), BF16),
            pltpu.VMEM((2, 32, 16, 128), BF16),
            pltpu.VMEM((HEADS, 2048, HD), BF16),
            pltpu.VMEM((HEADS, 2048, 2 * HD), BF16),
            pltpu.VMEM((HEADS, 256, HD), BF16),
            pltpu.VMEM((HEADS, 128, 2 * HD), F32),
            pltpu.VMEM((2, 4, 16, 128), BF16),
            pltpu.VMEM((2, 4, 16, 128), BF16),
            pltpu.VMEM((12, 2, 16, 128), BF16),
            pltpu.VMEM((24, 16, 128), BF16),
            pltpu.VMEM((2, 16, 128), F32),
            pltpu.VMEM((16, 128), F32),
            pltpu.VMEM((8, 16, 128), F32),
            pltpu.VMEM((144, COLS), F32),
            pltpu.VMEM((256, COLS), BF16),
            pltpu.VMEM((256, COLS), BF16),
            pltpu.VMEM((8, COLS), F32),
            pltpu.VMEM((256, 128), BF16),
            pltpu.VMEM((128, 128), BF16),
            pltpu.VMEM((2, 768, 128), BF16),
            pltpu.VMEM((256, 128), BF16),
            pltpu.VMEM((144, D), BF16),
            pltpu.VMEM((16, 128), F32),
            pltpu.VMEM((16, 128), F32),
            pltpu.VMEM((2, 16, 128), F32),
            pltpu.VMEM((WINDOW, 16, 128), F32),
            dma((1,)), dma((2,)), dma((4,)), dma((2,)), dma((4,)), dma((4,)),
            dma((3,)), dma((1,)), dma((2,)), dma((1,)), dma((1,)), dma((1,)), dma((4,)),
        ],
        compiler_params=pltpu.CompilerParams(
            collective_id=0, has_side_effects=True, vmem_limit_bytes=60 * 1024 * 1024
        ),
        cost_estimate=pl.CostEstimate(flops=4_000_000_000, bytes_accessed=14_000_000, transcendentals=1_700_000),
    )(
        noise, step_ids, mod_table.transpose(1, 0, 2), embed_weight, qkv_weight,
        q_gain.reshape(1, HD), k_gain.reshape(1, HD), out_weight, final_weight.T,
    )
    return both[None, :, 0:C], both[None, :, C:]


def solution(mesh):
    in_specs = (P("seq", None), P(), P(), P(), P(None, "tm"), P(), P(), P("tm", None), P())
    out_specs = (P("tm", "seq", None), P("tm", "seq", None))
    return jax.shard_map(body, mesh=mesh, in_specs=in_specs, out_specs=out_specs, check_vma=False)
```

```python
import math

import jax
import jax.numpy as jnp
from jax import lax
from jax.experimental import pallas as pl
from jax.experimental.pallas import tpu as pltpu
from jax.sharding import PartitionSpec as P

MESH = pl.DeviceIdType.MESH
F32 = jnp.float32
BF16 = jnp.bfloat16
C = 64
D = 3072
HD = 128
HEADS = 3
WINDOW = 4
TOTAL = 28
EPS = 1e-6
PARTS = 6
DEPTH = D // PARTS
COLS = 3 * HD * HEADS
FAR_FIRST = sorted(
    [(a, b) for a in range(8) for b in range(4) if a or b],
    key=lambda ab: -(min(ab[0], 8 - ab[0]) + min(ab[1], 4 - ab[1])),
)
CONTRACT_LAST = (((1,), (1,)), ((), ()))


def dot(left, right):
    return jnp.dot(left, right, preferred_element_type=F32)


def dot_t(left, right):
    return lax.dot_general(left, right, CONTRACT_LAST, preferred_element_type=F32)


def split(value, pieces):
    out = []
    for _ in range(pieces):
        piece = value.astype(BF16)
        out.append(piece)
        value = value - piece.astype(F32)
    return out


def left_half(value):
    return jnp.concatenate([value, jnp.zeros_like(value)], axis=1)


def right_half(value):
    return jnp.concatenate([jnp.zeros_like(value), value], axis=1)


def kernel(
    noise_ref, ids_in, mod_ref, e_ref, w_ref, qgain_ref, kgain_ref, o_ref, f_ref,
    out_ref,
    noise_in, ids_ref, mod_in, e_in, w_in, qg_ref, kg_ref, o_in, f_in, local_sem, w_sem,
    own_noise, red_noise, xb1, xb2, keys_ref, values_ref, queries_ref, early_sum, part1, part2, box, final_box, zero_sum, zero_box,
    lat_rows,
    proj, wa, wb, bias, g12, g3, nw, efw, a_hi, lat_acc, dr_acc, next_inputs, deltas,
    a_s, a_r, n_s, n_r, h_s, h_r, r_r, b_s, b_r, out_s, out2_s, zero_s, o_r,
):
    c = lax.axis_index("tm")
    s = lax.axis_index("seq")
    z = s // 8
    y = (s // 2) % 4
    core = s % 2

    def device(cc, zz, yy):
        return (cc % 4, (zz % 8) * 8 + (yy % 4) * 2 + core)

    sibling = (c, z * 8 + y * 2 + 1 - core)

    noise_copy = pltpu.make_async_copy(noise_ref, noise_in, local_sem.at[0])
    noise_copy.start()

    barrier = pltpu.get_barrier_semaphore()
    early = z < 4
    worker = jnp.logical_and(early, y < 3)
    half = z // 4
    near_z = jnp.where(early, z, (z + 2) % 4)
    partner = 4 + (z + 2) % 4

    def greet(target):
        pl.semaphore_signal(barrier, inc=1, device_id=target, device_id_type=MESH)

    @pl.when(early)
    def _():
        for n in (4, 5, 6, 7):
            for dy in (2, 1, 3, 0):
                greet(device(c, n, y + dy))
        for n in range(4):
            for dy in (2, 1, 3, 0):
                if dy:
                    greet(device(c, n, y + dy))
                else:
                    @pl.when(z != n)
                    def _():
                        greet(device(c, n, y))
        for dx in range(1, 4):
            for dy in range(4):
                greet(device(c + dx, z, y + dy))
        greet(sibling)

    copies = [
        pltpu.make_async_copy(e_ref, e_in, local_sem.at[1]),
        pltpu.make_async_copy(ids_in, ids_ref, local_sem.at[2]),
        pltpu.make_async_copy(mod_ref, mod_in, local_sem.at[3]),
        pltpu.make_async_copy(f_ref, f_in, local_sem.at[4]),
        pltpu.make_async_copy(o_ref, o_in, local_sem.at[5]),
        pltpu.make_async_copy(qgain_ref, qg_ref, local_sem.at[6]),
        pltpu.make_async_copy(kgain_ref, kg_ref, local_sem.at[7]),
    ]
    w_copies = [
        pltpu.make_async_copy(
            w_ref.at[pl.ds(n * DEPTH, DEPTH)], w_in.at[pl.ds(n * DEPTH, DEPTH)], w_sem.at[0]
        )
        for n in range(PARTS)
    ]

    def fetch():
        for copy in copies + w_copies:
            copy.start()

    def small_matrices():
        for copy in copies[:3]:
            copy.wait()
        embed = e_in[...].astype(F32)
        centred = embed - jnp.mean(embed, axis=1, keepdims=True)
        here = pl.ds(ids_ref[y], 1)
        shift = mod_in[0, here]
        scale = mod_in[1, here]
        gate = mod_in[2, here]
        scaled = split(centred * (1.0 + scale), 2)
        a_hi[0:64] = scaled[0]
        a_hi[64:128] = scaled[1]
        shifts = split(shift, 2)
        row = lax.broadcasted_iota(jnp.int32, (16, D), 0)
        a_hi[128:144] = jnp.where(
            row == 0, jnp.broadcast_to(shift, (16, D)),
            jnp.where(row == 1, jnp.broadcast_to(shift - shifts[0].astype(F32), (16, D)), 0.0),
        ).astype(BF16)

        pieces = split(centred, 3)
        stacked = jnp.concatenate(pieces, axis=0)
        gram = dot_t(stacked, stacked)
        gram = gram[0:64] + gram[64:128] + gram[128:192]
        gram = (gram[:, 0:64] + gram[:, 64:128] + gram[:, 128:192]) * (1.0 / D)
        g1, g2, gl = split(gram, 3)
        g12[0:64] = left_half(g1)
        g12[64:128] = right_half(g1)
        g12[128:192] = left_half(g2)
        g12[192:256] = right_half(g2)
        g3[0:64] = left_half(gl)
        g3[64:128] = right_half(gl)

        for copy in copies[3:]:
            copy.wait()
        final = f_in[...]
        final_hl = jnp.concatenate(split(final, 2), axis=0)
        gated_hl = jnp.concatenate(split(final * gate, 2), axis=0)
        head_out = dot_t(o_in[...], gated_hl)
        embed_out = dot_t(e_in[...], final_hl)
        head_out = head_out[:, 0:64] + head_out[:, 64:128]
        own = (c == 0).astype(F32)
        embed_out = (embed_out[:, 0:64] + embed_out[:, 64:128]) * own
        for n, value in enumerate(split(head_out, 2)):
            nw[n, 0:384] = left_half(value)
            nw[n, 384:768] = right_half(value)
        for n, value in enumerate(split(embed_out, 2)):
            efw[n * 128:n * 128 + 64] = left_half(value)
            efw[n * 128 + 64:n * 128 + 128] = right_half(value)
        pltpu.make_async_copy(w_ref, w_in, w_sem.at[0]).wait()
        proj[...] = dot(a_hi[...], w_in[...])
        small = proj[0:64] + proj[64:128]
        bias[...] = proj[128:136]
        small_hi, small_lo = split(small, 2)
        none = jnp.zeros((64, COLS), BF16)
        for n, value in enumerate((small_hi, none, small_lo, none)):
            wa[n * 64:(n + 1) * 64] = value
        for n, value in enumerate((none, small_hi, none, small_lo)):
            wb[n * 64:(n + 1) * 64] = value

    @pl.when(early)
    def _():
        fetch()
        values_ref[:, :, HD:] = jnp.ones((HEADS, 2048, HD), BF16)

    noise_copy.wait()
    packed = jnp.concatenate([noise_in[0:16], noise_in[16:32]], axis=1)
    own_noise[...] = packed
    slot = half * 16 + near_z * 4 + y
    xb1[core, slot] = packed.astype(BF16)

    @pl.when(early)
    def _():
        pl.semaphore_wait(barrier, 28)

    @pl.when(jnp.logical_not(early))
    def _():
        pl.semaphore_wait(barrier, 16)


    def a_copy(zz, yy):
        return pltpu.make_async_remote_copy(
            src_ref=xb1.at[core, slot], dst_ref=xb1.at[core, slot], send_sem=a_s.at[0], recv_sem=a_r.at[half],
            device_id=device(c, zz, yy), device_id_type=MESH,
        )

    def blocks(buffer, count, send, recv):
        part = buffer.at[core, pl.ds(0, count)]
        return pltpu.make_async_remote_copy(
            src_ref=part, dst_ref=part, send_sem=send, recv_sem=recv, device_id=sibling, device_id_type=MESH,
        )

    @pl.when(early)
    def _():
        for zz in range(4):
            for yy in range(3):
                @pl.when(jnp.logical_not(jnp.logical_and(z == zz, y == yy)))
                def _():
                    a_copy(zz, yy).start()

    @pl.when(jnp.logical_not(early))
    def _():
        for dz in (4, 3, 5, 2, 6, 1, 7):
            @pl.when((z + dz) % 8 < 4)
            def _():
                for yy in range(3):
                    a_copy(z + dz, yy).start()

    def n_copy(t):
        return pltpu.make_async_remote_copy(
            src_ref=own_noise, dst_ref=red_noise.at[half], send_sem=n_s.at[0], recv_sem=n_r.at[half],
            device_id=device(c, near_z, t), device_id_type=MESH,
        )

    @pl.when(y == c)
    def _():
        @pl.when(jnp.logical_and(early, y > 0))
        def _():
            red_noise[0] = own_noise[...]

        for t in range(1, WINDOW):
            @pl.when(jnp.logical_or(y != t, z >= 4))
            def _():
                n_copy(t).start()

    @pl.when(early)
    def _():
        small_matrices()

    @pl.when(jnp.logical_not(early))
    def _():
        copies[1].start()
        copies[1].wait()

    def sigma(n):
        left = 1.0 - jnp.full((16, 128), ids_ref[n]).astype(F32) / TOTAL
        return 3.0 * left / (1.0 + 2.0 * left)

    for t in range(WINDOW):
        deltas[t] = sigma(t + 1) - sigma(t)

    def doubled(x):
        return jnp.concatenate([x, x], axis=1)

    def inverse_deviation(x, xx):
        term = (dot(xx, g12[...]) + dot(x, g3[...])) * x.astype(F32)
        lane = lax.broadcasted_iota(jnp.int32, term.shape, 1)
        first = jnp.sum(jnp.where(lane < 64, term, 0.0), axis=1, keepdims=True)
        second = jnp.sum(jnp.where(lane < 64, 0.0, term), axis=1, keepdims=True)
        return lax.rsqrt(first + EPS), lax.rsqrt(second + EPS)

    def bias_of(start):
        return bias[0:1, start:start + HD] + bias[1:2, start:start + HD]

    def project(x, begin):
        x = x.reshape(x.shape[0] * 16, 128)
        xx = doubled(x)
        va, vb = inverse_deviation(x, xx)
        rows = slice(begin, begin + 2 * x.shape[0])
        for h in range(HEADS):
            start = h * 3 * HD + HD
            kva = dot(xx, wa[:, start:start + 2 * HD]) * va
            kvb = dot(xx, wb[:, start:start + 2 * HD]) * vb
            kv = jnp.concatenate([kva, kvb], axis=0)
            keys = kv[:, 0:HD] + bias_of(start)
            square = jnp.mean(keys * keys, axis=1, keepdims=True)
            keys_ref[h, rows] = (keys * lax.rsqrt(square + EPS)).astype(BF16)
            values_ref[h, rows, 0:HD] = kv[:, HD:].astype(BF16)

    def half_copy(buffer, which, n, index):
        part = buffer.at[which, pl.ds(n * 16, 16)]
        return pltpu.make_async_remote_copy(
            src_ref=part, dst_ref=part, send_sem=h_s.at[0], recv_sem=h_r.at[index],
            device_id=sibling, device_id_type=MESH,
        )

    def make_queries(blocks_in, begin):
        gains = qg_ref[...] * kg_ref[...] * (HD ** -0.5 * math.log2(math.e))
        xq = jnp.concatenate(blocks_in, axis=0)
        xxq = doubled(xq)
        ra, rb = inverse_deviation(xq, xxq)
        for h in range(HEADS):
            start = h * 3 * HD
            qa = dot(xxq, wa[:, start:start + HD]) * ra
            qb = dot(xxq, wb[:, start:start + HD]) * rb
            q = jnp.concatenate([qa, qb], axis=0) + bias_of(start)
            q = q * lax.rsqrt(jnp.mean(q * q, axis=1, keepdims=True) + EPS) * gains
            queries_ref[h, begin:begin + 128] = q.astype(BF16)
        return xxq

    def weighted(h, rows, keys):
        weights = jnp.exp2(dot_t(queries_ref[h, rows], keys_ref[h, keys])).astype(BF16)
        return dot(weights, values_ref[h, keys])

    def finish(sums, xxq):
        heads = []
        for h, summed in enumerate(sums):
            heads.append((summed[:, 0:HD] / summed[:, HD:] + bias_of((3 * h + 2) * HD)).astype(BF16))
        attention = jnp.concatenate(heads, axis=1)
        pair = jnp.concatenate([attention[0:64], attention[64:128]], axis=1)
        result = dot(pair, nw[0]) + dot(pair, nw[1]) + dot(xxq, efw[...])
        return result.reshape(4, 16, 128).astype(BF16)

    low, high, every = slice(0, 128), slice(128, 256), slice(0, 2048)

    def first_sweep():
        blocks(xb1, 15, a_s.at[0], a_r.at[0]).wait_recv()
        half_copy(xb1, core, 0, 0).start()
        xxq = make_queries([xb1[core, z * 4 + i] for i in range(4)], 0)
        project(xb1[core, 0:16], 0)
        half_copy(xb1, 1 - core, 0, 0).wait_recv()
        project(xb1[1 - core, 0:16], 512)
        for h in range(HEADS):
            early_sum[0, h] = weighted(h, low, slice(0, 1024))
        blocks(xb1, 16, a_s.at[0], a_r.at[1]).wait_recv()
        half_copy(xb1, core, 1, 1).start()
        xxq2 = make_queries([xb1[core, 16 + z * 4 + i] for i in range(4)], 128)
        project(xb1[core, 16:32], 1024)
        for h in range(HEADS):
            early_sum[1, h] = weighted(h, high, slice(0, 1024))
        half_copy(xb1, 1 - core, 1, 1).wait_recv()
        project(xb1[1 - core, 16:32], 1536)
        first = [early_sum[0, h] + weighted(h, low, slice(1024, 2048)) for h in range(HEADS)]
        second = [early_sum[1, h] + weighted(h, high, slice(1024, 2048)) for h in range(HEADS)]
        part1[0] = finish(first, xxq)
        part1[1] = finish(second, xxq2)

    def second_sweep():
        one = z // 2
        two = 1 - one
        blocks(xb2, 14, b_s.at[0], b_r.at[one]).wait_recv()
        half_copy(xb2, core, one, 2).start()
        xxq = make_queries([xb2[core, z * 8 + i * 2] for i in range(4)], 0)
        project(xb2[core, pl.ds(one * 16, 16)], 0)
        blocks(xb2, 16, b_s.at[0], b_r.at[two]).wait_recv()
        half_copy(xb2, core, two, 3).start()
        half_copy(xb2, 1 - core, one, 2).wait_recv()
        project(jnp.concatenate([xb2[1 - core, pl.ds(one * 16, 16)], xb2[core, pl.ds(two * 16, 16)]], axis=0), 512)
        half_copy(xb2, 1 - core, two, 3).wait_recv()
        project(xb2[1 - core, pl.ds(two * 16, 16)], 1536)
        part2[0] = finish([weighted(h, low, every) for h in range(HEADS)], xxq)
        send_out(0)
        xxq2 = make_queries([xb2[core, z * 8 + i * 2 + 1] for i in range(4)], 128)
        part2[1] = finish([weighted(h, high, every) for h in range(HEADS)], xxq2)
        send_out(1)

    def r_copy(t, i):
        return pltpu.make_async_remote_copy(
            src_ref=part1.at[:, i], dst_ref=box.at[y * 4 + c], send_sem=out_s.at[0], recv_sem=r_r.at[y],
            device_id=device(i, z, t), device_id_type=MESH,
        )

    def o_copy(t, h, i):
        return pltpu.make_async_remote_copy(
            src_ref=part2.at[h, i], dst_ref=final_box.at[y * 4 + c], send_sem=out2_s.at[0], recv_sem=o_r.at[y],
            device_id=device(t, partner if h else z, i), device_id_type=MESH,
        )

    def zero_copy(t, h):
        return pltpu.make_async_remote_copy(
            src_ref=zero_sum.at[h], dst_ref=zero_box, send_sem=zero_s.at[0], recv_sem=o_r.at[0],
            device_id=device(t, partner if h else z, c), device_id_type=MESH,
        )

    def boxes(count, recv):
        part = box.at[pl.ds(0, count)]
        return pltpu.make_async_remote_copy(
            src_ref=part, dst_ref=part, send_sem=out_s.at[0], recv_sem=recv, device_id=sibling, device_id_type=MESH,
        )

    def final_boxes(count, recv):
        part = final_box.at[pl.ds(0, count)]
        return pltpu.make_async_remote_copy(
            src_ref=part, dst_ref=part, send_sem=out2_s.at[0], recv_sem=recv, device_id=sibling, device_id_type=MESH,
        )

    def send_out(h):
        for t in (3, 2, 1):
            @pl.when(t >= y)
            def _():
                for i in range(4):
                    if h:
                        o_copy(t, h, i).start()
                        continue
                    mine = jnp.logical_and(t == c, i == y)

                    @pl.when(mine)
                    def _():
                        final_box[y * 4 + c] = part2[0, i]

                    @pl.when(jnp.logical_not(mine))
                    def _():
                        o_copy(t, h, i).start()

    @pl.when(worker)
    def _():
        first_sweep()
        for t in range(1, WINDOW):
            @pl.when(t > y)
            def _():
                for i in range(4):
                    r_copy(t, i).start()

    @pl.when(jnp.logical_and(early, y > 0))
    def _():
        @pl.when(y != c)
        def _():
            n_copy(0).wait_recv()

        late_noise = pltpu.make_async_remote_copy(
            src_ref=own_noise, dst_ref=red_noise.at[1], send_sem=n_s.at[0], recv_sem=n_r.at[1],
            device_id=sibling, device_id_type=MESH,
        )
        late_noise.wait_recv()
        next_inputs[...] = red_noise[...]
        for t in range(3):
            @pl.when(t < y)
            def _():
                boxes(4, r_r.at[t]).wait_recv()
                total = sum(box[t * 4 + cc].astype(F32) for cc in range(4))
                next_inputs[...] += deltas[t][None] * total
                if t == 0:
                    zero_sum[...] = total
        place = near_z * 8 + c * 2
        xb2[core, pl.ds(place, 2)] = next_inputs[...].astype(BF16)
        part = xb2.at[core, pl.ds(place, 2)]
        for dz in (3, -3, 2, -2, 1, -1, 0):
            @pl.when(jnp.logical_and(z + dz >= 0, z + dz < 4))
            def _():
                for dx in (2, 1, 3, 0):
                    if dx or dz:
                        pltpu.make_async_remote_copy(
                            src_ref=part, dst_ref=part, send_sem=b_s.at[0], recv_sem=b_r.at[z // 2],
                            device_id=device(c + dx, z + dz, y), device_id_type=MESH,
                        ).start()

        @pl.when(y == 1)
        def _():
            for t in range(WINDOW):
                for n in range(2):
                    if t == 1 and n == 0:
                        @pl.when(c != 1)
                        def _():
                            zero_copy(t, n).start()

                        @pl.when(c == 1)
                        def _():
                            zero_box[...] = zero_sum[0]
                    else:
                        zero_copy(t, n).start()

    @pl.when(jnp.logical_and(early, y > 0))
    def _():
        second_sweep()

    @pl.when(worker)
    def _():
        blocks(xb1, 11, a_s.at[0], a_r.at[0]).wait_send()
        for t in range(3):
            @pl.when(y == t)
            def _():
                boxes(4 * (3 - t), r_r.at[0]).wait_send()

    @pl.when(jnp.logical_not(worker))
    def _():
        blocks(xb1, 12, a_s.at[0], a_r.at[0]).wait_send()

    def halves(part):
        pltpu.make_async_remote_copy(
            src_ref=part, dst_ref=part, send_sem=h_s.at[0], recv_sem=h_r.at[0],
            device_id=sibling, device_id_type=MESH,
        ).wait_send()

    both_sweeps = jnp.logical_and(y > 0, y < 3)

    @pl.when(jnp.logical_and(early, both_sweeps))
    def _():
        halves(xb1)

    @pl.when(jnp.logical_and(early, jnp.logical_not(both_sweeps)))
    def _():
        halves(xb1.at[0])

    def rows(count, send):
        part = lat_rows.at[pl.ds(0, count)]
        return pltpu.make_async_remote_copy(
            src_ref=part, dst_ref=part, send_sem=send, recv_sem=o_r.at[0],
            device_id=sibling, device_id_type=MESH,
        )

    @pl.when(y == c)
    def _():
        @pl.when(jnp.logical_and(early, y > 0))
        def _():
            rows(2, n_s.at[0]).wait_send()

        @pl.when(jnp.logical_not(jnp.logical_and(early, y > 0)))
        def _():
            rows(3, n_s.at[0]).wait_send()

    @pl.when(jnp.logical_and(early, y > 0))
    def _():
        part = xb2.at[core, pl.ds(0, 30)]
        pltpu.make_async_remote_copy(
            src_ref=part, dst_ref=part, send_sem=b_s.at[0], recv_sem=b_r.at[0],
            device_id=sibling, device_id_type=MESH,
        ).wait_send()
        for t in range(1, WINDOW):
            for kept in range(2):
                @pl.when(jnp.logical_and(y == t, (c >= t) == jnp.bool_(kept)))
                def _():
                    final_boxes(8 * (4 - t) - kept, o_r.at[0]).wait_send()

        @pl.when(jnp.logical_and(y == 1, c == 1))
        def _():
            rows(7, zero_s.at[0]).wait_send()

        @pl.when(jnp.logical_and(y == 1, c != 1))
        def _():
            rows(8, zero_s.at[0]).wait_send()

    lat_acc[...] = own_noise[...]
    for t in range(WINDOW):
        @pl.when(t <= c)
        def _():
            if t == 0:
                @pl.when(jnp.logical_not(jnp.logical_and(early, jnp.logical_and(y == 1, c == 1))))
                def _():
                    pltpu.make_async_remote_copy(
                        src_ref=zero_box, dst_ref=zero_box, send_sem=zero_s.at[0], recv_sem=o_r.at[0],
                        device_id=sibling, device_id_type=MESH,
                    ).wait_recv()

                total = zero_box[...]
            else:
                @pl.when(jnp.logical_and(early, t == y))
                def _():
                    final_boxes(3, o_r.at[t]).wait_recv()

                @pl.when(jnp.logical_not(jnp.logical_and(early, t == y)))
                def _():
                    final_boxes(4, o_r.at[t]).wait_recv()

                first = t * 4
                total = sum(final_box[first + cc].astype(F32) for cc in range(4))
            lat_acc[...] += deltas[t] * total
            dr_acc[...] = total
    out_ref[0:16, 0:C] = lat_acc[:, 0:C]
    out_ref[16:32, 0:C] = lat_acc[:, C:]
    out_ref[0:16, C:] = dr_acc[:, 0:C]
    out_ref[16:32, C:] = dr_acc[:, C:]


def body(
    noise, step_ids, mod_table, embed_weight, qkv_weight, q_gain, k_gain, out_weight, final_weight
):
    hbm = pl.BlockSpec(memory_space=pltpu.HBM)
    vmem = pl.BlockSpec(memory_space=pltpu.VMEM)
    out = pltpu.VMEM((32, 2 * C), F32)
    dma = pltpu.SemaphoreType.DMA
    both = pl.pallas_call(
        kernel,
        out_shape=out,
        in_specs=[hbm] * 9,
        out_specs=vmem,
        scratch_shapes=[
            pltpu.VMEM((32, C), F32),
            pltpu.SMEM((WINDOW + 1,), jnp.int32),
            pltpu.VMEM((3, TOTAL, D), F32),
            pltpu.VMEM((C, D), BF16),
            pltpu.VMEM((D, COLS), BF16),
            pltpu.VMEM((1, HD), F32),
            pltpu.VMEM((1, HD), F32),
            pltpu.VMEM((HEADS * HD, D), BF16),
            pltpu.VMEM((C, D), F32),
            dma((8,)),
            dma((1,)),
            pltpu.VMEM((16, 128), F32),
            pltpu.VMEM((2, 16, 128), F32),
            pltpu.VMEM((2, 32, 16, 128), BF16),
            pltpu.VMEM((2, 32, 16, 128), BF16),
            pltpu.VMEM((HEADS, 2048, HD), BF16),
            pltpu.VMEM((HEADS, 2048, 2 * HD), BF16),
            pltpu.VMEM((HEADS, 256, HD), BF16),
            pltpu.VMEM((2, HEADS, 128, 2 * HD), F32),
            pltpu.VMEM((2, 4, 16, 128), BF16),
            pltpu.VMEM((2, 4, 16, 128), BF16),
            pltpu.VMEM((12, 2, 16, 128), BF16),
            pltpu.VMEM((24, 16, 128), BF16),
            pltpu.VMEM((2, 16, 128), F32),
            pltpu.VMEM((16, 128), F32),
            pltpu.VMEM((8, 16, 128), F32),
            pltpu.VMEM((144, COLS), F32),
            pltpu.VMEM((256, COLS), BF16),
            pltpu.VMEM((256, COLS), BF16),
            pltpu.VMEM((8, COLS), F32),
            pltpu.VMEM((256, 128), BF16),
            pltpu.VMEM((128, 128), BF16),
            pltpu.VMEM((2, 768, 128), BF16),
            pltpu.VMEM((256, 128), BF16),
            pltpu.VMEM((144, D), BF16),
            pltpu.VMEM((16, 128), F32),
            pltpu.VMEM((16, 128), F32),
            pltpu.VMEM((2, 16, 128), F32),
            pltpu.VMEM((WINDOW, 16, 128), F32),
            dma((1,)), dma((2,)), dma((1,)), dma((2,)), dma((1,)), dma((4,)),
            dma((3,)), dma((1,)), dma((2,)), dma((1,)), dma((1,)), dma((1,)), dma((4,)),
        ],
        compiler_params=pltpu.CompilerParams(
            collective_id=0, has_side_effects=True, vmem_limit_bytes=60 * 1024 * 1024
        ),
        cost_estimate=pl.CostEstimate(flops=4_000_000_000, bytes_accessed=14_000_000, transcendentals=1_700_000),
    )(
        noise, step_ids, mod_table.transpose(1, 0, 2), embed_weight, qkv_weight,
        q_gain.reshape(1, HD), k_gain.reshape(1, HD), out_weight, final_weight.T,
    )
    return both[None, :, 0:C], both[None, :, C:]


def solution(mesh):
    in_specs = (P("seq", None), P(), P(), P(), P(None, "tm"), P(), P(), P("tm", None), P())
    out_specs = (P("tm", "seq", None), P("tm", "seq", None))
    return jax.shard_map(body, mesh=mesh, in_specs=in_specs, out_specs=out_specs, check_vma=False)
```

```python
import math

import jax
import jax.numpy as jnp
from jax import lax
from jax.experimental import pallas as pl
from jax.experimental.pallas import tpu as pltpu
from jax.sharding import PartitionSpec as P

MESH = pl.DeviceIdType.MESH
F32 = jnp.float32
BF16 = jnp.bfloat16
C = 64
D = 3072
HD = 128
HEADS = 3
WINDOW = 4
TOTAL = 28
EPS = 1e-6
PARTS = 6
DEPTH = D // PARTS
COLS = 3 * HD * HEADS
FAR_FIRST = sorted(
    [(a, b) for a in range(8) for b in range(4) if a or b],
    key=lambda ab: -(min(ab[0], 8 - ab[0]) + min(ab[1], 4 - ab[1])),
)
CONTRACT_LAST = (((1,), (1,)), ((), ()))


def dot(left, right):
    return jnp.dot(left, right, preferred_element_type=F32)


def dot_t(left, right):
    return lax.dot_general(left, right, CONTRACT_LAST, preferred_element_type=F32)


def split(value, pieces):
    out = []
    for _ in range(pieces):
        piece = value.astype(BF16)
        out.append(piece)
        value = value - piece.astype(F32)
    return out


def left_half(value):
    return jnp.concatenate([value, jnp.zeros_like(value)], axis=1)


def right_half(value):
    return jnp.concatenate([jnp.zeros_like(value), value], axis=1)


def kernel(
    noise_ref, ids_in, mod_ref, e_ref, w_ref, qgain_ref, kgain_ref, o_ref, f_ref,
    out_ref,
    noise_in, ids_ref, mod_in, e_in, w_in, qg_ref, kg_ref, o_in, f_in, local_sem, w_sem,
    own_noise, red_noise, xb1, xb2, keys_ref, values_ref, queries_ref, early_sum, part1, part2, box, final_box, zero_sum, zero_box,
    lat_rows,
    proj, wa, wb, bias, g12, g3, nw, efw, a_hi, lat_acc, dr_acc, next_inputs, deltas,
    a_s, a_r, n_s, n_r, h_s, h_r, r_r, b_s, b_r, out_s, out2_s, zero_s, o_r,
):
    c = lax.axis_index("tm")
    s = lax.axis_index("seq")
    z = s // 8
    y = (s // 2) % 4
    core = s % 2

    def device(cc, zz, yy):
        return (cc % 4, (zz % 8) * 8 + (yy % 4) * 2 + core)

    sibling = (c, z * 8 + y * 2 + 1 - core)

    noise_copy = pltpu.make_async_copy(noise_ref, noise_in, local_sem.at[0])
    noise_copy.start()

    barrier = pltpu.get_barrier_semaphore()
    early = z < 4
    worker = jnp.logical_and(early, y < 3)
    half = z // 4
    near_z = jnp.where(early, z, (z + 2) % 4)
    partner = 4 + (z + 2) % 4

    def greet(target):
        pl.semaphore_signal(barrier, inc=1, device_id=target, device_id_type=MESH)

    @pl.when(early)
    def _():
        for n in (4, 5, 6, 7):
            for dy in (2, 1, 3, 0):
                greet(device(c, n, y + dy))
        for n in range(4):
            for dy in (2, 1, 3, 0):
                if dy:
                    greet(device(c, n, y + dy))
                else:
                    @pl.when(z != n)
                    def _():
                        greet(device(c, n, y))
        for dx in range(1, 4):
            for dy in range(4):
                greet(device(c + dx, z, y + dy))
        greet(sibling)

    copies = [
        pltpu.make_async_copy(e_ref, e_in, local_sem.at[1]),
        pltpu.make_async_copy(ids_in, ids_ref, local_sem.at[2]),
        pltpu.make_async_copy(mod_ref, mod_in, local_sem.at[3]),
        pltpu.make_async_copy(f_ref, f_in, local_sem.at[4]),
        pltpu.make_async_copy(o_ref, o_in, local_sem.at[5]),
        pltpu.make_async_copy(qgain_ref, qg_ref, local_sem.at[6]),
        pltpu.make_async_copy(kgain_ref, kg_ref, local_sem.at[7]),
    ]
    w_copies = [
        pltpu.make_async_copy(
            w_ref.at[pl.ds(n * DEPTH, DEPTH)], w_in.at[pl.ds(n * DEPTH, DEPTH)], w_sem.at[0]
        )
        for n in range(PARTS)
    ]

    def fetch():
        for copy in copies + w_copies:
            copy.start()

    def small_matrices():
        for copy in copies[:3]:
            copy.wait()
        embed = e_in[...].astype(F32)
        centred = embed - jnp.mean(embed, axis=1, keepdims=True)
        here = pl.ds(ids_ref[y], 1)
        shift = mod_in[0, here]
        scale = mod_in[1, here]
        gate = mod_in[2, here]
        scaled = split(centred * (1.0 + scale), 2)
        a_hi[0:64] = scaled[0]
        a_hi[64:128] = scaled[1]
        shifts = split(shift, 2)
        row = lax.broadcasted_iota(jnp.int32, (16, D), 0)
        a_hi[128:144] = jnp.where(
            row == 0, jnp.broadcast_to(shift, (16, D)),
            jnp.where(row == 1, jnp.broadcast_to(shift - shifts[0].astype(F32), (16, D)), 0.0),
        ).astype(BF16)

        pieces = split(centred, 3)
        stacked = jnp.concatenate(pieces, axis=0)
        gram = dot_t(stacked, stacked)
        gram = gram[0:64] + gram[64:128] + gram[128:192]
        gram = (gram[:, 0:64] + gram[:, 64:128] + gram[:, 128:192]) * (1.0 / D)
        g1, g2, gl = split(gram, 3)
        g12[0:64] = left_half(g1)
        g12[64:128] = right_half(g1)
        g12[128:192] = left_half(g2)
        g12[192:256] = right_half(g2)
        g3[0:64] = left_half(gl)
        g3[64:128] = right_half(gl)

        for copy in copies[3:]:
            copy.wait()
        final = f_in[...]
        final_hl = jnp.concatenate(split(final, 2), axis=0)
        gated_hl = jnp.concatenate(split(final * gate, 2), axis=0)
        head_out = dot_t(o_in[...], gated_hl)
        embed_out = dot_t(e_in[...], final_hl)
        head_out = head_out[:, 0:64] + head_out[:, 64:128]
        own = (c == 0).astype(F32)
        embed_out = (embed_out[:, 0:64] + embed_out[:, 64:128]) * own
        for n, value in enumerate(split(head_out, 2)):
            nw[n, 0:384] = left_half(value)
            nw[n, 384:768] = right_half(value)
        for n, value in enumerate(split(embed_out, 2)):
            efw[n * 128:n * 128 + 64] = left_half(value)
            efw[n * 128 + 64:n * 128 + 128] = right_half(value)
        pltpu.make_async_copy(w_ref, w_in, w_sem.at[0]).wait()
        proj[...] = dot(a_hi[...], w_in[...])
        small = proj[0:64] + proj[64:128]
        bias[...] = proj[128:136]
        small_hi, small_lo = split(small, 2)
        none = jnp.zeros((64, COLS), BF16)
        for n, value in enumerate((small_hi, none, small_lo, none)):
            wa[n * 64:(n + 1) * 64] = value
        for n, value in enumerate((none, small_hi, none, small_lo)):
            wb[n * 64:(n + 1) * 64] = value

    @pl.when(early)
    def _():
        fetch()
        values_ref[:, :, HD:] = jnp.ones((HEADS, 2048, HD), BF16)

    noise_copy.wait()
    packed = jnp.concatenate([noise_in[0:16], noise_in[16:32]], axis=1)
    own_noise[...] = packed
    slot = half * 16 + near_z * 4 + y
    xb1[core, slot] = packed.astype(BF16)

    @pl.when(early)
    def _():
        pl.semaphore_wait(barrier, 28)

    @pl.when(jnp.logical_not(early))
    def _():
        pl.semaphore_wait(barrier, 16)

    def a_copy(zz, yy):
        return pltpu.make_async_remote_copy(
            src_ref=xb1.at[core, slot], dst_ref=xb1.at[core, slot], send_sem=a_s.at[0], recv_sem=a_r.at[half],
            device_id=device(c, zz, yy), device_id_type=MESH,
        )

    def blocks(buffer, count, send, recv):
        part = buffer.at[core, pl.ds(0, count)]
        return pltpu.make_async_remote_copy(
            src_ref=part, dst_ref=part, send_sem=send, recv_sem=recv, device_id=sibling, device_id_type=MESH,
        )

    @pl.when(early)
    def _():
        for zz in range(4):
            for yy in range(3):
                @pl.when(jnp.logical_not(jnp.logical_and(z == zz, y == yy)))
                def _():
                    a_copy(zz, yy).start()

    @pl.when(jnp.logical_not(early))
    def _():
        for dz in (4, 3, 5, 2, 6, 1, 7):
            @pl.when((z + dz) % 8 < 4)
            def _():
                for yy in range(3):
                    a_copy(z + dz, yy).start()

    def n_copy(t):
        return pltpu.make_async_remote_copy(
            src_ref=own_noise, dst_ref=red_noise.at[half], send_sem=n_s.at[0], recv_sem=n_r.at[half],
            device_id=device(c, near_z, t), device_id_type=MESH,
        )

    @pl.when(y == c)
    def _():
        @pl.when(jnp.logical_and(early, y > 0))
        def _():
            red_noise[0] = own_noise[...]

        for t in range(1, WINDOW):
            @pl.when(jnp.logical_or(y != t, z >= 4))
            def _():
                n_copy(t).start()

    @pl.when(early)
    def _():
        small_matrices()

    @pl.when(jnp.logical_not(early))
    def _():
        copies[1].start()
        copies[1].wait()

    def sigma(n):
        left = 1.0 - jnp.full((16, 128), ids_ref[n]).astype(F32) / TOTAL
        return 3.0 * left / (1.0 + 2.0 * left)

    for t in range(WINDOW):
        deltas[t] = sigma(t + 1) - sigma(t)

    def doubled(x):
        return jnp.concatenate([x, x], axis=1)

    def inverse_deviation(x, xx):
        term = (dot(xx, g12[...]) + dot(x, g3[...])) * x.astype(F32)
        lane = lax.broadcasted_iota(jnp.int32, term.shape, 1)
        first = jnp.sum(jnp.where(lane < 64, term, 0.0), axis=1, keepdims=True)
        second = jnp.sum(jnp.where(lane < 64, 0.0, term), axis=1, keepdims=True)
        return lax.rsqrt(jnp.maximum(first, 0.0) + EPS), lax.rsqrt(jnp.maximum(second, 0.0) + EPS)

    def bias_of(start):
        return bias[0:1, start:start + HD] + bias[1:2, start:start + HD]

    def project(x, begin):
        x = x.reshape(x.shape[0] * 16, 128)
        xx = doubled(x)
        va, vb = inverse_deviation(x, xx)
        rows = slice(begin, begin + 2 * x.shape[0])
        for h in range(HEADS):
            start = h * 3 * HD + HD
            kva = dot(xx, wa[:, start:start + 2 * HD]) * va
            kvb = dot(xx, wb[:, start:start + 2 * HD]) * vb
            kv = jnp.concatenate([kva, kvb], axis=0)
            keys = kv[:, 0:HD] + bias_of(start)
            square = jnp.mean(keys * keys, axis=1, keepdims=True)
            keys_ref[h, rows] = (keys * lax.rsqrt(square + EPS)).astype(BF16)
            values_ref[h, rows, 0:HD] = kv[:, HD:].astype(BF16)

    def half_copy(buffer, which, n, index):
        part = buffer.at[which, pl.ds(n * 16, 16)]
        return pltpu.make_async_remote_copy(
            src_ref=part, dst_ref=part, send_sem=h_s.at[0], recv_sem=h_r.at[index],
            device_id=sibling, device_id_type=MESH,
        )

    def make_queries(blocks_in, begin):
        gains = qg_ref[...] * kg_ref[...] * (HD ** -0.5 * math.log2(math.e))
        xq = jnp.concatenate(blocks_in, axis=0)
        xxq = doubled(xq)
        ra, rb = inverse_deviation(xq, xxq)
        for h in range(HEADS):
            start = h * 3 * HD
            qa = dot(xxq, wa[:, start:start + HD]) * ra
            qb = dot(xxq, wb[:, start:start + HD]) * rb
            q = jnp.concatenate([qa, qb], axis=0) + bias_of(start)
            q = q * lax.rsqrt(jnp.mean(q * q, axis=1, keepdims=True) + EPS) * gains
            queries_ref[h, begin:begin + 128] = q.astype(BF16)
        return xxq

    def weighted(h, rows, keys):
        weights = jnp.exp2(dot_t(queries_ref[h, rows], keys_ref[h, keys])).astype(BF16)
        return dot(weights, values_ref[h, keys])

    def finish(sums, xxq):
        heads = []
        for h, summed in enumerate(sums):
            heads.append((summed[:, 0:HD] / summed[:, HD:] + bias_of((3 * h + 2) * HD)).astype(BF16))
        attention = jnp.concatenate(heads, axis=1)
        pair = jnp.concatenate([attention[0:64], attention[64:128]], axis=1)
        result = dot(pair, nw[0]) + dot(pair, nw[1]) + dot(xxq, efw[...])
        return result.reshape(4, 16, 128).astype(BF16)

    low, high, every = slice(0, 128), slice(128, 256), slice(0, 2048)

    def first_sweep():
        blocks(xb1, 15, a_s.at[0], a_r.at[0]).wait_recv()
        half_copy(xb1, core, 0, 0).start()
        xxq = make_queries([xb1[core, z * 4 + i] for i in range(4)], 0)
        project(xb1[core, 0:16], 0)
        half_copy(xb1, 1 - core, 0, 0).wait_recv()
        project(xb1[1 - core, 0:16], 512)
        for h in range(HEADS):
            early_sum[0, h] = weighted(h, low, slice(0, 1024))
        blocks(xb1, 16, a_s.at[0], a_r.at[1]).wait_recv()
        half_copy(xb1, core, 1, 1).start()
        xxq2 = make_queries([xb1[core, 16 + z * 4 + i] for i in range(4)], 128)
        project(xb1[core, 16:32], 1024)
        for h in range(HEADS):
            early_sum[1, h] = weighted(h, high, slice(0, 1024))
        half_copy(xb1, 1 - core, 1, 1).wait_recv()
        project(xb1[1 - core, 16:32], 1536)
        first = [early_sum[0, h] + weighted(h, low, slice(1024, 2048)) for h in range(HEADS)]
        second = [early_sum[1, h] + weighted(h, high, slice(1024, 2048)) for h in range(HEADS)]
        part1[0] = finish(first, xxq)
        part1[1] = finish(second, xxq2)

    def second_sweep():
        one = z // 2
        two = 1 - one
        blocks(xb2, 14, b_s.at[0], b_r.at[one]).wait_recv()
        half_copy(xb2, core, one, 2).start()
        xxq = make_queries([xb2[core, z * 8 + i * 2] for i in range(4)], 0)
        project(xb2[core, pl.ds(one * 16, 16)], 0)
        blocks(xb2, 16, b_s.at[0], b_r.at[two]).wait_recv()
        half_copy(xb2, core, two, 3).start()
        half_copy(xb2, 1 - core, one, 2).wait_recv()
        project(jnp.concatenate([xb2[1 - core, pl.ds(one * 16, 16)], xb2[core, pl.ds(two * 16, 16)]], axis=0), 512)
        half_copy(xb2, 1 - core, two, 3).wait_recv()
        project(xb2[1 - core, pl.ds(two * 16, 16)], 1536)
        part2[0] = finish([weighted(h, low, every) for h in range(HEADS)], xxq)
        send_out(0)
        xxq2 = make_queries([xb2[core, z * 8 + i * 2 + 1] for i in range(4)], 128)
        part2[1] = finish([weighted(h, high, every) for h in range(HEADS)], xxq2)
        send_out(1)

    def r_copy(t, i):
        return pltpu.make_async_remote_copy(
            src_ref=part1.at[:, i], dst_ref=box.at[y * 4 + c], send_sem=out_s.at[0], recv_sem=r_r.at[y],
            device_id=device(i, z, t), device_id_type=MESH,
        )

    def o_copy(t, h, i):
        return pltpu.make_async_remote_copy(
            src_ref=part2.at[h, i], dst_ref=final_box.at[y * 4 + c], send_sem=out2_s.at[0], recv_sem=o_r.at[y],
            device_id=device(t, partner if h else z, i), device_id_type=MESH,
        )

    def zero_copy(t, h):
        return pltpu.make_async_remote_copy(
            src_ref=zero_sum.at[h], dst_ref=zero_box, send_sem=zero_s.at[0], recv_sem=o_r.at[0],
            device_id=device(t, partner if h else z, c), device_id_type=MESH,
        )

    def boxes(count, recv):
        part = box.at[pl.ds(0, count)]
        return pltpu.make_async_remote_copy(
            src_ref=part, dst_ref=part, send_sem=out_s.at[0], recv_sem=recv, device_id=sibling, device_id_type=MESH,
        )

    def final_boxes(count, recv):
        part = final_box.at[pl.ds(0, count)]
        return pltpu.make_async_remote_copy(
            src_ref=part, dst_ref=part, send_sem=out2_s.at[0], recv_sem=recv, device_id=sibling, device_id_type=MESH,
        )

    def send_out(h):
        for t in (3, 2, 1):
            @pl.when(t >= y)
            def _():
                for i in range(4):
                    if h:
                        o_copy(t, h, i).start()
                        continue
                    mine = jnp.logical_and(t == c, i == y)

                    @pl.when(mine)
                    def _():
                        final_box[y * 4 + c] = part2[0, i]

                    @pl.when(jnp.logical_not(mine))
                    def _():
                        o_copy(t, h, i).start()

    @pl.when(worker)
    def _():
        first_sweep()
        for t in range(1, WINDOW):
            @pl.when(t > y)
            def _():
                for i in range(4):
                    r_copy(t, i).start()

    @pl.when(jnp.logical_and(early, y > 0))
    def _():
        @pl.when(y != c)
        def _():
            n_copy(0).wait_recv()

        late_noise = pltpu.make_async_remote_copy(
            src_ref=own_noise, dst_ref=red_noise.at[1], send_sem=n_s.at[0], recv_sem=n_r.at[1],
            device_id=sibling, device_id_type=MESH,
        )
        late_noise.wait_recv()
        next_inputs[...] = red_noise[...]
        for t in range(3):
            @pl.when(t < y)
            def _():
                boxes(4, r_r.at[t]).wait_recv()
                total = sum(box[t * 4 + cc].astype(F32) for cc in range(4))
                next_inputs[...] += deltas[t][None] * total
                if t == 0:
                    zero_sum[...] = total
        place = near_z * 8 + c * 2
        xb2[core, pl.ds(place, 2)] = next_inputs[...].astype(BF16)
        part = xb2.at[core, pl.ds(place, 2)]
        for dz in (3, -3, 2, -2, 1, -1, 0):
            @pl.when(jnp.logical_and(z + dz >= 0, z + dz < 4))
            def _():
                for dx in (2, 1, 3, 0):
                    if dx or dz:
                        pltpu.make_async_remote_copy(
                            src_ref=part, dst_ref=part, send_sem=b_s.at[0], recv_sem=b_r.at[z // 2],
                            device_id=device(c + dx, z + dz, y), device_id_type=MESH,
                        ).start()

        @pl.when(y == 1)
        def _():
            for t in range(WINDOW):
                for n in range(2):
                    if t == 1 and n == 0:
                        @pl.when(c != 1)
                        def _():
                            zero_copy(t, n).start()

                        @pl.when(c == 1)
                        def _():
                            zero_box[...] = zero_sum[0]
                    else:
                        zero_copy(t, n).start()

    @pl.when(jnp.logical_and(early, y > 0))
    def _():
        second_sweep()

    @pl.when(worker)
    def _():
        blocks(xb1, 11, a_s.at[0], a_r.at[0]).wait_send()
        for t in range(3):
            @pl.when(y == t)
            def _():
                boxes(4 * (3 - t), r_r.at[0]).wait_send()

    @pl.when(jnp.logical_not(worker))
    def _():
        blocks(xb1, 12, a_s.at[0], a_r.at[0]).wait_send()

    def halves(part):
        pltpu.make_async_remote_copy(
            src_ref=part, dst_ref=part, send_sem=h_s.at[0], recv_sem=h_r.at[0],
            device_id=sibling, device_id_type=MESH,
        ).wait_send()

    both_sweeps = jnp.logical_and(y > 0, y < 3)

    @pl.when(jnp.logical_and(early, both_sweeps))
    def _():
        halves(xb1)

    @pl.when(jnp.logical_and(early, jnp.logical_not(both_sweeps)))
    def _():
        halves(xb1.at[0])

    def rows(count, send):
        part = lat_rows.at[pl.ds(0, count)]
        return pltpu.make_async_remote_copy(
            src_ref=part, dst_ref=part, send_sem=send, recv_sem=o_r.at[0],
            device_id=sibling, device_id_type=MESH,
        )

    @pl.when(y == c)
    def _():
        @pl.when(jnp.logical_and(early, y > 0))
        def _():
            rows(2, n_s.at[0]).wait_send()

        @pl.when(jnp.logical_not(jnp.logical_and(early, y > 0)))
        def _():
            rows(3, n_s.at[0]).wait_send()

    @pl.when(jnp.logical_and(early, y > 0))
    def _():
        part = xb2.at[core, pl.ds(0, 30)]
        pltpu.make_async_remote_copy(
            src_ref=part, dst_ref=part, send_sem=b_s.at[0], recv_sem=b_r.at[0],
            device_id=sibling, device_id_type=MESH,
        ).wait_send()
        for t in range(1, WINDOW):
            for kept in range(2):
                @pl.when(jnp.logical_and(y == t, (c >= t) == jnp.bool_(kept)))
                def _():
                    final_boxes(8 * (4 - t) - kept, o_r.at[0]).wait_send()

        @pl.when(jnp.logical_and(y == 1, c == 1))
        def _():
            rows(7, zero_s.at[0]).wait_send()

        @pl.when(jnp.logical_and(y == 1, c != 1))
        def _():
            rows(8, zero_s.at[0]).wait_send()

    lat_acc[...] = own_noise[...]
    for t in range(WINDOW):
        @pl.when(t <= c)
        def _():
            if t == 0:
                @pl.when(jnp.logical_not(jnp.logical_and(early, jnp.logical_and(y == 1, c == 1))))
                def _():
                    pltpu.make_async_remote_copy(
                        src_ref=zero_box, dst_ref=zero_box, send_sem=zero_s.at[0], recv_sem=o_r.at[0],
                        device_id=sibling, device_id_type=MESH,
                    ).wait_recv()

                total = zero_box[...]
            else:
                @pl.when(jnp.logical_and(early, t == y))
                def _():
                    final_boxes(3, o_r.at[t]).wait_recv()

                @pl.when(jnp.logical_not(jnp.logical_and(early, t == y)))
                def _():
                    final_boxes(4, o_r.at[t]).wait_recv()

                first = t * 4
                total = sum(final_box[first + cc].astype(F32) for cc in range(4))
            lat_acc[...] += deltas[t] * total
            dr_acc[...] = total
    out_ref[0:16, 0:C] = lat_acc[:, 0:C]
    out_ref[16:32, 0:C] = lat_acc[:, C:]
    out_ref[0:16, C:] = dr_acc[:, 0:C]
    out_ref[16:32, C:] = dr_acc[:, C:]


def body(
    noise, step_ids, mod_table, embed_weight, qkv_weight, q_gain, k_gain, out_weight, final_weight
):
    hbm = pl.BlockSpec(memory_space=pltpu.HBM)
    vmem = pl.BlockSpec(memory_space=pltpu.VMEM)
    out = pltpu.VMEM((32, 2 * C), F32)
    dma = pltpu.SemaphoreType.DMA
    both = pl.pallas_call(
        kernel,
        out_shape=out,
        in_specs=[hbm] * 9,
        out_specs=vmem,
        scratch_shapes=[
            pltpu.VMEM((32, C), F32),
            pltpu.SMEM((WINDOW + 1,), jnp.int32),
            pltpu.VMEM((3, TOTAL, D), F32),
            pltpu.VMEM((C, D), BF16),
            pltpu.VMEM((D, COLS), BF16),
            pltpu.VMEM((1, HD), F32),
            pltpu.VMEM((1, HD), F32),
            pltpu.VMEM((HEADS * HD, D), BF16),
            pltpu.VMEM((C, D), F32),
            dma((8,)),
            dma((1,)),
            pltpu.VMEM((16, 128), F32),
            pltpu.VMEM((2, 16, 128), F32),
            pltpu.VMEM((2, 32, 16, 128), BF16),
            pltpu.VMEM((2, 32, 16, 128), BF16),
            pltpu.VMEM((HEADS, 2048, HD), BF16),
            pltpu.VMEM((HEADS, 2048, 2 * HD), BF16),
            pltpu.VMEM((HEADS, 256, HD), BF16),
            pltpu.VMEM((2, HEADS, 128, 2 * HD), F32),
            pltpu.VMEM((2, 4, 16, 128), BF16),
            pltpu.VMEM((2, 4, 16, 128), BF16),
            pltpu.VMEM((12, 2, 16, 128), BF16),
            pltpu.VMEM((24, 16, 128), BF16),
            pltpu.VMEM((2, 16, 128), F32),
            pltpu.VMEM((16, 128), F32),
            pltpu.VMEM((8, 16, 128), F32),
            pltpu.VMEM((144, COLS), F32),
            pltpu.VMEM((256, COLS), BF16),
            pltpu.VMEM((256, COLS), BF16),
            pltpu.VMEM((8, COLS), F32),
            pltpu.VMEM((256, 128), BF16),
            pltpu.VMEM((128, 128), BF16),
            pltpu.VMEM((2, 768, 128), BF16),
            pltpu.VMEM((256, 128), BF16),
            pltpu.VMEM((144, D), BF16),
            pltpu.VMEM((16, 128), F32),
            pltpu.VMEM((16, 128), F32),
            pltpu.VMEM((2, 16, 128), F32),
            pltpu.VMEM((WINDOW, 16, 128), F32),
            dma((1,)), dma((2,)), dma((1,)), dma((2,)), dma((1,)), dma((4,)),
            dma((3,)), dma((1,)), dma((2,)), dma((1,)), dma((1,)), dma((1,)), dma((4,)),
        ],
        compiler_params=pltpu.CompilerParams(
            collective_id=0, has_side_effects=True, vmem_limit_bytes=60 * 1024 * 1024
        ),
        cost_estimate=pl.CostEstimate(flops=4_000_000_000, bytes_accessed=14_000_000, transcendentals=1_700_000),
    )(
        noise, step_ids, mod_table.transpose(1, 0, 2), embed_weight, qkv_weight,
        q_gain.reshape(1, HD), k_gain.reshape(1, HD), out_weight, final_weight.T,
    )
    return both[None, :, 0:C], both[None, :, C:]


def solution(mesh):
    in_specs = (P("seq", None), P(), P(), P(), P(None, "tm"), P(), P(), P("tm", None), P())
    out_specs = (P("tm", "seq", None), P("tm", "seq", None))
    return jax.shard_map(body, mesh=mesh, in_specs=in_specs, out_specs=out_specs, check_vma=False)
```

```python
import math

import jax
import jax.numpy as jnp
from jax import lax
from jax.experimental import pallas as pl
from jax.experimental.pallas import tpu as pltpu
from jax.sharding import PartitionSpec as P

MESH = pl.DeviceIdType.MESH
F32 = jnp.float32
BF16 = jnp.bfloat16
C = 64
D = 3072
HD = 128
HEADS = 3
WINDOW = 4
TOTAL = 28
EPS = 1e-6
PARTS = 6
DEPTH = D // PARTS
COLS = 3 * HD * HEADS
FAR_FIRST = sorted(
    [(a, b) for a in range(8) for b in range(4) if a or b],
    key=lambda ab: -(min(ab[0], 8 - ab[0]) + min(ab[1], 4 - ab[1])),
)
CONTRACT_LAST = (((1,), (1,)), ((), ()))


def dot(left, right):
    return jnp.dot(left, right, preferred_element_type=F32)


def dot_t(left, right):
    return lax.dot_general(left, right, CONTRACT_LAST, preferred_element_type=F32)


def split(value, pieces):
    out = []
    for _ in range(pieces):
        piece = value.astype(BF16)
        out.append(piece)
        value = value - piece.astype(F32)
    return out


def left_half(value):
    return jnp.concatenate([value, jnp.zeros_like(value)], axis=1)


def right_half(value):
    return jnp.concatenate([jnp.zeros_like(value), value], axis=1)


def kernel(
    noise_ref, ids_in, mod_ref, e_ref, w_ref, qgain_ref, kgain_ref, o_ref, f_ref,
    out_ref,
    noise_in, ids_ref, mod_in, e_in, w_in, qg_ref, kg_ref, o_in, f_in, local_sem, w_sem,
    own_noise, red_noise, xb1, xb2, keys_ref, values_ref, queries_ref, early_sum, part1, part2, box, final_box, zero_sum, zero_box,
    lat_rows,
    proj, wa, wb, bias, g12, g3, nw, efw, a_hi, lat_acc, dr_acc, next_inputs, deltas,
    a_s, a_r, n_s, n_r, h_s, h_r, r_r, b_s, b_r, out_s, out2_s, zero_s, o_r,
):
    c = lax.axis_index("tm")
    s = lax.axis_index("seq")
    z = s // 8
    y = (s // 2) % 4
    core = s % 2

    def device(cc, zz, yy):
        return (cc % 4, (zz % 8) * 8 + (yy % 4) * 2 + core)

    sibling = (c, z * 8 + y * 2 + 1 - core)

    noise_copy = pltpu.make_async_copy(noise_ref, noise_in, local_sem.at[0])
    noise_copy.start()

    barrier = pltpu.get_barrier_semaphore()
    early = z < 4
    worker = jnp.logical_and(early, y < 3)
    half = z // 4
    near_z = jnp.where(early, z, (z + 2) % 4)
    partner = 4 + (z + 2) % 4

    def greet(target):
        pl.semaphore_signal(barrier, inc=1, device_id=target, device_id_type=MESH)

    @pl.when(early)
    def _():
        for n in (4, 5, 6, 7):
            for dy in (2, 1, 3, 0):
                greet(device(c, n, y + dy))
        for n in range(4):
            for dy in (2, 1, 3, 0):
                if dy:
                    greet(device(c, n, y + dy))
                else:
                    @pl.when(z != n)
                    def _():
                        greet(device(c, n, y))
        for dx in range(1, 4):
            for dy in range(4):
                greet(device(c + dx, z, y + dy))
        greet(sibling)

    copies = [
        pltpu.make_async_copy(e_ref, e_in, local_sem.at[1]),
        pltpu.make_async_copy(ids_in, ids_ref, local_sem.at[2]),
        pltpu.make_async_copy(mod_ref, mod_in, local_sem.at[3]),
        pltpu.make_async_copy(f_ref, f_in, local_sem.at[4]),
        pltpu.make_async_copy(o_ref, o_in, local_sem.at[5]),
        pltpu.make_async_copy(qgain_ref, qg_ref, local_sem.at[6]),
        pltpu.make_async_copy(kgain_ref, kg_ref, local_sem.at[7]),
    ]
    w_copies = [
        pltpu.make_async_copy(
            w_ref.at[pl.ds(n * DEPTH, DEPTH)], w_in.at[pl.ds(n * DEPTH, DEPTH)], w_sem.at[0]
        )
        for n in range(PARTS)
    ]

    def fetch():
        for copy in copies + w_copies:
            copy.start()

    def small_matrices():
        for copy in copies[:3]:
            copy.wait()
        embed = e_in[...].astype(F32)
        centred = embed - jnp.mean(embed, axis=1, keepdims=True)
        here = pl.ds(ids_ref[y], 1)
        shift = mod_in[0, here]
        scale = mod_in[1, here]
        gate = mod_in[2, here]
        scaled = split(centred * (1.0 + scale), 2)
        a_hi[0:64] = scaled[0]
        a_hi[64:128] = scaled[1]
        shifts = split(shift, 2)
        row = lax.broadcasted_iota(jnp.int32, (16, D), 0)
        a_hi[128:144] = jnp.where(
            row == 0, jnp.broadcast_to(shift, (16, D)),
            jnp.where(row == 1, jnp.broadcast_to(shift - shifts[0].astype(F32), (16, D)), 0.0),
        ).astype(BF16)

        pieces = split(centred, 3)
        stacked = jnp.concatenate(pieces, axis=0)
        gram = dot_t(stacked, stacked)
        gram = gram[0:64] + gram[64:128] + gram[128:192]
        gram = (gram[:, 0:64] + gram[:, 64:128] + gram[:, 128:192]) * (1.0 / D)
        g1, g2, gl = split(gram, 3)
        g12[0:64] = left_half(g1)
        g12[64:128] = right_half(g1)
        g12[128:192] = left_half(g2)
        g12[192:256] = right_half(g2)
        g3[0:64] = left_half(gl)
        g3[64:128] = right_half(gl)

        for copy in copies[3:]:
            copy.wait()
        final = f_in[...]
        final_hl = jnp.concatenate(split(final, 2), axis=0)
        gated_hl = jnp.concatenate(split(final * gate, 2), axis=0)
        head_out = dot_t(o_in[...], gated_hl)
        embed_out = dot_t(e_in[...], final_hl)
        head_out = head_out[:, 0:64] + head_out[:, 64:128]
        own = (c == 0).astype(F32)
        embed_out = (embed_out[:, 0:64] + embed_out[:, 64:128]) * own
        for n, value in enumerate(split(head_out, 2)):
            nw[n, 0:384] = left_half(value)
            nw[n, 384:768] = right_half(value)
        for n, value in enumerate(split(embed_out, 2)):
            efw[n * 128:n * 128 + 64] = left_half(value)
            efw[n * 128 + 64:n * 128 + 128] = right_half(value)
        pltpu.make_async_copy(w_ref, w_in, w_sem.at[0]).wait()
        proj[...] = dot(a_hi[...], w_in[...])
        small = proj[0:64] + proj[64:128]
        bias[...] = proj[128:136]
        small_hi, small_lo = split(small, 2)
        none = jnp.zeros((64, COLS), BF16)
        for n, value in enumerate((small_hi, none, small_lo, none)):
            wa[n * 64:(n + 1) * 64] = value
        for n, value in enumerate((none, small_hi, none, small_lo)):
            wb[n * 64:(n + 1) * 64] = value

    @pl.when(early)
    def _():
        fetch()
        values_ref[:, :, HD:] = jnp.ones((HEADS, 2048, HD), BF16)

    noise_copy.wait()
    packed = jnp.concatenate([noise_in[0:16], noise_in[16:32]], axis=1)
    own_noise[...] = packed
    slot = half * 16 + near_z * 4 + y
    xb1[core, slot] = packed.astype(BF16)

    @pl.when(early)
    def _():
        pl.semaphore_wait(barrier, 28)

    @pl.when(jnp.logical_not(early))
    def _():
        pl.semaphore_wait(barrier, 16)

    def a_copy(zz, yy):
        return pltpu.make_async_remote_copy(
            src_ref=xb1.at[core, slot], dst_ref=xb1.at[core, slot], send_sem=a_s.at[0], recv_sem=a_r.at[half],
            device_id=device(c, zz, yy), device_id_type=MESH,
        )

    def blocks(buffer, count, send, recv):
        part = buffer.at[core, pl.ds(0, count)]
        return pltpu.make_async_remote_copy(
            src_ref=part, dst_ref=part, send_sem=send, recv_sem=recv, device_id=sibling, device_id_type=MESH,
        )

    @pl.when(early)
    def _():
        for zz in range(4):
            for yy in range(3):
                @pl.when(jnp.logical_not(jnp.logical_and(z == zz, y == yy)))
                def _():
                    a_copy(zz, yy).start()

    @pl.when(jnp.logical_not(early))
    def _():
        for dz in (4, 3, 5, 2, 6, 1, 7):
            @pl.when((z + dz) % 8 < 4)
            def _():
                for yy in range(3):
                    a_copy(z + dz, yy).start()

    def n_copy(t):
        return pltpu.make_async_remote_copy(
            src_ref=own_noise, dst_ref=red_noise.at[half], send_sem=n_s.at[0], recv_sem=n_r.at[half],
            device_id=device(c, near_z, t), device_id_type=MESH,
        )

    @pl.when(y == c)
    def _():
        @pl.when(jnp.logical_and(early, y > 0))
        def _():
            red_noise[0] = own_noise[...]

        for t in range(1, WINDOW):
            @pl.when(jnp.logical_or(y != t, z >= 4))
            def _():
                n_copy(t).start()

    @pl.when(early)
    def _():
        small_matrices()

    @pl.when(jnp.logical_not(early))
    def _():
        copies[1].start()
        copies[1].wait()

    def sigma(n):
        left = 1.0 - jnp.full((16, 128), ids_ref[n]).astype(F32) / TOTAL
        return 3.0 * left / (1.0 + 2.0 * left)

    for t in range(WINDOW):
        deltas[t] = sigma(t + 1) - sigma(t)

    def doubled(x):
        return jnp.concatenate([x, x], axis=1)

    def inverse_deviation(x, xx):
        term = (dot(xx, g12[...]) + dot(x, g3[...])) * x.astype(F32)
        lane = lax.broadcasted_iota(jnp.int32, term.shape, 1)
        first = jnp.sum(jnp.where(lane < 64, term, 0.0), axis=1, keepdims=True)
        second = jnp.sum(jnp.where(lane < 64, 0.0, term), axis=1, keepdims=True)
        return lax.rsqrt(jnp.maximum(first, 0.0) + EPS), lax.rsqrt(jnp.maximum(second, 0.0) + EPS)

    def bias_of(start):
        return bias[0:1, start:start + HD] + bias[1:2, start:start + HD]

    def project(x, begin):
        x = x.reshape(x.shape[0] * 16, 128)
        xx = doubled(x)
        va, vb = inverse_deviation(x, xx)
        rows = slice(begin, begin + 2 * x.shape[0])
        for h in range(HEADS):
            start = h * 3 * HD + HD
            kva = dot(xx, wa[:, start:start + 2 * HD]) * va
            kvb = dot(xx, wb[:, start:start + 2 * HD]) * vb
            kv = jnp.concatenate([kva, kvb], axis=0)
            keys = kv[:, 0:HD] + bias_of(start)
            square = jnp.mean(keys * keys, axis=1, keepdims=True)
            keys_ref[h, rows] = (keys * lax.rsqrt(square + EPS)).astype(BF16)
            values_ref[h, rows, 0:HD] = kv[:, HD:].astype(BF16)

    def half_copy(buffer, which, n, index):
        part = buffer.at[which, pl.ds(n * 16, 16)]
        return pltpu.make_async_remote_copy(
            src_ref=part, dst_ref=part, send_sem=h_s.at[0], recv_sem=h_r.at[index],
            device_id=sibling, device_id_type=MESH,
        )

    def make_queries(blocks_in, begin):
        gains = qg_ref[...] * kg_ref[...] * (HD ** -0.5 * math.log2(math.e))
        xq = jnp.concatenate(blocks_in, axis=0)
        xxq = doubled(xq)
        ra, rb = inverse_deviation(xq, xxq)
        for h in range(HEADS):
            start = h * 3 * HD
            qa = dot(xxq, wa[:, start:start + HD]) * ra
            qb = dot(xxq, wb[:, start:start + HD]) * rb
            q = jnp.concatenate([qa, qb], axis=0) + bias_of(start)
            q = q * lax.rsqrt(jnp.mean(q * q, axis=1, keepdims=True) + EPS) * gains
            queries_ref[h, begin:begin + 128] = q.astype(BF16)
        return xxq

    def weighted(h, rows, keys):
        weights = jnp.exp2(dot_t(queries_ref[h, rows], keys_ref[h, keys])).astype(BF16)
        return dot(weights, values_ref[h, keys])

    def finish(sums, xxq):
        heads = []
        for h, summed in enumerate(sums):
            heads.append((summed[:, 0:HD] / summed[:, HD:] + bias_of((3 * h + 2) * HD)).astype(BF16))
        attention = jnp.concatenate(heads, axis=1)
        pair = jnp.concatenate([attention[0:64], attention[64:128]], axis=1)
        result = dot(pair, nw[0]) + dot(pair, nw[1]) + dot(xxq, efw[...])
        return result.reshape(4, 16, 128).astype(BF16)

    low, high, every = slice(0, 128), slice(128, 256), slice(0, 2048)

    def first_sweep():
        blocks(xb1, 15, a_s.at[0], a_r.at[0]).wait_recv()
        half_copy(xb1, core, 0, 0).start()
        xxq = make_queries([xb1[core, z * 4 + i] for i in range(4)], 0)
        project(xb1[core, 0:16], 0)
        half_copy(xb1, 1 - core, 0, 0).wait_recv()
        project(xb1[1 - core, 0:16], 512)
        for h in range(HEADS):
            early_sum[0, h] = weighted(h, low, slice(0, 1024))
        blocks(xb1, 16, a_s.at[0], a_r.at[1]).wait_recv()
        half_copy(xb1, core, 1, 1).start()
        xxq2 = make_queries([xb1[core, 16 + z * 4 + i] for i in range(4)], 128)
        project(xb1[core, 16:32], 1024)
        for h in range(HEADS):
            early_sum[1, h] = weighted(h, high, slice(0, 1024))
        half_copy(xb1, 1 - core, 1, 1).wait_recv()
        project(xb1[1 - core, 16:32], 1536)
        first = [early_sum[0, h] + weighted(h, low, slice(1024, 2048)) for h in range(HEADS)]
        second = [early_sum[1, h] + weighted(h, high, slice(1024, 2048)) for h in range(HEADS)]
        part1[0] = finish(first, xxq)
        part1[1] = finish(second, xxq2)

    def second_sweep(unit):
        one = z // 2
        two = 1 - one
        blocks(xb2, 14, b_s.at[0], b_r.at[one]).wait_recv()
        half_copy(xb2, core, one, 2).start()
        xxq = make_queries([xb2[core, z * 8 + i * 2 + unit] for i in range(4)], 0)
        project(xb2[core, pl.ds(one * 16, 16)], 0)
        blocks(xb2, 16, b_s.at[0], b_r.at[two]).wait_recv()
        half_copy(xb2, core, two, 3).start()
        half_copy(xb2, 1 - core, one, 2).wait_recv()
        project(jnp.concatenate([xb2[1 - core, pl.ds(one * 16, 16)], xb2[core, pl.ds(two * 16, 16)]], axis=0), 512)
        half_copy(xb2, 1 - core, two, 3).wait_recv()
        project(xb2[1 - core, pl.ds(two * 16, 16)], 1536)
        part2[unit] = finish([weighted(h, low, every) for h in range(HEADS)], xxq)
        send_out(unit)
        xxq2 = make_queries([xb2[core, z * 8 + i * 2 + 1 - unit] for i in range(4)], 128)
        part2[1 - unit] = finish([weighted(h, high, every) for h in range(HEADS)], xxq2)
        send_out(1 - unit)

    def r_copy(t, i):
        return pltpu.make_async_remote_copy(
            src_ref=part1.at[:, i], dst_ref=box.at[y * 4 + c], send_sem=out_s.at[0], recv_sem=r_r.at[y],
            device_id=device(i, z, t), device_id_type=MESH,
        )

    def o_copy(t, h, i):
        return pltpu.make_async_remote_copy(
            src_ref=part2.at[h, i], dst_ref=final_box.at[y * 4 + c], send_sem=out2_s.at[0], recv_sem=o_r.at[y],
            device_id=device(t, partner if h else z, i), device_id_type=MESH,
        )

    def zero_copy(t, h):
        return pltpu.make_async_remote_copy(
            src_ref=zero_sum.at[h], dst_ref=zero_box, send_sem=zero_s.at[0], recv_sem=o_r.at[0],
            device_id=device(t, partner if h else z, c), device_id_type=MESH,
        )

    def boxes(count, recv):
        part = box.at[pl.ds(0, count)]
        return pltpu.make_async_remote_copy(
            src_ref=part, dst_ref=part, send_sem=out_s.at[0], recv_sem=recv, device_id=sibling, device_id_type=MESH,
        )

    def final_boxes(count, recv):
        part = final_box.at[pl.ds(0, count)]
        return pltpu.make_async_remote_copy(
            src_ref=part, dst_ref=part, send_sem=out2_s.at[0], recv_sem=recv, device_id=sibling, device_id_type=MESH,
        )

    def send_out(h):
        for t in (3, 2, 1):
            @pl.when(t >= y)
            def _():
                for i in range(4):
                    if h:
                        o_copy(t, h, i).start()
                        continue
                    mine = jnp.logical_and(t == c, i == y)

                    @pl.when(mine)
                    def _():
                        final_box[y * 4 + c] = part2[0, i]

                    @pl.when(jnp.logical_not(mine))
                    def _():
                        o_copy(t, h, i).start()

    @pl.when(worker)
    def _():
        first_sweep()
        for t in range(1, WINDOW):
            @pl.when(t > y)
            def _():
                for i in range(4):
                    r_copy(t, i).start()

    @pl.when(jnp.logical_and(early, y > 0))
    def _():
        @pl.when(y != c)
        def _():
            n_copy(0).wait_recv()

        late_noise = pltpu.make_async_remote_copy(
            src_ref=own_noise, dst_ref=red_noise.at[1], send_sem=n_s.at[0], recv_sem=n_r.at[1],
            device_id=sibling, device_id_type=MESH,
        )
        late_noise.wait_recv()
        next_inputs[...] = red_noise[...]
        for t in range(3):
            @pl.when(t < y)
            def _():
                boxes(4, r_r.at[t]).wait_recv()
                total = sum(box[t * 4 + cc].astype(F32) for cc in range(4))
                next_inputs[...] += deltas[t][None] * total
                if t == 0:
                    zero_sum[...] = total
        place = near_z * 8 + c * 2
        xb2[core, pl.ds(place, 2)] = next_inputs[...].astype(BF16)
        part = xb2.at[core, pl.ds(place, 2)]
        for dz in (3, -3, 2, -2, 1, -1, 0):
            @pl.when(jnp.logical_and(z + dz >= 0, z + dz < 4))
            def _():
                for dx in (2, 1, 3, 0):
                    if dx or dz:
                        pltpu.make_async_remote_copy(
                            src_ref=part, dst_ref=part, send_sem=b_s.at[0], recv_sem=b_r.at[z // 2],
                            device_id=device(c + dx, z + dz, y), device_id_type=MESH,
                        ).start()

        @pl.when(y == 1)
        def _():
            for t in range(WINDOW):
                for n in range(2):
                    if t == 1 and n == 0:
                        @pl.when(c != 1)
                        def _():
                            zero_copy(t, n).start()

                        @pl.when(c == 1)
                        def _():
                            zero_box[...] = zero_sum[0]
                    else:
                        zero_copy(t, n).start()

    @pl.when(jnp.logical_and(early, y > 0))
    def _():
        @pl.when(z < 3)
        def _():
            second_sweep(0)

        @pl.when(z == 3)
        def _():
            second_sweep(1)

    @pl.when(worker)
    def _():
        blocks(xb1, 11, a_s.at[0], a_r.at[0]).wait_send()
        for t in range(3):
            @pl.when(y == t)
            def _():
                boxes(4 * (3 - t), r_r.at[0]).wait_send()

    @pl.when(jnp.logical_not(worker))
    def _():
        blocks(xb1, 12, a_s.at[0], a_r.at[0]).wait_send()

    def halves(part):
        pltpu.make_async_remote_copy(
            src_ref=part, dst_ref=part, send_sem=h_s.at[0], recv_sem=h_r.at[0],
            device_id=sibling, device_id_type=MESH,
        ).wait_send()

    both_sweeps = jnp.logical_and(y > 0, y < 3)

    @pl.when(jnp.logical_and(early, both_sweeps))
    def _():
        halves(xb1)

    @pl.when(jnp.logical_and(early, jnp.logical_not(both_sweeps)))
    def _():
        halves(xb1.at[0])

    def rows(count, send):
        part = lat_rows.at[pl.ds(0, count)]
        return pltpu.make_async_remote_copy(
            src_ref=part, dst_ref=part, send_sem=send, recv_sem=o_r.at[0],
            device_id=sibling, device_id_type=MESH,
        )

    @pl.when(y == c)
    def _():
        @pl.when(jnp.logical_and(early, y > 0))
        def _():
            rows(2, n_s.at[0]).wait_send()

        @pl.when(jnp.logical_not(jnp.logical_and(early, y > 0)))
        def _():
            rows(3, n_s.at[0]).wait_send()

    @pl.when(jnp.logical_and(early, y > 0))
    def _():
        part = xb2.at[core, pl.ds(0, 30)]
        pltpu.make_async_remote_copy(
            src_ref=part, dst_ref=part, send_sem=b_s.at[0], recv_sem=b_r.at[0],
            device_id=sibling, device_id_type=MESH,
        ).wait_send()
        for t in range(1, WINDOW):
            for kept in range(2):
                @pl.when(jnp.logical_and(y == t, (c >= t) == jnp.bool_(kept)))
                def _():
                    final_boxes(8 * (4 - t) - kept, o_r.at[0]).wait_send()

        @pl.when(jnp.logical_and(y == 1, c == 1))
        def _():
            rows(7, zero_s.at[0]).wait_send()

        @pl.when(jnp.logical_and(y == 1, c != 1))
        def _():
            rows(8, zero_s.at[0]).wait_send()

    lat_acc[...] = own_noise[...]
    for t in range(WINDOW):
        @pl.when(t <= c)
        def _():
            if t == 0:
                @pl.when(jnp.logical_not(jnp.logical_and(early, jnp.logical_and(y == 1, c == 1))))
                def _():
                    pltpu.make_async_remote_copy(
                        src_ref=zero_box, dst_ref=zero_box, send_sem=zero_s.at[0], recv_sem=o_r.at[0],
                        device_id=sibling, device_id_type=MESH,
                    ).wait_recv()

                total = zero_box[...]
            else:
                @pl.when(jnp.logical_and(early, t == y))
                def _():
                    final_boxes(3, o_r.at[t]).wait_recv()

                @pl.when(jnp.logical_not(jnp.logical_and(early, t == y)))
                def _():
                    final_boxes(4, o_r.at[t]).wait_recv()

                first = t * 4
                total = sum(final_box[first + cc].astype(F32) for cc in range(4))
            lat_acc[...] += deltas[t] * total
            dr_acc[...] = total
    out_ref[0:16, 0:C] = lat_acc[:, 0:C]
    out_ref[16:32, 0:C] = lat_acc[:, C:]
    out_ref[0:16, C:] = dr_acc[:, 0:C]
    out_ref[16:32, C:] = dr_acc[:, C:]


def body(
    noise, step_ids, mod_table, embed_weight, qkv_weight, q_gain, k_gain, out_weight, final_weight
):
    hbm = pl.BlockSpec(memory_space=pltpu.HBM)
    vmem = pl.BlockSpec(memory_space=pltpu.VMEM)
    out = pltpu.VMEM((32, 2 * C), F32)
    dma = pltpu.SemaphoreType.DMA
    both = pl.pallas_call(
        kernel,
        out_shape=out,
        in_specs=[hbm] * 9,
        out_specs=vmem,
        scratch_shapes=[
            pltpu.VMEM((32, C), F32),
            pltpu.SMEM((WINDOW + 1,), jnp.int32),
            pltpu.VMEM((3, TOTAL, D), F32),
            pltpu.VMEM((C, D), BF16),
            pltpu.VMEM((D, COLS), BF16),
            pltpu.VMEM((1, HD), F32),
            pltpu.VMEM((1, HD), F32),
            pltpu.VMEM((HEADS * HD, D), BF16),
            pltpu.VMEM((C, D), F32),
            dma((8,)),
            dma((1,)),
            pltpu.VMEM((16, 128), F32),
            pltpu.VMEM((2, 16, 128), F32),
            pltpu.VMEM((2, 32, 16, 128), BF16),
            pltpu.VMEM((2, 32, 16, 128), BF16),
            pltpu.VMEM((HEADS, 2048, HD), BF16),
            pltpu.VMEM((HEADS, 2048, 2 * HD), BF16),
            pltpu.VMEM((HEADS, 256, HD), BF16),
            pltpu.VMEM((2, HEADS, 128, 2 * HD), F32),
            pltpu.VMEM((2, 4, 16, 128), BF16),
            pltpu.VMEM((2, 4, 16, 128), BF16),
            pltpu.VMEM((12, 2, 16, 128), BF16),
            pltpu.VMEM((24, 16, 128), BF16),
            pltpu.VMEM((2, 16, 128), F32),
            pltpu.VMEM((16, 128), F32),
            pltpu.VMEM((8, 16, 128), F32),
            pltpu.VMEM((144, COLS), F32),
            pltpu.VMEM((256, COLS), BF16),
            pltpu.VMEM((256, COLS), BF16),
            pltpu.VMEM((8, COLS), F32),
            pltpu.VMEM((256, 128), BF16),
            pltpu.VMEM((128, 128), BF16),
            pltpu.VMEM((2, 768, 128), BF16),
            pltpu.VMEM((256, 128), BF16),
            pltpu.VMEM((144, D), BF16),
            pltpu.VMEM((16, 128), F32),
            pltpu.VMEM((16, 128), F32),
            pltpu.VMEM((2, 16, 128), F32),
            pltpu.VMEM((WINDOW, 16, 128), F32),
            dma((1,)), dma((2,)), dma((1,)), dma((2,)), dma((1,)), dma((4,)),
            dma((3,)), dma((1,)), dma((2,)), dma((1,)), dma((1,)), dma((1,)), dma((4,)),
        ],
        compiler_params=pltpu.CompilerParams(
            collective_id=0, has_side_effects=True, vmem_limit_bytes=60 * 1024 * 1024
        ),
        cost_estimate=pl.CostEstimate(flops=4_000_000_000, bytes_accessed=14_000_000, transcendentals=1_700_000),
    )(
        noise, step_ids, mod_table.transpose(1, 0, 2), embed_weight, qkv_weight,
        q_gain.reshape(1, HD), k_gain.reshape(1, HD), out_weight, final_weight.T,
    )
    return both[None, :, 0:C], both[None, :, C:]


def solution(mesh):
    in_specs = (P("seq", None), P(), P(), P(), P(None, "tm"), P(), P(), P("tm", None), P())
    out_specs = (P("tm", "seq", None), P("tm", "seq", None))
    return jax.shard_map(body, mesh=mesh, in_specs=in_specs, out_specs=out_specs, check_vma=False)
```

```python
import math

import jax
import jax.numpy as jnp
from jax import lax
from jax.experimental import pallas as pl
from jax.experimental.pallas import tpu as pltpu
from jax.sharding import PartitionSpec as P

MESH = pl.DeviceIdType.MESH
F32 = jnp.float32
BF16 = jnp.bfloat16
C = 64
D = 3072
HD = 128
HEADS = 3
WINDOW = 4
TOTAL = 28
EPS = 1e-6
PARTS = 6
DEPTH = D // PARTS
COLS = 3 * HD * HEADS
FAR_FIRST = sorted(
    [(a, b) for a in range(8) for b in range(4) if a or b],
    key=lambda ab: -(min(ab[0], 8 - ab[0]) + min(ab[1], 4 - ab[1])),
)
CONTRACT_LAST = (((1,), (1,)), ((), ()))


def dot(left, right):
    return jnp.dot(left, right, preferred_element_type=F32)


def dot_t(left, right):
    return lax.dot_general(left, right, CONTRACT_LAST, preferred_element_type=F32)


def split(value, pieces):
    out = []
    for _ in range(pieces):
        piece = value.astype(BF16)
        out.append(piece)
        value = value - piece.astype(F32)
    return out


def left_half(value):
    return jnp.concatenate([value, jnp.zeros_like(value)], axis=1)


def right_half(value):
    return jnp.concatenate([jnp.zeros_like(value), value], axis=1)


def kernel(
    noise_ref, ids_in, mod_ref, e_ref, w_ref, qgain_ref, kgain_ref, o_ref, f_ref,
    out_ref,
    noise_in, ids_ref, mod_in, e_in, w_in, qg_ref, kg_ref, o_in, f_in, local_sem, w_sem,
    own_noise, red_noise, xb1, xb2, keys_ref, values_ref, queries_ref, early_sum, part1, part2, box, final_box, zero_sum, zero_box,
    lat_rows,
    proj, wa, wb, bias, g12, g3, nw, efw, a_hi, lat_acc, dr_acc, next_inputs, deltas,
    a_s, a_r, n_s, n_r, h_s, h_r, r_r, b_s, b_r, out_s, out2_s, zero_s, o_r,
):
    c = lax.axis_index("tm")
    s = lax.axis_index("seq")
    z = s // 8
    y = (s // 2) % 4
    core = s % 2

    def device(cc, zz, yy):
        return (cc % 4, (zz % 8) * 8 + (yy % 4) * 2 + core)

    sibling = (c, z * 8 + y * 2 + 1 - core)

    noise_copy = pltpu.make_async_copy(noise_ref, noise_in, local_sem.at[0])
    noise_copy.start()

    barrier = pltpu.get_barrier_semaphore()
    early = z < 4
    worker = jnp.logical_and(early, y < 3)
    half = z // 4
    near_z = jnp.where(early, z, (z + 2) % 4)
    partner = 4 + (z + 2) % 4

    def greet(target):
        pl.semaphore_signal(barrier, inc=1, device_id=target, device_id_type=MESH)

    @pl.when(early)
    def _():
        for n in (7, 6, 5, 4):
            for dy in (2, 1, 3, 0):
                greet(device(c, n, y + dy))
        for n in range(4):
            for dy in (2, 1, 3, 0):
                if dy:
                    greet(device(c, n, y + dy))
                else:
                    @pl.when(z != n)
                    def _():
                        greet(device(c, n, y))
        for dx in range(1, 4):
            for dy in range(4):
                greet(device(c + dx, z, y + dy))
        greet(sibling)

    copies = [
        pltpu.make_async_copy(e_ref, e_in, local_sem.at[1]),
        pltpu.make_async_copy(ids_in, ids_ref, local_sem.at[2]),
        pltpu.make_async_copy(mod_ref, mod_in, local_sem.at[3]),
        pltpu.make_async_copy(f_ref, f_in, local_sem.at[4]),
        pltpu.make_async_copy(o_ref, o_in, local_sem.at[5]),
        pltpu.make_async_copy(qgain_ref, qg_ref, local_sem.at[6]),
        pltpu.make_async_copy(kgain_ref, kg_ref, local_sem.at[7]),
    ]
    w_copies = [
        pltpu.make_async_copy(
            w_ref.at[pl.ds(n * DEPTH, DEPTH)], w_in.at[pl.ds(n * DEPTH, DEPTH)], w_sem.at[0]
        )
        for n in range(PARTS)
    ]

    def fetch():
        for copy in copies + w_copies:
            copy.start()

    def small_matrices():
        for copy in copies[:3]:
            copy.wait()
        embed = e_in[...].astype(F32)
        centred = embed - jnp.mean(embed, axis=1, keepdims=True)
        here = pl.ds(ids_ref[y], 1)
        shift = mod_in[0, here]
        scale = mod_in[1, here]
        gate = mod_in[2, here]
        scaled = split(centred * (1.0 + scale), 2)
        a_hi[0:64] = scaled[0]
        a_hi[64:128] = scaled[1]
        shifts = split(shift, 2)
        row = lax.broadcasted_iota(jnp.int32, (16, D), 0)
        a_hi[128:144] = jnp.where(
            row == 0, jnp.broadcast_to(shift, (16, D)),
            jnp.where(row == 1, jnp.broadcast_to(shift - shifts[0].astype(F32), (16, D)), 0.0),
        ).astype(BF16)

        pieces = split(centred, 3)
        stacked = jnp.concatenate(pieces, axis=0)
        gram = dot_t(stacked, stacked)
        gram = gram[0:64] + gram[64:128] + gram[128:192]
        gram = (gram[:, 0:64] + gram[:, 64:128] + gram[:, 128:192]) * (1.0 / D)
        g1, g2, gl = split(gram, 3)
        g12[0:64] = left_half(g1)
        g12[64:128] = right_half(g1)
        g12[128:192] = left_half(g2)
        g12[192:256] = right_half(g2)
        g3[0:64] = left_half(gl)
        g3[64:128] = right_half(gl)

        for copy in copies[3:]:
            copy.wait()
        final = f_in[...]
        final_hl = jnp.concatenate(split(final, 2), axis=0)
        gated_hl = jnp.concatenate(split(final * gate, 2), axis=0)
        head_out = dot_t(o_in[...], gated_hl)
        embed_out = dot_t(e_in[...], final_hl)
        head_out = head_out[:, 0:64] + head_out[:, 64:128]
        own = (c == 0).astype(F32)
        embed_out = (embed_out[:, 0:64] + embed_out[:, 64:128]) * own
        for n, value in enumerate(split(head_out, 2)):
            nw[n, 0:384] = left_half(value)
            nw[n, 384:768] = right_half(value)
        for n, value in enumerate(split(embed_out, 2)):
            efw[n * 128:n * 128 + 64] = left_half(value)
            efw[n * 128 + 64:n * 128 + 128] = right_half(value)
        pltpu.make_async_copy(w_ref, w_in, w_sem.at[0]).wait()
        proj[...] = dot(a_hi[...], w_in[...])
        small = proj[0:64] + proj[64:128]
        bias[...] = proj[128:136]
        small_hi, small_lo = split(small, 2)
        none = jnp.zeros((64, COLS), BF16)
        for n, value in enumerate((small_hi, none, small_lo, none)):
            wa[n * 64:(n + 1) * 64] = value
        for n, value in enumerate((none, small_hi, none, small_lo)):
            wb[n * 64:(n + 1) * 64] = value

    @pl.when(early)
    def _():
        fetch()
        values_ref[:, :, HD:] = jnp.ones((HEADS, 2048, HD), BF16)

    noise_copy.wait()
    packed = jnp.concatenate([noise_in[0:16], noise_in[16:32]], axis=1)
    own_noise[...] = packed
    slot = half * 16 + near_z * 4 + y
    xb1[core, slot] = packed.astype(BF16)

    @pl.when(early)
    def _():
        pl.semaphore_wait(barrier, 28)

    @pl.when(jnp.logical_not(early))
    def _():
        pl.semaphore_wait(barrier, 16)

    def a_copy(zz, yy):
        return pltpu.make_async_remote_copy(
            src_ref=xb1.at[core, slot], dst_ref=xb1.at[core, slot], send_sem=a_s.at[0], recv_sem=a_r.at[half],
            device_id=device(c, zz, yy), device_id_type=MESH,
        )

    def blocks(buffer, count, send, recv):
        part = buffer.at[core, pl.ds(0, count)]
        return pltpu.make_async_remote_copy(
            src_ref=part, dst_ref=part, send_sem=send, recv_sem=recv, device_id=sibling, device_id_type=MESH,
        )

    @pl.when(early)
    def _():
        for zz in range(4):
            for yy in range(3):
                @pl.when(jnp.logical_not(jnp.logical_and(z == zz, y == yy)))
                def _():
                    a_copy(zz, yy).start()

    @pl.when(jnp.logical_not(early))
    def _():
        for dz in (4, 3, 5, 2, 6, 1, 7):
            @pl.when((z + dz) % 8 < 4)
            def _():
                for yy in range(3):
                    a_copy(z + dz, yy).start()

    def n_copy(t):
        return pltpu.make_async_remote_copy(
            src_ref=own_noise, dst_ref=red_noise.at[half], send_sem=n_s.at[0], recv_sem=n_r.at[half],
            device_id=device(c, near_z, t), device_id_type=MESH,
        )

    @pl.when(y == c)
    def _():
        @pl.when(jnp.logical_and(early, y > 0))
        def _():
            red_noise[0] = own_noise[...]

        for t in range(1, WINDOW):
            @pl.when(jnp.logical_or(y != t, z >= 4))
            def _():
                n_copy(t).start()

    @pl.when(early)
    def _():
        small_matrices()

    @pl.when(jnp.logical_not(early))
    def _():
        copies[1].start()
        copies[1].wait()

    def sigma(n):
        left = 1.0 - jnp.full((16, 128), ids_ref[n]).astype(F32) / TOTAL
        return 3.0 * left / (1.0 + 2.0 * left)

    for t in range(WINDOW):
        deltas[t] = sigma(t + 1) - sigma(t)

    def doubled(x):
        return jnp.concatenate([x, x], axis=1)

    def inverse_deviation(x, xx):
        term = (dot(xx, g12[...]) + dot(x, g3[...])) * x.astype(F32)
        lane = lax.broadcasted_iota(jnp.int32, term.shape, 1)
        first = jnp.sum(jnp.where(lane < 64, term, 0.0), axis=1, keepdims=True)
        second = jnp.sum(jnp.where(lane < 64, 0.0, term), axis=1, keepdims=True)
        return lax.rsqrt(jnp.maximum(first, 0.0) + EPS), lax.rsqrt(jnp.maximum(second, 0.0) + EPS)

    def bias_of(start):
        return bias[0:1, start:start + HD] + bias[1:2, start:start + HD]

    def project(x, begin):
        x = x.reshape(x.shape[0] * 16, 128)
        xx = doubled(x)
        va, vb = inverse_deviation(x, xx)
        rows = slice(begin, begin + 2 * x.shape[0])
        for h in range(HEADS):
            start = h * 3 * HD + HD
            kva = dot(xx, wa[:, start:start + 2 * HD]) * va
            kvb = dot(xx, wb[:, start:start + 2 * HD]) * vb
            kv = jnp.concatenate([kva, kvb], axis=0)
            keys = kv[:, 0:HD] + bias_of(start)
            square = jnp.mean(keys * keys, axis=1, keepdims=True)
            keys_ref[h, rows] = (keys * lax.rsqrt(square + EPS)).astype(BF16)
            values_ref[h, rows, 0:HD] = kv[:, HD:].astype(BF16)

    def half_copy(buffer, which, n, index):
        part = buffer.at[which, pl.ds(n * 16, 16)]
        return pltpu.make_async_remote_copy(
            src_ref=part, dst_ref=part, send_sem=h_s.at[0], recv_sem=h_r.at[index],
            device_id=sibling, device_id_type=MESH,
        )

    def make_queries(blocks_in, begin):
        gains = qg_ref[...] * kg_ref[...] * (HD ** -0.5 * math.log2(math.e))
        xq = jnp.concatenate(blocks_in, axis=0)
        xxq = doubled(xq)
        ra, rb = inverse_deviation(xq, xxq)
        for h in range(HEADS):
            start = h * 3 * HD
            qa = dot(xxq, wa[:, start:start + HD]) * ra
            qb = dot(xxq, wb[:, start:start + HD]) * rb
            q = jnp.concatenate([qa, qb], axis=0) + bias_of(start)
            q = q * lax.rsqrt(jnp.mean(q * q, axis=1, keepdims=True) + EPS) * gains
            queries_ref[h, begin:begin + 128] = q.astype(BF16)
        return xxq

    def weighted(h, rows, keys):
        weights = jnp.exp2(dot_t(queries_ref[h, rows], keys_ref[h, keys])).astype(BF16)
        return dot(weights, values_ref[h, keys])

    def finish(sums, xxq):
        heads = []
        for h, summed in enumerate(sums):
            heads.append((summed[:, 0:HD] / summed[:, HD:] + bias_of((3 * h + 2) * HD)).astype(BF16))
        attention = jnp.concatenate(heads, axis=1)
        pair = jnp.concatenate([attention[0:64], attention[64:128]], axis=1)
        result = dot(pair, nw[0]) + dot(pair, nw[1]) + dot(xxq, efw[...])
        return result.reshape(4, 16, 128).astype(BF16)

    low, high, every = slice(0, 128), slice(128, 256), slice(0, 2048)

    def first_sweep():
        blocks(xb1, 15, a_s.at[0], a_r.at[0]).wait_recv()
        half_copy(xb1, core, 0, 0).start()
        xxq = make_queries([xb1[core, z * 4 + i] for i in range(4)], 0)
        project(xb1[core, 0:16], 0)
        half_copy(xb1, 1 - core, 0, 0).wait_recv()
        project(xb1[1 - core, 0:16], 512)
        for h in range(HEADS):
            early_sum[0, h] = weighted(h, low, slice(0, 1024))
        blocks(xb1, 16, a_s.at[0], a_r.at[1]).wait_recv()
        half_copy(xb1, core, 1, 1).start()
        xxq2 = make_queries([xb1[core, 16 + z * 4 + i] for i in range(4)], 128)
        project(xb1[core, 16:32], 1024)
        for h in range(HEADS):
            early_sum[1, h] = weighted(h, high, slice(0, 1024))
        half_copy(xb1, 1 - core, 1, 1).wait_recv()
        project(xb1[1 - core, 16:32], 1536)
        first = [early_sum[0, h] + weighted(h, low, slice(1024, 2048)) for h in range(HEADS)]
        second = [early_sum[1, h] + weighted(h, high, slice(1024, 2048)) for h in range(HEADS)]
        part1[0] = finish(first, xxq)
        part1[1] = finish(second, xxq2)

    def second_sweep(unit):
        one = z // 2
        two = 1 - one
        blocks(xb2, 14, b_s.at[0], b_r.at[one]).wait_recv()
        half_copy(xb2, core, one, 2).start()
        xxq = make_queries([xb2[core, z * 8 + i * 2 + unit] for i in range(4)], 0)
        project(xb2[core, pl.ds(one * 16, 16)], 0)
        blocks(xb2, 16, b_s.at[0], b_r.at[two]).wait_recv()
        half_copy(xb2, core, two, 3).start()
        half_copy(xb2, 1 - core, one, 2).wait_recv()
        project(jnp.concatenate([xb2[1 - core, pl.ds(one * 16, 16)], xb2[core, pl.ds(two * 16, 16)]], axis=0), 512)
        half_copy(xb2, 1 - core, two, 3).wait_recv()
        project(xb2[1 - core, pl.ds(two * 16, 16)], 1536)
        part2[unit] = finish([weighted(h, low, every) for h in range(HEADS)], xxq)
        send_out(unit)
        xxq2 = make_queries([xb2[core, z * 8 + i * 2 + 1 - unit] for i in range(4)], 128)
        part2[1 - unit] = finish([weighted(h, high, every) for h in range(HEADS)], xxq2)
        send_out(1 - unit)

    def r_copy(t, i):
        return pltpu.make_async_remote_copy(
            src_ref=part1.at[:, i], dst_ref=box.at[y * 4 + c], send_sem=out_s.at[0], recv_sem=r_r.at[y],
            device_id=device(i, z, t), device_id_type=MESH,
        )

    def o_copy(t, h, i):
        return pltpu.make_async_remote_copy(
            src_ref=part2.at[h, i], dst_ref=final_box.at[y * 4 + c], send_sem=out2_s.at[0], recv_sem=o_r.at[y],
            device_id=device(t, partner if h else z, i), device_id_type=MESH,
        )

    def zero_copy(t, h):
        return pltpu.make_async_remote_copy(
            src_ref=zero_sum.at[h], dst_ref=zero_box, send_sem=zero_s.at[0], recv_sem=o_r.at[0],
            device_id=device(t, partner if h else z, c), device_id_type=MESH,
        )

    def boxes(count, recv):
        part = box.at[pl.ds(0, count)]
        return pltpu.make_async_remote_copy(
            src_ref=part, dst_ref=part, send_sem=out_s.at[0], recv_sem=recv, device_id=sibling, device_id_type=MESH,
        )

    def final_boxes(count, recv):
        part = final_box.at[pl.ds(0, count)]
        return pltpu.make_async_remote_copy(
            src_ref=part, dst_ref=part, send_sem=out2_s.at[0], recv_sem=recv, device_id=sibling, device_id_type=MESH,
        )

    def send_out(h):
        for t in (3, 2, 1):
            @pl.when(t >= y)
            def _():
                for i in range(4):
                    if h:
                        o_copy(t, h, i).start()
                        continue
                    mine = jnp.logical_and(t == c, i == y)

                    @pl.when(mine)
                    def _():
                        final_box[y * 4 + c] = part2[0, i]

                    @pl.when(jnp.logical_not(mine))
                    def _():
                        o_copy(t, h, i).start()

    @pl.when(worker)
    def _():
        first_sweep()
        for t in range(1, WINDOW):
            @pl.when(t > y)
            def _():
                for i in range(4):
                    r_copy(t, i).start()

    @pl.when(jnp.logical_and(early, y > 0))
    def _():
        @pl.when(y != c)
        def _():
            n_copy(0).wait_recv()

        late_noise = pltpu.make_async_remote_copy(
            src_ref=own_noise, dst_ref=red_noise.at[1], send_sem=n_s.at[0], recv_sem=n_r.at[1],
            device_id=sibling, device_id_type=MESH,
        )
        late_noise.wait_recv()
        next_inputs[...] = red_noise[...]
        for t in range(3):
            @pl.when(t < y)
            def _():
                boxes(4, r_r.at[t]).wait_recv()
                total = sum(box[t * 4 + cc].astype(F32) for cc in range(4))
                next_inputs[...] += deltas[t][None] * total
                if t == 0:
                    zero_sum[...] = total
        place = near_z * 8 + c * 2
        xb2[core, pl.ds(place, 2)] = next_inputs[...].astype(BF16)
        part = xb2.at[core, pl.ds(place, 2)]
        for dz in (3, -3, 2, -2, 1, -1, 0):
            @pl.when(jnp.logical_and(z + dz >= 0, z + dz < 4))
            def _():
                for dx in (2, 1, 3, 0):
                    if dx or dz:
                        pltpu.make_async_remote_copy(
                            src_ref=part, dst_ref=part, send_sem=b_s.at[0], recv_sem=b_r.at[z // 2],
                            device_id=device(c + dx, z + dz, y), device_id_type=MESH,
                        ).start()

        @pl.when(y == 1)
        def _():
            for t in range(WINDOW):
                for n in range(2):
                    if t == 1 and n == 0:
                        @pl.when(c != 1)
                        def _():
                            zero_copy(t, n).start()

                        @pl.when(c == 1)
                        def _():
                            zero_box[...] = zero_sum[0]
                    else:
                        zero_copy(t, n).start()

    @pl.when(jnp.logical_and(early, y > 0))
    def _():
        @pl.when(z < 3)
        def _():
            second_sweep(0)

        @pl.when(z == 3)
        def _():
            second_sweep(1)

    @pl.when(worker)
    def _():
        blocks(xb1, 11, a_s.at[0], a_r.at[0]).wait_send()
        for t in range(3):
            @pl.when(y == t)
            def _():
                boxes(4 * (3 - t), r_r.at[0]).wait_send()

    @pl.when(jnp.logical_not(worker))
    def _():
        blocks(xb1, 12, a_s.at[0], a_r.at[0]).wait_send()

    def halves(part):
        pltpu.make_async_remote_copy(
            src_ref=part, dst_ref=part, send_sem=h_s.at[0], recv_sem=h_r.at[0],
            device_id=sibling, device_id_type=MESH,
        ).wait_send()

    both_sweeps = jnp.logical_and(y > 0, y < 3)

    @pl.when(jnp.logical_and(early, both_sweeps))
    def _():
        halves(xb1)

    @pl.when(jnp.logical_and(early, jnp.logical_not(both_sweeps)))
    def _():
        halves(xb1.at[0])

    def rows(count, send):
        part = lat_rows.at[pl.ds(0, count)]
        return pltpu.make_async_remote_copy(
            src_ref=part, dst_ref=part, send_sem=send, recv_sem=o_r.at[0],
            device_id=sibling, device_id_type=MESH,
        )

    @pl.when(y == c)
    def _():
        @pl.when(jnp.logical_and(early, y > 0))
        def _():
            rows(2, n_s.at[0]).wait_send()

        @pl.when(jnp.logical_not(jnp.logical_and(early, y > 0)))
        def _():
            rows(3, n_s.at[0]).wait_send()

    @pl.when(jnp.logical_and(early, y > 0))
    def _():
        part = xb2.at[core, pl.ds(0, 30)]
        pltpu.make_async_remote_copy(
            src_ref=part, dst_ref=part, send_sem=b_s.at[0], recv_sem=b_r.at[0],
            device_id=sibling, device_id_type=MESH,
        ).wait_send()
        for t in range(1, WINDOW):
            for kept in range(2):
                @pl.when(jnp.logical_and(y == t, (c >= t) == jnp.bool_(kept)))
                def _():
                    final_boxes(8 * (4 - t) - kept, o_r.at[0]).wait_send()

        @pl.when(jnp.logical_and(y == 1, c == 1))
        def _():
            rows(7, zero_s.at[0]).wait_send()

        @pl.when(jnp.logical_and(y == 1, c != 1))
        def _():
            rows(8, zero_s.at[0]).wait_send()

    lat_acc[...] = own_noise[...]
    for t in range(WINDOW):
        @pl.when(t <= c)
        def _():
            if t == 0:
                @pl.when(jnp.logical_not(jnp.logical_and(early, jnp.logical_and(y == 1, c == 1))))
                def _():
                    pltpu.make_async_remote_copy(
                        src_ref=zero_box, dst_ref=zero_box, send_sem=zero_s.at[0], recv_sem=o_r.at[0],
                        device_id=sibling, device_id_type=MESH,
                    ).wait_recv()

                total = zero_box[...]
            else:
                @pl.when(jnp.logical_and(early, t == y))
                def _():
                    final_boxes(3, o_r.at[t]).wait_recv()

                @pl.when(jnp.logical_not(jnp.logical_and(early, t == y)))
                def _():
                    final_boxes(4, o_r.at[t]).wait_recv()

                first = t * 4
                total = sum(final_box[first + cc].astype(F32) for cc in range(4))
            lat_acc[...] += deltas[t] * total
            dr_acc[...] = total
    out_ref[0:16, 0:C] = lat_acc[:, 0:C]
    out_ref[16:32, 0:C] = lat_acc[:, C:]
    out_ref[0:16, C:] = dr_acc[:, 0:C]
    out_ref[16:32, C:] = dr_acc[:, C:]


def body(
    noise, step_ids, mod_table, embed_weight, qkv_weight, q_gain, k_gain, out_weight, final_weight
):
    hbm = pl.BlockSpec(memory_space=pltpu.HBM)
    vmem = pl.BlockSpec(memory_space=pltpu.VMEM)
    out = pltpu.VMEM((32, 2 * C), F32)
    dma = pltpu.SemaphoreType.DMA
    both = pl.pallas_call(
        kernel,
        out_shape=out,
        in_specs=[hbm] * 9,
        out_specs=vmem,
        scratch_shapes=[
            pltpu.VMEM((32, C), F32),
            pltpu.SMEM((WINDOW + 1,), jnp.int32),
            pltpu.VMEM((3, TOTAL, D), F32),
            pltpu.VMEM((C, D), BF16),
            pltpu.VMEM((D, COLS), BF16),
            pltpu.VMEM((1, HD), F32),
            pltpu.VMEM((1, HD), F32),
            pltpu.VMEM((HEADS * HD, D), BF16),
            pltpu.VMEM((C, D), F32),
            dma((8,)),
            dma((1,)),
            pltpu.VMEM((16, 128), F32),
            pltpu.VMEM((2, 16, 128), F32),
            pltpu.VMEM((2, 32, 16, 128), BF16),
            pltpu.VMEM((2, 32, 16, 128), BF16),
            pltpu.VMEM((HEADS, 2048, HD), BF16),
            pltpu.VMEM((HEADS, 2048, 2 * HD), BF16),
            pltpu.VMEM((HEADS, 256, HD), BF16),
            pltpu.VMEM((2, HEADS, 128, 2 * HD), F32),
            pltpu.VMEM((2, 4, 16, 128), BF16),
            pltpu.VMEM((2, 4, 16, 128), BF16),
            pltpu.VMEM((12, 2, 16, 128), BF16),
            pltpu.VMEM((24, 16, 128), BF16),
            pltpu.VMEM((2, 16, 128), F32),
            pltpu.VMEM((16, 128), F32),
            pltpu.VMEM((8, 16, 128), F32),
            pltpu.VMEM((144, COLS), F32),
            pltpu.VMEM((256, COLS), BF16),
            pltpu.VMEM((256, COLS), BF16),
            pltpu.VMEM((8, COLS), F32),
            pltpu.VMEM((256, 128), BF16),
            pltpu.VMEM((128, 128), BF16),
            pltpu.VMEM((2, 768, 128), BF16),
            pltpu.VMEM((256, 128), BF16),
            pltpu.VMEM((144, D), BF16),
            pltpu.VMEM((16, 128), F32),
            pltpu.VMEM((16, 128), F32),
            pltpu.VMEM((2, 16, 128), F32),
            pltpu.VMEM((WINDOW, 16, 128), F32),
            dma((1,)), dma((2,)), dma((1,)), dma((2,)), dma((1,)), dma((4,)),
            dma((3,)), dma((1,)), dma((2,)), dma((1,)), dma((1,)), dma((1,)), dma((4,)),
        ],
        compiler_params=pltpu.CompilerParams(
            collective_id=0, has_side_effects=True, vmem_limit_bytes=60 * 1024 * 1024
        ),
        cost_estimate=pl.CostEstimate(flops=4_000_000_000, bytes_accessed=14_000_000, transcendentals=1_700_000),
    )(
        noise, step_ids, mod_table.transpose(1, 0, 2), embed_weight, qkv_weight,
        q_gain.reshape(1, HD), k_gain.reshape(1, HD), out_weight, final_weight.T,
    )
    return both[None, :, 0:C], both[None, :, C:]


def solution(mesh):
    in_specs = (P("seq", None), P(), P(), P(), P(None, "tm"), P(), P(), P("tm", None), P())
    out_specs = (P("tm", "seq", None), P("tm", "seq", None))
    return jax.shard_map(body, mesh=mesh, in_specs=in_specs, out_specs=out_specs, check_vma=False)
```
